32 devices in a mesh: wide: 8 (over y, x, core), narrow: 4 (over z).
Axes of the slice: x: 2, y: 2, z: 4, core: 2. Of those that a mesh axis runs over, the one named last changes fastest.
Arguments:
- block_input: bfloat16 [12288, 768], P('wide', 'narrow'), may hold values from -4 to 4
- time_embed: float32 [24, 128], P('wide'), may hold values from -3 to 3
- seq_lengths: int32 [8, 3], P('wide'), may hold values from 1 to 768, 1536 in all within a row
- w_qkv: bfloat16 [3, 768, 768], P(None, None, 'narrow'), may hold values from -0.21875 to 0.21875
- w_out: bfloat16 [768, 768], P('narrow'), may hold values from -0.625 to 0.625
- w_up: bfloat16 [768, 3072], P(None, 'narrow'), may hold values from -0.21875 to 0.21875
- b_up: float32 [3072], P('narrow'), may hold values from -1.5 to 1.5
- w_down: bfloat16 [3072, 768], P('narrow'), may hold values from -0.109375 to 0.109375
- b_down: float32 [768], replicated, may hold values from -1.5 to 1.5
- gain_one: float32 [768], replicated, may hold values from 0.5 to 1.5
- gain_two: float32 [768], replicated, may hold values from 0.5 to 1.5
- w_ada: bfloat16 [128, 4608], replicated, may hold values from -0.5 to 0.5
- b_ada: float32 [4608], replicated, may hold values from -0.9 to 0.9
- out_grad: bfloat16 [12288, 768], P('wide', 'narrow'), may hold values from -4 to 4
Outputs:
- block_output: bfloat16 [12288, 768], P('wide', 'narrow')
- input_grad: float32 [12288, 768], P('wide', 'narrow')
- time_grad: float32 [24, 128], P('wide')
- grad_qkv: float32 [3, 768, 768], P(None, None, 'narrow')
- grad_out: float32 [768, 768], P('narrow')
- grad_up: float32 [768, 3072], P(None, 'narrow')
- grad_bias_up: float32 [3072], P('narrow')
- grad_down: float32 [3072, 768], P('narrow')
- grad_bias_down: float32 [768], replicated
- grad_gain_one: float32 [768], replicated
- grad_gain_two: float32 [768], replicated
- grad_ada: float32 [128, 4608], replicated
- grad_bias_ada: float32 [4608], replicated
The draws below stay inside these ranges and needn't reach their ends.
Inputs may be any that keep to these rules, and one draw needn't show every extreme that they name: `seq_lengths`: each row holds the lengths of the 3 sequences of one index of wide, summing to 1536; the largest in each row is exactly 768.
All inputs are finite; a program needn't handle non-finite values.
Results may differ from the reference program's by a relative error of at most 0.023.
The reference program's roundings to bfloat16 on the way count: a program that leaves them out, or rounds other values in their place, can miss the bound.
Values may be sent and summed in bfloat16 or wider, within the bound.
A program may use at most 192 MiB of HBM per device.

```python
import math
import jax
import jax.numpy as jnp
import numpy as np
from jax import lax

D = 768
HEADS = 12
HD = 64
FF = 3072
COND = 128
ROWS = 1536
SLOTS = 3
LONGEST = 768
TOKENS = 12288
SEQS = 24
N_WIDE = 8


def block_scale(rng, extent, shards, least, top_value):
    level = 1.0
    for position, blocks in shards:
        draws = jax.random.uniform(jax.random.fold_in(jax.random.fold_in(rng, 6), position), (blocks,), jnp.float32, least / len(shards), top_value / len(shards))
        level = level * jnp.repeat(jnp.exp(draws), extent[position] // blocks).reshape((-1,) + (1,) * (len(extent) - 1 - position))
    return level


def split_up(number_of, total, bound, slope):
    portions = [(1 << 20) // math.isqrt(standing ** slope) + 1 for standing in range(2, number_of + 1)]
    rest, counts = total - bound - (number_of - 1), [1] * (number_of - 1)
    while rest > 0:
        movable = [i for i in range(number_of - 1) if counts[i] < bound]
        pool, left = sum([portions[i] for i in movable]), rest
        for i in movable:
            more = min(bound - counts[i], max(1, left * portions[i] // pool), rest)
            counts[i] = counts[i] + more
            rest = rest - more
    return np.array([bound] + counts)


def uneven(rng, number_of, total, most, slope):
    if number_of == 2:
        one = jax.random.randint(rng, (), max(1, total - most), min(most, total - 1) + 1)
        return jnp.stack([one, total - one])
    lengths = jnp.asarray(split_up(number_of, total, most, slope), jnp.int32)
    twos = (number_of - 1) // 2
    source_of, taker = lengths[1:1 + 2 * twos:2], lengths[2:2 + 2 * twos:2]
    slack = jnp.minimum(source_of - 1, most - taker)
    shifted = jax.random.randint(jax.random.fold_in(rng, 1), (twos,), 0, 1 << 20) % (slack + 1)
    lengths = lengths.at[1:1 + 2 * twos:2].set(source_of - shifted).at[2:2 + 2 * twos:2].set(taker + shifted)
    return lengths[jax.random.permutation(jax.random.fold_in(rng, 2), number_of)]


def gaussian(rng, extent, width, bound, cuts=(), kind=jnp.bfloat16):
    entries = width * jax.random.normal(rng, extent, jnp.float32)
    if cuts:
        entries = entries * block_scale(rng, extent, cuts, -0.22, 0.18)
    return jnp.clip(entries, -bound, bound).astype(kind)


def setup_inputs(seed: int = 0) -> dict:
    keys = jax.random.split(jax.random.key(seed), 15)
    return {
        "block_input": gaussian(keys[0], (TOKENS, D), 1.0, 4.0, ((0, 8), (1, 4))),
        "time_embed": gaussian(keys[1], (SEQS, COND), 1.0, 3.0, ((0, 8),), jnp.float32),
        "seq_lengths": jax.vmap(lambda own: uneven(own, SLOTS, ROWS, LONGEST, 2))(jax.random.split(keys[2], N_WIDE)).reshape((N_WIDE, SLOTS)).astype(jnp.int32),
        "w_qkv": gaussian(keys[3], (3, D, D), D ** -0.5, 0.21875, ((2, 4),)),
        "w_out": gaussian(keys[4], (D, D), (max(D // 8, 1)) ** -0.5, 0.625, ((0, 4),)),
        "w_up": gaussian(keys[5], (D, FF), D ** -0.5, 0.21875, ((1, 4),)),
        "b_up": gaussian(keys[6], (FF,), 0.5, 1.5, ((0, 4),), jnp.float32),
        "w_down": gaussian(keys[7], (FF, D), FF ** -0.5, 0.109375, ((0, 4),)),
        "b_down": gaussian(keys[8], (D,), 0.5, 1.5, (), jnp.float32),
        "gain_one": jnp.clip(1.0 + 0.1 * jax.random.normal(keys[9], (D,), jnp.float32), 0.5, 1.5),
        "gain_two": jnp.clip(1.0 + 0.1 * jax.random.normal(keys[10], (D,), jnp.float32), 0.5, 1.5),
        "w_ada": gaussian(keys[11], (COND, 6 * D), COND ** -0.5, 0.5),
        "b_ada": gaussian(keys[12], (6 * D,), 0.3, 0.9, (), jnp.float32),
        "out_grad": gaussian(keys[13], (TOKENS, D), 1.0, 4.0, ((0, 8), (1, 4))),
    }


@jax.custom_vjp
def low(v):
    return lax.optimization_barrier(v.astype(jnp.bfloat16)).astype(jnp.float32)

@jax.custom_vjp
def low_back(v):
    return v

def low_keep(v):
    return (low(v), None)

def low_pass(kept, grad):
    return (grad,)

def back_keep(v):
    return (v, None)

def back_low(kept, grad):
    return (low(grad),)
low.defvjp(low_keep, low_pass)
low_back.defvjp(back_keep, back_low)
epsilon = 1e-05
highest = lax.Precision.HIGHEST

def norm_rows(inputs, norm_gain):
    row_mean = lax.optimization_barrier(jnp.mean(inputs, axis=-1, keepdims=True))
    centered = inputs - row_mean
    variance = lax.optimization_barrier(jnp.mean(centered * centered, axis=-1, keepdims=True))
    return centered * lax.rsqrt(variance + epsilon) * norm_gain

def rotary(inputs, positions):
    halfway = inputs.shape[-1] // 2
    inverse = 10000.0 ** (-2.0 * jnp.arange(halfway, dtype=jnp.float32) / inputs.shape[-1])
    angles = positions.astype(jnp.float32)[:, None] * inverse[None, :]
    cosine = jnp.cos(angles)[:, None, :]
    sine_table = jnp.sin(angles)[:, None, :]
    first_half = inputs[..., :halfway]
    second_half = inputs[..., halfway:]
    return jnp.concatenate([first_half * cosine - second_half * sine_table, second_half * cosine + first_half * sine_table], axis=-1)

def segments(seq_lengths, row_count):
    seq_ends = jnp.cumsum(seq_lengths).astype(jnp.int32)
    seq_starts = seq_ends - seq_lengths.astype(jnp.int32)
    row_index = jnp.arange(row_count, dtype=jnp.int32)
    segment = lax.optimization_barrier(jnp.sum((row_index[:, None] >= seq_ends[None, :]).astype(jnp.int32), axis=1)).astype(jnp.int32)
    onehot = segment[:, None] == jnp.arange(seq_lengths.shape[0], dtype=jnp.int32)[None, :]
    positions = row_index - lax.optimization_barrier(jnp.sum(jnp.where(onehot, seq_starts[None, :], 0), axis=1)).astype(jnp.int32)
    return (segment, onehot.astype(jnp.float32), positions)

def group_forward(params, group_input, group_time, seq_lengths):
    w_qkv, w_out, w_up, b_up, w_down, b_down, gain_one, gain_two, w_ada, b_ada = params
    segment, slot_table, positions = segments(seq_lengths, ROWS)
    context = jax.nn.silu(group_time)
    modulation = low_back(jnp.dot(low(context), w_ada, precision=highest)) + b_ada
    pieces = [jnp.dot(slot_table, modulation[:, piece_index * D:(piece_index + 1) * D], precision=highest) for piece_index in range(6)]
    shift_one, scale_one, gate_one, shift_two, scale_two, gate_two = pieces
    input_one = low(norm_rows(group_input, gain_one) * (1.0 + scale_one) + shift_one)
    query = low_back(jnp.dot(input_one, w_qkv[0], precision=highest)).reshape(ROWS, HEADS, HD)
    key_raw = low_back(jnp.dot(input_one, w_qkv[1], precision=highest)).reshape(ROWS, HEADS, HD)
    values = low(low_back(jnp.dot(input_one, w_qkv[2], precision=highest))).reshape(ROWS, HEADS, HD)
    queries = low(rotary(query, positions) * 0.125)
    key_rows = low(rotary(key_raw, positions))
    scores = low_back(jnp.einsum('qhd,khd->hqk', queries, key_rows, precision=highest))
    same_seq = segment[:, None] == segment[None, :]
    masked = jnp.where(same_seq[None], scores, -1e+30)
    row_max = lax.optimization_barrier(jnp.max(masked, axis=-1, keepdims=True))
    expos = jnp.exp(masked - row_max)
    probabilities = expos / lax.optimization_barrier(jnp.sum(expos, axis=-1, keepdims=True))
    mixed = low(low_back(jnp.einsum('hqk,khd->qhd', low(probabilities), values, precision=highest))).reshape(ROWS, D)
    attention = low_back(jnp.dot(mixed, w_out, precision=highest))
    hidden_one = group_input + gate_one * attention
    input_two = low(norm_rows(hidden_one, gain_two) * (1.0 + scale_two) + shift_two)
    pre_act = low_back(jnp.dot(input_two, w_up, precision=highest)) + b_up
    activated = low(jax.nn.gelu(pre_act, approximate=True))
    feed_out = low_back(jnp.dot(activated, w_down, precision=highest)) + b_down
    return hidden_one + gate_two * feed_out

def reference(block_input, time_embed, seq_lengths, w_qkv, w_out, w_up, b_up, w_down, b_down, gain_one, gain_two, w_ada, b_ada, out_grad):
    weights = tuple((weight_arg.astype(jnp.float32) for weight_arg in (w_qkv, w_out, w_up, b_up, w_down, b_down, gain_one, gain_two, w_ada, b_ada)))
    grouped_lengths = seq_lengths.astype(jnp.int32)

    def forward(inputs, times, params):
        group_step = jax.checkpoint(group_forward)

        def advance(totals, pieces):
            return (totals, group_step(params, pieces[0], pieces[1], pieces[2]))
        stacked = (inputs.reshape(N_WIDE, ROWS, D), times.reshape(N_WIDE, SLOTS, COND), grouped_lengths)
        unused, outputs = lax.scan(advance, jnp.zeros((), jnp.float32), stacked)
        return outputs.reshape(N_WIDE * ROWS, D)
    result, pullback = jax.vjp(forward, block_input.astype(jnp.float32), time_embed.astype(jnp.float32), weights)
    input_grad, time_grad, param_grads = pullback(out_grad.astype(jnp.float32))
    grad_qkv, grad_out, grad_up, grad_bias_up, grad_down, grad_bias_down, grad_gain_one, grad_gain_two, grad_ada, grad_bias_ada = param_grads
    return (result.astype(jnp.bfloat16), input_grad, time_grad, grad_qkv, grad_out, grad_up, grad_bias_up, grad_down, grad_bias_down, grad_gain_one, grad_gain_two, grad_ada, grad_bias_ada)
```

```python
import functools

import jax
import jax.numpy as jnp
from jax import lax
from jax.experimental import pallas as pl
from jax.experimental.pallas import tpu as pltpu
from jax.sharding import PartitionSpec as P

HD = 64
epsilon = 1e-05
highest = lax.Precision.HIGHEST
MESH = pl.DeviceIdType.MESH
CHUNKS = 3
F32 = jnp.float32
BF16 = jnp.bfloat16


def place():
    w = lax.axis_index("wide")
    z = lax.axis_index("narrow")
    return w, z, w % 2, (w // 2) % 2, (w // 4) % 2


def flip(w, bit, step):
    return w + step * (1 - 2 * bit)


def remote(src, dst, send, recv, device):
    return pltpu.make_async_remote_copy(
        src_ref=src, dst_ref=dst, send_sem=send, recv_sem=recv, device_id=device, device_id_type=MESH
    )


def greet(devices):
    barrier = pltpu.get_barrier_semaphore()
    for device in devices:
        pl.semaphore_signal(barrier, inc=1, device_id=device, device_id_type=MESH)
    pl.semaphore_wait(barrier, len(devices))


def column_peers(w, z, c):
    return [
        (w if same else flip(w, c, 1), (z + dz) % 4) for same in (1, 0) for dz in range(4) if not (same and dz == 0)
    ]


def gather_kernel(
    x, dy, w_attn, w_up, w_down, b_up, info,
    x_out, dy_out, w_out, b_out, info_out,
    x_send, x_recv, pair_send, pair_recv, local_sem, home_send, block_recv, ring_send, plane_send, b_send, b_recv,
):
    w, z, c, bx, by = place()
    part = x.shape[0] // 4
    rows = w_attn.shape[0] // 4
    across_x, across_y = flip(w, bx, 2), flip(w, by, 4)
    other = flip(w, c, 1)
    greet(column_peers(w, z, c) + [(across_x, z), (across_y, z)])
    block_a = pl.ds(pl.multiple_of(bx * rows, rows), rows)
    block_b = pl.ds(pl.multiple_of((2 + by) * rows, rows), rows)

    info_copy = remote(info, info_out, pair_send.at[2], pair_recv.at[2], (other, z))
    info_copy.start()

    def exchange(k, source, target):
        for j in range(4):
            device = (w - c + j % 2, 2 * c + j // 2)
            mine = (c == j % 2) & (device[1] == z)
            block = source.at[pl.ds(j * part, part)]

            @pl.when(mine)
            def _():
                pltpu.make_async_copy(block, target.at[j % 2, z], x_recv.at[k, z]).start()

            @pl.when(jnp.logical_not(mine))
            def _():
                remote(block, target.at[j % 2, z], x_send.at[k, j], x_recv.at[k, z], device).start()

    def exchange_sent(k, source, target):
        for j in range(4):
            mine = (c == j % 2) & (2 * c + j // 2 == z)

            @pl.when(jnp.logical_not(mine))
            def _():
                block = source.at[pl.ds(j * part, part)]
                remote(block, target.at[j % 2, z], x_send.at[k, j], x_recv.at[k, z], (w, z)).wait_send()

    def exchange_done(k, source, target):
        for slot in range(4):
            pltpu.make_async_copy(source.at[pl.ds(0, part)], target.at[c, slot], x_recv.at[k, slot]).wait()
        pair = remote(target.at[c], target.at[c], pair_send.at[k], pair_recv.at[k], (other, z))
        pair.start()

    def pair_done(k, target):
        remote(target.at[c], target.at[1 - c], pair_send.at[k], pair_recv.at[k], (other, z)).wait_recv()

    exchange(0, x, x_out)
    for dz in range(1, 4):
        remote(b_up, b_out.at[z], b_send.at[dz], b_recv.at[dz], (w, (z + dz) % 4)).start()
    pltpu.make_async_copy(b_up, b_out.at[z], b_send.at[0]).start()

    chunks = (w_attn, w_up, w_down)
    far = [(z - 2 * c - q) % 4 for q in range(2)]
    for t in range(CHUNKS):
        for q in range(2):

            @pl.when(far[q] == 0)
            def _():
                pltpu.make_async_copy(chunks[t], w_out.at[t, q], local_sem.at[t]).start()
                for n, block in enumerate((block_a, block_b)):
                    for m, step in enumerate((1, 3)):
                        remote(
                            chunks[t].at[block], w_out.at[t, q, block], home_send.at[t, 2 * n + m],
                            block_recv.at[t, q, n], (w, (z + step) % 4),
                        ).start()

    exchange(1, dy, dy_out)
    exchange_done(0, x, x_out)

    def landed(t, q, n, block):
        pltpu.make_async_copy(w_out.at[t, q, block], w_out.at[t, q, block], block_recv.at[t, q, n]).wait()

    def ring(t, q, n, block, step):
        return remote(
            w_out.at[t, q, block], w_out.at[t, q, block], ring_send.at[t, q], block_recv.at[t, q, n],
            (w, (z + step) % 4),
        )

    def plane(t, q, n, block):
        return remote(
            w_out.at[t, q, block], w_out.at[t, q, block], plane_send.at[t, q, n], block_recv.at[t, q, 2 + n],
            ((across_x, across_y)[n], z),
        )

    for t in range(CHUNKS):
        for q in range(2):

            @pl.when(far[q] == 1)
            def _():
                landed(t, q, 0, block_a)
                ring(t, q, 0, block_a, 1).start()
                plane(t, q, 0, block_a).start()
                landed(t, q, 1, block_b)
                plane(t, q, 1, block_b).start()

            @pl.when(far[q] == 3)
            def _():
                landed(t, q, 1, block_b)
                ring(t, q, 1, block_b, 3).start()
                plane(t, q, 1, block_b).start()
                landed(t, q, 0, block_a)
                plane(t, q, 0, block_a).start()

        for q in range(2):

            @pl.when(far[q] == 2)
            def _():
                landed(t, q, 0, block_a)
                plane(t, q, 0, block_a).start()
                landed(t, q, 1, block_b)
                plane(t, q, 1, block_b).start()

    exchange_done(1, dy, dy_out)
    other_a = pl.ds(pl.multiple_of((1 - bx) * rows, rows), rows)
    other_b = pl.ds(pl.multiple_of((3 - by) * rows, rows), rows)
    for t in range(CHUNKS):
        for q in range(2):

            @pl.when(far[q] == 0)
            def _():
                pltpu.make_async_copy(chunks[t], w_out.at[t, q], local_sem.at[t]).wait()
                for n, block in enumerate((block_a, block_b)):
                    for m, step in enumerate((1, 3)):
                        remote(
                            chunks[t].at[block], w_out.at[t, q, block], home_send.at[t, 2 * n + m],
                            block_recv.at[t, q, n], (w, (z + step) % 4),
                        ).wait_send()

            @pl.when(far[q] == 1)
            def _():
                ring(t, q, 0, block_a, 1).wait_send()

            @pl.when(far[q] == 3)
            def _():
                ring(t, q, 1, block_b, 3).wait_send()

            @pl.when(far[q] != 0)
            def _():
                plane(t, q, 0, block_a).wait_send()
                plane(t, q, 1, block_b).wait_send()
                landed(t, q, 2, other_a)
                landed(t, q, 3, other_b)

    pair_done(0, x_out)
    pair_done(1, dy_out)
    for k, (source, target) in enumerate(((x, x_out), (dy, dy_out))):
        exchange_sent(k, source, target)
        remote(target.at[c], target.at[c], pair_send.at[k], pair_recv.at[k], (other, z)).wait_send()
    info_copy.wait()
    for dz in range(1, 4):
        remote(b_up, b_out.at[(z - dz) % 4], b_send.at[dz], b_recv.at[dz], (w, (z + dz) % 4)).wait()
    pltpu.make_async_copy(b_up, b_out.at[z], b_send.at[0]).wait()


def gather_all(x, dy, w_attn, w_up, w_down, b_up, info):
    rows, width = x.shape
    size = w_attn.shape[0]
    any_space = pl.BlockSpec(memory_space=pl.ANY)
    dma = pltpu.SemaphoreType.DMA
    return pl.pallas_call(
        gather_kernel,
        out_shape=(
            jax.ShapeDtypeStruct((2, 4, rows // 4, width), BF16),
            jax.ShapeDtypeStruct((2, 4, rows // 4, width), BF16),
            jax.ShapeDtypeStruct((CHUNKS, 2, size, size), BF16),
            jax.ShapeDtypeStruct((4,) + b_up.shape, F32),
            jax.ShapeDtypeStruct(info.shape, F32),
        ),
        in_specs=[any_space] * 7,
        out_specs=(any_space,) * 5,
        scratch_shapes=[
            dma((2, 4)), dma((2, 4)), dma((3,)), dma((3,)), dma((CHUNKS,)), dma((CHUNKS, 4)), dma((CHUNKS, 2, 4)),
            dma((CHUNKS, 2)), dma((CHUNKS, 2, 2)), dma((4,)), dma((4,)),
        ],
        compiler_params=pltpu.CompilerParams(collective_id=0, has_side_effects=True),
        name="gather_all",
    )(x, dy, w_attn, w_up, w_down, b_up, info)


def reduce_kernel(
    n_wide, sub, grads, out_rows, in_rows,
    g_out, out_o, in_o,
    near, ring_in, own, mids, finals,
    o_send, o_recv, near_send, near_recv, ring_send, ring_recv, mid_send, mid_recv, push_send, push_recv, pair_send,
    pair_recv,
):
    w, z, c, bx, by = place()
    members = n_wide // 4
    plane_count = n_wide // 2
    rows = grads.shape[2] // 4
    plane_at = w // 2
    across = (flip(w, bx, 2), flip(w, by, 4))
    other = flip(w, c, 1)
    plane_peers = [((w + step) % n_wide, z) for step in range(1, n_wide)]
    z_peers = [(w, (z + dz) % 4) for dz in range(1, 4)]
    greet(plane_peers + z_peers + [(other, (z + dz) % 4) for dz in range(1, 4)])
    blocks = (
        pl.ds(pl.multiple_of(bx * rows, rows), rows),
        pl.ds(pl.multiple_of((2 + by) * rows, rows), rows),
    )
    others = (
        pl.ds(pl.multiple_of((1 - bx) * rows, rows), rows),
        pl.ds(pl.multiple_of((3 - by) * rows, rows), rows),
    )
    far = [(z - 2 * c - q) % 4 for q in range(2)]
    home = c == z // 2
    member = (w // 4, bx + 2 * (w // 8))
    part = out_rows.shape[1] // 2

    def near_copy(t, q, n):
        return remote(
            grads.at[t, q, others[n]], near.at[t, q, n], near_send.at[t, q, n], near_recv.at[t, q, n], (across[n], z)
        )

    order = (2, 1, 0)
    for t in order:
        for q in range(2):
            for n in range(2):
                near_copy(t, q, n).start()

    def spread(k, source, target, start):
        for dest in range(4):
            device = (w - c + z // 2, dest)
            mine = (c == z // 2) & (z == dest)
            slot = 2 * (z % 2) + c
            block = source.at[dest, pl.ds(pl.multiple_of(c * part, part), part)]

            @pl.when(mine)
            def _():
                if start:
                    pltpu.make_async_copy(block, target.at[slot], o_recv.at[k, slot]).start()

            @pl.when(jnp.logical_not(mine))
            def _():
                copy = remote(block, target.at[slot], o_send.at[k, dest], o_recv.at[k, slot], device)
                copy.start() if start else copy.wait_send()

    spread(0, out_rows, out_o, True)
    spread(1, in_rows, in_o, True)

    def tiles(step):
        def run(i, carry):
            step(pl.ds(pl.multiple_of(i * 16, 16), 16))
            return carry

        lax.fori_loop(0, rows // 16, run, 0)

    def ring_copy(t, q, n, slot, step):
        return remote(
            own.at[t, q, n, pl.ds(0, rows)], ring_in.at[t, q, slot], ring_send.at[t, q, n], ring_recv.at[t, q, slot],
            (w, (z + step) % 4),
        )

    def near_add(t, q, n):
        near_copy(t, q, n).wait_recv()
        base = (bx, 2 + by)[n] * rows

        def step(s):
            place_rows = pl.ds(pl.multiple_of(base + s.start, 16), 16)
            own[t, q, n, s] = (grads[t, q, place_rows].astype(F32) + near[t, q, n, s].astype(F32)).astype(BF16)

        tiles(step)

    def arrived(t, q, slot):
        pltpu.make_async_copy(ring_in.at[t, q, slot], ring_in.at[t, q, slot], ring_recv.at[t, q, slot]).wait()

    def add_in(t, q, n, slots):
        def step(s):
            total = own[t, q, n, s].astype(F32)
            for slot in slots:
                total = total + ring_in[t, q, slot, s].astype(F32)
            own[t, q, n, s] = total.astype(BF16)

        tiles(step)

    def mid_copy(t, n, m):
        device_w = ((2 * m + bx) * 2 + c, (4 * (m // 2) + 2 * by + m % 2) * 2 + c)[n]
        return remote(
            own.at[t, z % 2, n, pl.ds(m * sub, sub)], mids.at[t, n, member[n]], mid_send.at[t, n, m],
            mid_recv.at[t, n, member[n]], (device_w, z),
        )

    def push_copy(t, n, step):
        target = g_out.at[t, (bx, 2 + by)[n], pl.ds(pl.multiple_of(member[n] * sub, sub), sub)]
        return remote(
            finals.at[t, n], target, push_send.at[t, n, step], push_recv.at[t, n, step],
            ((w + 2 * step) % n_wide, z),
        )

    def local_copy(t, n):
        target = g_out.at[t, (bx, 2 + by)[n], pl.ds(pl.multiple_of(member[n] * sub, sub), sub)]
        return pltpu.make_async_copy(finals.at[t, n], target, push_recv.at[t, n, 0])

    def pair_copy(t):
        return remote(g_out.at[t], g_out.at[t], pair_send.at[t], pair_recv.at[t], (other, z))

    for t in order:
        for q in range(2):
            for n in range(2):
                near_add(t, q, n)

            @pl.when(far[q] == 2)
            def _():
                ring_copy(t, q, 0, 0, 3).start()
                ring_copy(t, q, 1, 0, 1).start()

            @pl.when(far[q] == 1)
            def _():
                ring_copy(t, q, 1, 1, 3).start()

            @pl.when(far[q] == 3)
            def _():
                ring_copy(t, q, 0, 2, 1).start()

    for t in order:
        for q in range(2):

            @pl.when(far[q] == 1)
            def _():
                arrived(t, q, 0)
                add_in(t, q, 0, (0,))
                ring_copy(t, q, 0, 0, 3).start()

            @pl.when(far[q] == 3)
            def _():
                arrived(t, q, 0)
                add_in(t, q, 1, (0,))
                ring_copy(t, q, 1, 3, 1).start()

    for t in order:
        for q in range(2):

            @pl.when(far[q] == 0)
            def _():
                for slot in range(4):
                    arrived(t, q, slot)
                add_in(t, q, 0, (0, 2))
                add_in(t, q, 1, (1, 3))
                for n in range(2):
                    for m in range(members):

                        @pl.when(member[n] != m)
                        def _():
                            mid_copy(t, n, m).start()

    for t in order:

        @pl.when(home)
        def _():
            for n in range(2):
                for m in range(members):

                    @pl.when(member[n] != m)
                    def _():
                        pltpu.make_async_copy(mids.at[t, n, m], mids.at[t, n, m], mid_recv.at[t, n, m]).wait()

                first = member[n] * sub

                def run(i, carry):
                    s = pl.ds(pl.multiple_of(i * 16, 16), 16)
                    total = own[t, z % 2, n, pl.ds(pl.multiple_of(first + i * 16, 16), 16)].astype(F32)
                    for m in range(members):
                        term = mids[t, n, m, s].astype(F32)
                        total = total + jnp.where(member[n] == m, 0.0, term)
                    finals[t, n, s] = total.astype(BF16)
                    return carry

                lax.fori_loop(0, sub // 16, run, 0)
                local_copy(t, n).start()
                for step in range(1, plane_count):
                    push_copy(t, n, step).start()

    for t in order:

        @pl.when(home)
        def _():
            for n in range(2):
                local_copy(t, n).wait()
                for step in range(1, plane_count):
                    push_copy(t, n, step).wait_recv()
            pair_copy(t).start()

    for t in order:

        @pl.when(home)
        def _():
            pair_copy(t).wait_send()
            for n in range(2):
                for step in range(1, plane_count):
                    push_copy(t, n, step).wait_send()
                for m in range(members):

                    @pl.when(member[n] != m)
                    def _():
                        mid_copy(t, n, m).wait_send()

        @pl.when(jnp.logical_not(home))
        def _():
            pair_copy(t).wait_recv()

        for q in range(2):
            for n in range(2):
                near_copy(t, q, n).wait_send()

            @pl.when(far[q] != 0)
            def _():
                for n in range(2):
                    ring_copy(t, q, n, 0, 1).wait_send()

    for k, (source, target) in enumerate(((out_rows, out_o), (in_rows, in_o))):
        for slot in range(4):
            pltpu.make_async_copy(source.at[0, pl.ds(0, part)], target.at[slot], o_recv.at[k, slot]).wait()
        spread(k, source, target, False)


def reduce_all(n_wide, grads, out_rows, in_rows):
    size = grads.shape[-1]
    rows = size // 4
    members = n_wide // 4
    sub = -(-rows // members // 16) * 16
    part, width = out_rows.shape[1] // 2, out_rows.shape[2]
    any_space = pl.BlockSpec(memory_space=pl.ANY)
    dma = pltpu.SemaphoreType.DMA
    spread = max(rows, members * sub)
    g_out, out_o, in_o = pl.pallas_call(
        functools.partial(reduce_kernel, n_wide, sub),
        out_shape=(
            jax.ShapeDtypeStruct((CHUNKS, 4, members * sub, size), BF16),
            jax.ShapeDtypeStruct((4, part, width), BF16),
            jax.ShapeDtypeStruct((4, part, width), BF16),
        ),
        in_specs=[pl.BlockSpec(memory_space=pltpu.VMEM), any_space, any_space],
        out_specs=(any_space,) * 3,
        scratch_shapes=[
            pltpu.VMEM((CHUNKS, 2, 2, rows, size), BF16),
            pltpu.VMEM((CHUNKS, 2, 4, rows, size), BF16),
            pltpu.VMEM((CHUNKS, 2, 2, spread, size), BF16),
            pltpu.VMEM((CHUNKS, 2, members, sub, size), BF16),
            pltpu.VMEM((CHUNKS, 2, sub, size), BF16),
            dma((2, 4)), dma((2, 4)), dma((CHUNKS, 2, 2)), dma((CHUNKS, 2, 2)), dma((CHUNKS, 2, 2)), dma((CHUNKS, 2, 4)),
            dma((CHUNKS, 2, members)), dma((CHUNKS, 2, members)), dma((CHUNKS, 2, n_wide // 2)),
            dma((CHUNKS, 2, n_wide // 2)), dma((CHUNKS,)), dma((CHUNKS,)),
        ],
        compiler_params=pltpu.CompilerParams(
            collective_id=1, has_side_effects=True, vmem_limit_bytes=56 * 1024 * 1024
        ),
        name="reduce_all",
    )(grads, out_rows, in_rows)
    return g_out[:, :, :rows].reshape(CHUNKS, size, size), out_o, in_o


def norm_stats(inputs):
    row_mean = jnp.mean(inputs, axis=-1, keepdims=True)
    centered = inputs - row_mean
    variance = jnp.mean(centered * centered, axis=-1, keepdims=True)
    scaled = lax.rsqrt(variance + epsilon)
    return (centered * scaled, scaled)


def norm_back(grad_normed, normed, scaled):
    first_term = jnp.mean(grad_normed, axis=-1, keepdims=True)
    second_term = jnp.mean(grad_normed * normed, axis=-1, keepdims=True)
    return scaled * (grad_normed - first_term - normed * second_term)


def gelu_tanh(inputs):
    return jax.nn.gelu(inputs, approximate=True)


def rotary_tables(positions, head_size):
    halfway = head_size // 2
    inverse = 10000.0 ** (-2.0 * jnp.arange(halfway, dtype=F32) / head_size)
    angles = positions.astype(F32)[:, None] * inverse[None, :]
    return (jnp.cos(angles)[:, None, :], jnp.sin(angles)[:, None, :])


def rotate(inputs, cosine, sine_table):
    halfway = inputs.shape[-1] // 2
    first_half = inputs[..., :halfway]
    second_half = inputs[..., halfway:]
    return jnp.concatenate(
        [
            first_half * cosine - second_half * sine_table,
            second_half * cosine + first_half * sine_table,
        ],
        axis=-1,
    )


def body(
    n_wide,
    block_input,
    time_embed,
    seq_lengths,
    w_qkv,
    w_out,
    w_up,
    b_up,
    w_down,
    b_down,
    gain_one,
    gain_two,
    w_ada,
    b_ada,
    out_grad,
):
    w, z, core, _, _ = place()
    row_count, own_width = block_input.shape
    half = row_count // 2
    size = w_qkv.shape[1]
    slots, cond = time_embed.shape
    quarter = w_qkv.shape[2]
    heads = 2 * quarter // HD
    pair_index = [(i, i ^ 1) for i in range(n_wide)]

    def long_start(lengths):
        slot = jnp.argmax(lengths)
        return slot, jnp.sum(jnp.where(jnp.arange(slots) < slot, lengths, 0))

    lengths = seq_lengths[0]
    own_slot, own_start = long_start(lengths)

    def turn(rows, shift):
        return lax.dynamic_slice_in_dim(jnp.concatenate([rows, rows], axis=0), shift, row_count, 0)

    info = jnp.concatenate(
        [time_embed, jnp.pad(lengths.astype(F32)[None], ((0, 0), (0, cond - slots))), jnp.zeros((8 - slots - 1, cond))]
    )
    w_attn = jnp.concatenate([jnp.swapaxes(w_qkv, 1, 2).reshape(-1, size), w_out], axis=0)
    b_rows = jnp.pad(b_up.reshape(-1, 128), ((0, 2), (0, 0)))
    x_parts, dy_parts, weights, b_parts, info_other = gather_all(
        turn(block_input, own_start), turn(out_grad, own_start), w_attn, w_up, w_down, b_rows, info
    )

    def whole(parts):
        return jnp.swapaxes(parts, 1, 2).reshape(half, size)

    inputs = whole(x_parts).astype(F32)
    grad_two = whole(dy_parts).astype(F32)
    info = jnp.where(core == z // 2, info, info_other)
    times = info[:slots]
    lengths = info[slots, :slots].astype(jnp.int32)
    long_slot, _ = long_start(lengths)
    second_half = z % 2 == 1
    slot_a = jnp.where(second_half, (long_slot + 1) % slots, long_slot)
    slot_b = jnp.where(second_half, (long_slot + 2) % slots, long_slot)
    bound = jnp.where(second_half, lengths[slot_a], half)
    row_ids = jnp.arange(half, dtype=jnp.int32)
    first = row_ids < bound
    positions = jnp.where(first, row_ids, row_ids - bound)
    cosine, sine_table = rotary_tables(positions, HD)
    context = jax.nn.silu(times)
    context_low = context.astype(BF16)
    modulation = jnp.dot(context_low, w_ada, preferred_element_type=F32) + b_ada
    mod_a, mod_b = modulation[slot_a], modulation[slot_b]
    pieces = [
        jnp.where(first[:, None], mod_a[None, i * size : (i + 1) * size], mod_b[None, i * size : (i + 1) * size])
        for i in range(6)
    ]
    shift_one, scale_one, gate_one, shift_two, scale_two, gate_two = pieces
    w_qkv_t = weights[0, :, : 3 * quarter].reshape(2, 3, quarter, size)
    w_out_own = weights[0, :, 3 * quarter :].reshape(2 * quarter, size)
    w_up_own, w_down_own = weights[1], weights[2].reshape(-1, size)
    b_own = lax.dynamic_slice_in_dim(b_parts, 2 * core, 2, 0)[:, :6].reshape(-1)

    normed_one, scaled_one = norm_stats(inputs)
    input_one = (normed_one * gain_one * (1.0 + scale_one) + shift_one).astype(BF16)
    projected = jnp.einsum("rd,qted->trqe", input_one, w_qkv_t, preferred_element_type=F32)
    projected = projected.reshape(3, half, heads, HD)
    queries = (rotate(projected[0], cosine, sine_table) * 0.125).astype(BF16)
    key_rows = rotate(projected[1], cosine, sine_table).astype(BF16)
    values = projected[2].astype(BF16)
    same_seq = first[:, None] == first[None, :]
    scores = jnp.einsum("qhd,khd->hqk", queries, key_rows, preferred_element_type=F32)
    masked = jnp.where(same_seq[None], scores, -1e30)
    row_max = jnp.max(masked, axis=-1, keepdims=True)
    expos = jnp.exp(masked - row_max)
    row_total = jnp.sum(expos, axis=-1, keepdims=True)
    probabilities = expos / row_total
    low_probs = probabilities.astype(BF16)
    mixed = jnp.einsum("hqk,khd->qhd", low_probs, values, preferred_element_type=F32)
    mixed = mixed.astype(BF16).reshape(half, heads * HD)

    def both_cores(partial):
        partial = partial.astype(BF16)
        return partial.astype(F32) + lax.ppermute(partial, "wide", pair_index).astype(F32)

    attention = both_cores(jnp.dot(mixed, w_out_own, preferred_element_type=F32))
    hidden_one = inputs + gate_one * attention
    normed_two, scaled_two = norm_stats(hidden_one)
    input_two = (normed_two * gain_two * (1.0 + scale_two) + shift_two).astype(BF16)
    pre_act = jnp.einsum("rd,qdf->rqf", input_two, w_up_own, preferred_element_type=F32).reshape(half, -1) + b_own
    activated, gelu_back = jax.vjp(gelu_tanh, pre_act)
    act_low = activated.astype(BF16)
    feed_out = both_cores(jnp.dot(act_low, w_down_own, preferred_element_type=F32)) + b_down
    hidden_two = hidden_one + gate_two * feed_out
    block_output = hidden_two.astype(BF16)

    grad_gate_two = grad_two * feed_out
    grad_feed = grad_two * gate_two
    grad_bias_down = jnp.sum(grad_feed, axis=0)
    feed_low = grad_feed.astype(BF16)
    grad_down = jnp.einsum("rf,rd->fd", act_low, feed_low, preferred_element_type=F32)
    grad_act = jnp.einsum("rd,fd->rf", feed_low, w_down_own, preferred_element_type=F32)
    grad_pre = gelu_back(grad_act)[0]
    grad_bias_up = jnp.sum(grad_pre, axis=0)
    pre_low = grad_pre.astype(BF16).reshape(half, 2, -1)
    grad_up = jnp.einsum("rd,rqf->qdf", input_two, pre_low, preferred_element_type=F32)
    grad_in_two = both_cores(jnp.einsum("rqf,qdf->rd", pre_low, w_up_own, preferred_element_type=F32))
    grad_one = grad_two + norm_back(grad_in_two * (1.0 + scale_two) * gain_two, normed_two, scaled_two)
    grad_scale_two = grad_in_two * normed_two * gain_two
    grad_gain_two = jnp.sum(grad_in_two * normed_two * (1.0 + scale_two), axis=0)
    grad_gate_one = grad_one * attention
    attn_low = (grad_one * gate_one).astype(BF16)
    grad_out = jnp.einsum("rc,rd->cd", mixed, attn_low, preferred_element_type=F32)
    grad_mixed = jnp.einsum("rd,cd->rc", attn_low, w_out_own, preferred_element_type=F32)
    grad_mixed = grad_mixed.astype(BF16).reshape(half, heads, HD)
    grad_values = jnp.einsum("hqk,qhd->khd", low_probs, grad_mixed, preferred_element_type=F32)
    grad_weights = jnp.einsum("qhd,khd->hqk", grad_mixed, values, preferred_element_type=F32)
    row_dot = jnp.sum(probabilities * grad_weights, axis=-1, keepdims=True)
    grad_scores = (probabilities * (grad_weights - row_dot)).astype(BF16)
    grad_query = jnp.einsum("hqk,khd->qhd", grad_scores, key_rows, preferred_element_type=F32)
    grad_key = jnp.einsum("hqk,qhd->khd", grad_scores, queries, preferred_element_type=F32)
    grad_query = rotate(grad_query * 0.125, cosine, -sine_table)
    grad_key = rotate(grad_key, cosine, -sine_table)
    grad_proj = jnp.stack([grad_query, grad_key, grad_values]).astype(BF16).reshape(3, half, 2, quarter)
    grad_qkv = jnp.einsum("trqe,rd->qted", grad_proj, input_one, preferred_element_type=F32)
    grad_in_one = both_cores(jnp.einsum("trqe,qted->rd", grad_proj, w_qkv_t, preferred_element_type=F32))
    input_grad = grad_one + norm_back(grad_in_one * (1.0 + scale_one) * gain_one, normed_one, scaled_one)
    grad_scale_one = grad_in_one * normed_one * gain_one
    grad_gain_one = jnp.sum(grad_in_one * normed_one * (1.0 + scale_one), axis=0)
    row_grads = [grad_in_one, grad_scale_one, grad_gate_one, grad_in_two, grad_scale_two, grad_gate_two]
    slot_table = jnp.stack([first, jnp.logical_not(first)], axis=1).astype(F32)
    grad_mod = jnp.concatenate(
        [jnp.einsum("rs,rd->sd", slot_table, piece_grad, precision=highest) for piece_grad in row_grads], axis=1
    )

    shared = jnp.concatenate([grad_mod.reshape(-1), grad_bias_down, grad_gain_one, grad_gain_two])
    share = shared.shape[0] // 2
    message = jnp.concatenate([lax.dynamic_slice_in_dim(shared, core * share, share, 0), grad_bias_up]).astype(BF16)
    gathered = lax.all_gather(message, ("wide", "narrow"))
    gathered = gathered.reshape(n_wide // 2, 2, 4, -1)

    grads = jnp.stack(
        [
            jnp.concatenate([grad_qkv.reshape(2, 3 * quarter, size), grad_out.reshape(2, quarter, size)], axis=1),
            grad_up,
            grad_down.reshape(2, size, size),
        ]
    ).astype(BF16)

    def split(rows):
        return jnp.swapaxes(rows.astype(BF16).reshape(half, 4, own_width), 0, 1)

    g_own, out_parts, in_parts = reduce_all(n_wide, grads, split(block_output), split(input_grad))

    def unturn(parts):
        return turn(parts.reshape(row_count, own_width), (row_count - own_start) % row_count)

    final_output = unturn(out_parts)
    final_input_grad = unturn(in_parts).astype(F32)

    all_shared = jnp.swapaxes(gathered[..., :share], 1, 2).reshape(n_wide // 2, 4, 2 * share)
    all_mod = all_shared[..., : 12 * size].reshape(n_wide // 2, 4, 2, 6 * size)
    sums = jnp.sum(all_shared[..., 12 * size :].astype(F32), axis=(0, 1)).reshape(3, size)
    grad_bias_down, grad_gain_one, grad_gain_two = sums[0], sums[1], sums[2]
    up_parts = lax.dynamic_index_in_dim(gathered[..., share:], z // 2, 1, False)
    up_sum = jnp.sum(up_parts.astype(F32), axis=(0, 1)).reshape(2, size)
    grad_bias_up = lax.dynamic_index_in_dim(up_sum, z % 2, 0, False)

    all_mod = all_mod.reshape(n_wide, 2, 2, 6 * size)
    all_info = lax.all_gather(
        jnp.concatenate([time_embed, jnp.pad(seq_lengths.astype(F32), ((0, 0), (0, cond - slots)))]), "wide"
    )
    all_lengths = all_info[:, slots, :slots].astype(jnp.int32)
    long_slots = jnp.argmax(all_lengths, axis=1)
    all_context = jax.nn.silu(all_info[:, :slots]).astype(BF16)
    row_slots = jnp.stack(
        [long_slots, long_slots, (long_slots + 1) % slots, (long_slots + 2) % slots], axis=1
    )
    rows_context = jnp.take_along_axis(all_context, row_slots[:, :, None], axis=1)
    all_rows = all_mod.reshape(n_wide * 4, 6 * size)
    grad_bias_ada = jnp.sum(all_rows.astype(F32), axis=0)
    grad_ada = jnp.einsum("sc,sm->cm", rows_context.reshape(-1, cond), all_rows, preferred_element_type=F32)
    own_rows = lax.dynamic_index_in_dim(all_mod.reshape(n_wide, 4, 6 * size), w, 0, False)
    own_row_slots = jnp.stack([own_slot, own_slot, (own_slot + 1) % slots, (own_slot + 2) % slots])
    placed = (own_row_slots[None, :] == jnp.arange(slots)[:, None]).astype(BF16)
    mod_low = jnp.dot(placed, own_rows, preferred_element_type=F32).astype(BF16)
    grad_context = jnp.einsum("sm,cm->sc", mod_low, w_ada, preferred_element_type=F32)
    _, silu_back = jax.vjp(jax.nn.silu, time_embed)
    time_grad = silu_back(grad_context)[0]
    g_attn = g_own[0].astype(F32)
    grad_qkv = jnp.swapaxes(g_attn[: 3 * quarter].reshape(3, quarter, size), 1, 2)
    return (
        final_output,
        final_input_grad,
        time_grad,
        grad_qkv,
        g_attn[3 * quarter :],
        g_own[1].astype(F32),
        grad_bias_up,
        g_own[2].astype(F32),
        grad_bias_down,
        grad_gain_one,
        grad_gain_two,
        grad_ada,
        grad_bias_ada,
    )


def solution(mesh):
    return jax.shard_map(
        functools.partial(body, mesh.shape["wide"]),
        mesh=mesh,
        in_specs=(
            P("wide", "narrow"),
            P("wide", None),
            P("wide", None),
            P(None, None, "narrow"),
            P("narrow", None),
            P(None, "narrow"),
            P("narrow"),
            P("narrow", None),
            P(),
            P(),
            P(),
            P(),
            P(),
            P("wide", "narrow"),
        ),
        out_specs=(
            P("wide", "narrow"),
            P("wide", "narrow"),
            P("wide", None),
            P(None, None, "narrow"),
            P("narrow", None),
            P(None, "narrow"),
            P("narrow"),
            P("narrow", None),
            P(),
            P(),
            P(),
            P(),
            P(),
        ),
        check_vma=False,
    )
```

```python
import functools
from types import SimpleNamespace

import jax
import jax.numpy as jnp
from jax import lax
from jax.experimental import pallas as pl
from jax.experimental.pallas import tpu as pltpu
from jax.sharding import PartitionSpec as P

HD = 64
LOG2_E = 1.4426950408889634
epsilon = 1e-05
MESH = pl.DeviceIdType.MESH
CHUNKS = 3
F32 = jnp.float32
BF16 = jnp.bfloat16


def flip(w, bit, step):
    return w + step * (1 - 2 * bit)


def remote(src, dst, send, recv, device):
    return pltpu.make_async_remote_copy(
        src_ref=src, dst_ref=dst, send_sem=send, recv_sem=recv, device_id=device, device_id_type=MESH
    )


def landed(ref, sem):
    pltpu.make_async_copy(ref, ref, sem).wait()


def dot(a, b, dims):
    return lax.dot_general(a, b, (dims, ((), ())), preferred_element_type=F32)


def nn(a, b):
    return dot(a, b, ((1,), (0,)))


def nt(a, b):
    return dot(a, b, ((1,), (1,)))


def tn(a, b):
    return dot(a, b, ((0,), (0,)))


TILE = 256


def tiles(count, step, size=TILE):
    def run(i, carry):
        step(pl.ds(pl.multiple_of(i * size, size), size), i * size)
        return carry

    lax.fori_loop(0, count // size, run, 0)


def norm_stats(inputs):
    row_mean = jnp.mean(inputs, axis=-1, keepdims=True)
    centered = inputs - row_mean
    variance = jnp.mean(centered * centered, axis=-1, keepdims=True)
    scaled = lax.rsqrt(variance + epsilon)
    return (centered * scaled, scaled)


def norm_back(grad_normed, normed, scaled):
    first_term = jnp.mean(grad_normed, axis=-1, keepdims=True)
    second_term = jnp.mean(grad_normed * normed, axis=-1, keepdims=True)
    return scaled * (grad_normed - first_term - normed * second_term)


GAIN_ONE, SHIFT_ONE, GATE_ONE, GAIN_TWO, SHIFT_TWO, GATE_TWO, RISE_ONE, RISE_TWO = range(8)
SUM_G1, SUM_G1N, SUM_GATE_ONE, SUM_G2, SUM_G2N, SUM_GATE_TWO, SUM_DY = range(7)


def chosen(mods, first, piece):
    return jnp.where(first, mods[piece : piece + 1, :], mods[8 + piece : 9 + piece, :])


def first_rows(bound, start, count):
    return (lax.broadcasted_iota(jnp.int32, (count, 1), 0) + start).astype(F32) < bound


def add_sums(sums, piece, first, values):
    total = jnp.sum(values, axis=0, keepdims=True)
    head = jnp.sum(jnp.where(first, values, 0.0), axis=0, keepdims=True)
    sums[piece : piece + 1, :] += head
    sums[8 + piece : 9 + piece, :] += total - head


def swapped(pair):
    lane = lax.broadcasted_iota(jnp.int32, pair.shape, 1)
    return jnp.where(lane % HD < HD // 2, pltpu.roll(pair, 128 - HD // 2, 1), pltpu.roll(pair, HD // 2, 1))


def lanes(g):
    return pl.ds(g * 128, 128)


def head_only(pair, hh):
    lane = lax.broadcasted_iota(jnp.int32, pair.shape, 1)
    return jnp.where((lane < HD) == (hh == 0), pair, jnp.zeros_like(pair))


def project(bound, start, rows, x, mods, cosine, sine, w_attn, in_one, q, k, v):
    s = pl.ds(pl.multiple_of(start, 64), rows)
    first = first_rows(bound, start, rows)
    normed, _ = norm_stats(x[s, :].astype(F32))
    low = (normed * chosen(mods, first, GAIN_ONE) + chosen(mods, first, SHIFT_ONE)).astype(BF16)
    in_one[s, :] = low
    cos_rows, sin_rows = cosine[s, :], sine[s, :]
    for t, target in enumerate((q, k)):
        raw = nt(low, w_attn[t])
        for g in range(raw.shape[1] // 128):
            pair = raw[:, g * 128 : (g + 1) * 128]
            turned = pair * cos_rows + swapped(pair) * sin_rows
            target[s, lanes(g)] = (turned * (0.125 * LOG2_E if t == 0 else 1.0)).astype(BF16)
    v[s, :] = nt(low, w_attn[2]).astype(BF16)


def attend(bound, g, q, k, v, probs, scales, mixed):
    rows = q.shape[0]

    def step(s, start):
        first = first_rows(bound, start, TILE)
        column = lax.broadcasted_iota(jnp.int32, (1, rows), 1).astype(F32) < bound
        bias = jnp.where(first == column, 0.0, -1e30)
        halves = []
        for hh in range(2):
            scores = nt(head_only(q[s, lanes(g)], hh), k[:, lanes(g)]) + bias
            expos = jnp.exp2(scores - jnp.max(scores, axis=-1, keepdims=True))
            low = expos.astype(BF16)
            probs[2 * g + hh, s, :] = low
            scale = 1.0 / jnp.sum(expos, axis=-1, keepdims=True)
            kept = scales[s, :]
            scales[s, :] = jnp.where(lax.broadcasted_iota(jnp.int32, kept.shape, 1) == 2 * g + hh, scale, kept)
            halves.append(nn(low, v[:, lanes(g)]) * scale)
        lane = lax.broadcasted_iota(jnp.int32, halves[0].shape, 1)
        mixed[s, lanes(g)] = jnp.where(lane < HD, halves[0], halves[1]).astype(BF16)

    tiles(rows, step)


def mix_out(mixed, w_attn, part, share):
    def step(s, start):
        part[0, s, :] = nn(mixed[s, :], w_attn[3]).astype(BF16)
        share(s, start)

    tiles(mixed.shape[0], step)


def both(part, s):
    return part[0, s, :].astype(F32) + part[1, s, :].astype(F32)


def hidden_rows(first, s, x, mods, attn_part):
    return x[s, :].astype(F32) + chosen(mods, first, GATE_ONE) * both(attn_part, s)


def feed_up(bound, x, mods, attn_part, w_up, b_up, in_two, act, slope, arrived):
    def step(s, start):
        arrived(s, start)
        first = first_rows(bound, start, TILE)
        normed, _ = norm_stats(hidden_rows(first, s, x, mods, attn_part))
        low = (normed * chosen(mods, first, GAIN_TWO) + chosen(mods, first, SHIFT_TWO)).astype(BF16)
        in_two[s, :] = low
        for n in range(2):
            pre = nn(low, w_up[n]) + b_up[n]
            square = pre * pre
            bent = jnp.tanh(0.7978845608028654 * pre * (1.0 + 0.044715 * square))
            rise = 0.5 * (1.0 + bent)
            act[n, s, :] = (pre * rise).astype(BF16)
            inner = 0.7978845608028654 + 0.10703222443 * square
            slope[n, s, :] = (rise + 0.5 * pre * (1.0 - bent * bent) * inner).astype(BF16)

    tiles(x.shape[0], step)


def feed_grads(bound, dy, mods, feed_low, sums):
    def step(s, start):
        first = first_rows(bound, start, TILE)
        grads = dy[s, :].astype(F32)
        add_sums(sums, SUM_DY, first, grads)
        feed_low[s, :] = (grads * chosen(mods, first, GATE_TWO)).astype(BF16)

    tiles(dy.shape[0], step)


def feed_down(act, w_down, part, share):
    def step(s, start):
        part[0, s, :] = (nn(act[0, s, :], w_down[0]) + nn(act[1, s, :], w_down[1])).astype(BF16)
        share(s, start)

    tiles(act.shape[1], step)


def feed_out(bound, x, dy, mods, attn_part, feed_part, b_down, out, sums, arrived):
    def step(s, start):
        arrived(s, start)
        first = first_rows(bound, start, TILE)
        rows = both(feed_part, s) + b_down
        out[s, :] = (hidden_rows(first, s, x, mods, attn_part) + chosen(mods, first, GATE_TWO) * rows).astype(BF16)
        add_sums(sums, SUM_GATE_TWO, first, dy[s, :].astype(F32) * rows)

    tiles(dy.shape[0], step)


def feed_back(feed_low, slope, w_up, w_down, bias_up, part, share):
    def step(s, start):
        low = feed_low[s, :]
        total = None
        for n in range(2):
            grad_pre = nt(low, w_down[n]) * slope[n, s, :].astype(F32)
            bias_up[n : n + 1, :] += jnp.sum(grad_pre, axis=0, keepdims=True)
            pre = grad_pre.astype(BF16)
            slope[n, s, :] = pre
            term = nt(pre, w_up[n])
            total = term if total is None else total + term
        part[0, s, :] = total.astype(BF16)
        share(s, start)

    tiles(feed_low.shape[0], step)


def weight_grad(left, right, target):
    def step(s, start):
        target[s, :] = tn(left[:, s], right[...]).astype(BF16)

    size = TILE if left.shape[1] % TILE == 0 else 128
    tiles(left.shape[1], step, size)


def norm_two_back(bound, x, dy, mods, back_part, attn_part, w_attn, grad_one, attn_low, grad_mixed, sums, arrived):
    def step(s, start):
        arrived(s, start)
        first = first_rows(bound, start, TILE)
        grads = both(back_part, s)
        normed, scaled = norm_stats(hidden_rows(first, s, x, mods, attn_part))
        add_sums(sums, SUM_G2, first, grads)
        add_sums(sums, SUM_G2N, first, grads * normed)
        rows = dy[s, :].astype(F32) + norm_back(grads * chosen(mods, first, GAIN_TWO), normed, scaled)
        grad_one[s, :] = rows
        add_sums(sums, SUM_GATE_ONE, first, rows * both(attn_part, s))
        low = (rows * chosen(mods, first, GATE_ONE)).astype(BF16)
        attn_low[s, :] = low
        grad_mixed[s, :] = nt(low, w_attn[3]).astype(BF16)

    tiles(dy.shape[0], step)


def attend_back(g, q, k, v, probs, scales, mixed, grad_mixed, cosine, sine, total_k, total_v, grad_q, grad_k, grad_v):
    rows = q.shape[0]

    def turned_back(pair, s):
        return pair * cosine[s, :] - swapped(pair) * sine[s, :]

    total_k[...] = jnp.zeros_like(total_k)
    total_v[...] = jnp.zeros_like(total_v)

    def step(s, start):
        upstream = grad_mixed[s, lanes(g)]
        product = upstream.astype(F32) * mixed[s, lanes(g)].astype(F32)
        halves = []
        for hh in range(2):
            kept = scales[s, :]
            here = lax.broadcasted_iota(jnp.int32, kept.shape, 1) == 2 * g + hh
            scale = jnp.sum(jnp.where(here, kept, 0.0), axis=-1, keepdims=True)
            row_dot = jnp.sum(head_only(product, hh), axis=-1, keepdims=True) * scale
            up_head = (head_only(upstream, hh).astype(F32) * scale).astype(BF16)
            low = probs[2 * g + hh, s, :]
            grad_weights = nt(up_head, v[:, lanes(g)])
            grad_scores = (low.astype(F32) * (grad_weights - row_dot)).astype(BF16)
            halves.append(nn(grad_scores, k[:, lanes(g)]))
            total_v[...] += tn(low, up_head)
            total_k[...] += tn(grad_scores, head_only(q[s, lanes(g)], hh))
        lane = lax.broadcasted_iota(jnp.int32, halves[0].shape, 1)
        pair = jnp.where(lane < HD, halves[0], halves[1]) * 0.125
        grad_q[s, lanes(g)] = turned_back(pair, s).astype(BF16)

    tiles(rows, step)

    def finish(s, start):
        grad_k[s, lanes(g)] = turned_back(total_k[s, :] * (1.0 / LOG2_E), s).astype(BF16)
        grad_v[s, lanes(g)] = total_v[s, :].astype(BF16)

    tiles(rows, finish)


def project_back(grad_q, grad_k, grad_v, w_attn, part, share):
    def step(s, start):
        total = nn(grad_q[s, :], w_attn[0]) + nn(grad_k[s, :], w_attn[1]) + nn(grad_v[s, :], w_attn[2])
        part[0, s, :] = total.astype(BF16)
        share(s, start)

    tiles(grad_q.shape[0], step)


def norm_one_back(bound, x, mods, back_part, grad_one, in_grad, sums, arrived):
    def step(s, start):
        arrived(s, start)
        first = first_rows(bound, start, TILE)
        grads = both(back_part, s)
        normed, scaled = norm_stats(x[s, :].astype(F32))
        add_sums(sums, SUM_G1, first, grads)
        add_sums(sums, SUM_G1N, first, grads * normed)
        rows = grad_one[s, :] + norm_back(grads * chosen(mods, first, GAIN_ONE), normed, scaled)
        in_grad[s, :] = rows.astype(BF16)

    tiles(x.shape[0], step)


ROW_B_UP, ROW_B_DOWN, ROW_GAIN_ONE, ROW_GAIN_TWO, ROW_B_ADA = 0, 1, 2, 3, 8
MSG_MOD, MSG_B_DOWN, MSG_GAIN_ONE, MSG_GAIN_TWO, MSG_B_UP, MSG_CONTEXT = 0, 6, 7, 8, 9, 11
MSG_ROWS = 16


def scratch_plan(n_wide, rows, width, size, cond):
    half, heads = rows // 2, 2 * width // HD
    block = size // 4
    buffers = {
        "raw": ((2, width, rows), BF16),
        "tail": ((half // 2, 128), F32),
        "small": ((16, size), F32),
        "b_all": ((4, 8, size), F32),
        "b_own": ((8, size), F32),
        "info": ((2, 8, 128), F32),
        "context": ((8, 128), F32),
        "mods": ((16, size), F32),
        "sums": ((16, size), F32),
        "bias_up": ((8, size), F32),
        "message": ((MSG_ROWS, size), BF16),
        "rest": ((2, 4, half // 4, 128), BF16),
        "result_rest": ((2, 4, half // 4, 128), BF16),
        "x_low": ((half, size), BF16),
        "dy_low": ((half, size), BF16),
        "cosine": ((half, 128), F32),
        "sine": ((half, 128), F32),
        "w_attn": ((4, 2 * block, size), BF16),
        "w_ff": ((2, 2, size, size), BF16),
        "in_one": ((half, size), BF16),
        "q": ((half, 2 * width), BF16),
        "k": ((half, 2 * width), BF16),
        "v": ((half, 2 * width), BF16),
        "probs": ((heads, half, half), BF16),
        "scales": ((half, 128), F32),
        "mixed": ((half, 2 * width), BF16),
        "attn_part": ((2, half, size), BF16),
        "feed_part": ((2, half, size), BF16),
        "back_part": ((2, half, size), BF16),
        "in_two": ((half, size), BF16),
        "act": ((2, half, size), BF16),
        "slope": ((2, half, size), BF16),
        "out_low": ((half, size), BF16),
        "feed_low": ((half, size), BF16),
        "grad_one": ((half, size), F32),
        "grad_mixed": ((half, 2 * width), BF16),
        "total_k": ((half, 128), F32),
        "total_v": ((half, 128), F32),
        "grad_q": ((half, 2 * width), BF16),
        "grad_k": ((half, 2 * width), BF16),
        "grad_v": ((half, 2 * width), BF16),
        "g_attn": ((4, 2 * block, size), BF16),
        "g_ff": ((2, 2, size, size), BF16),
        "near_half": ((CHUNKS, 2, 2, block // 2, size), BF16),
        "near_full": ((CHUNKS, 2, 2, block, size), BF16),
        "from_z": ((CHUNKS, 3, block, size), BF16),
    }
    planes = n_wide // 2
    groups = n_wide // 8
    semaphores = {
        "load": (26,),
        "msg_load": (n_wide, 4),
        "end_small": (17,),
        "pair": (4,),
        "pair_in": (4,),
        "b_send": (4,),
        "b_in": (4,),
        "x_send": (2, 4, 2),
        "x_in": (2, 4, 2),
        "home": (CHUNKS, 4),
        "home_send": (CHUNKS, 2),
        "edge_send": (CHUNKS, 2),
        "z_in": (CHUNKS, 2),
        "w_send": (CHUNKS, 2, 4),
        "w_in": (CHUNKS, 2, 4),
        "part_send": (4, 4),
        "part_in": (4, 4),
        "out_send": (2, 4, 2),
        "out_in": (2, 4, 2),
        "g_send": (CHUNKS, 2, 5),
        "g_in": (CHUNKS, 2, 4),
        "gz_in": (CHUNKS, 3),
        "group_send": (CHUNKS, groups),
        "group_in": (CHUNKS, groups),
        "group_load": (CHUNKS,),
        "end_send": (CHUNKS, 8),
        "end_in": (CHUNKS, 9),
        "m_send": (5,),
        "m_in": (5,),
        "mp_send": (planes,),
        "mp_in": (planes,),
    }
    return buffers, semaphores


def layer_kernel(n_wide, rows, width, size, cond, slots, *refs):
    buffers, semaphores = scratch_plan(n_wide, rows, width, size, cond)
    names = (
        ["lengths", "x", "dy", "w_qkv", "w_out", "w_up", "w_down", "b_up", "b_down", "gain_one", "gain_two", "w_ada"]
        + ["b_ada", "times", "out_t", "in_t", "out_o", "in_o", "out_r", "in_r", "g_out", "messages", "groups"]
        + ["ada_out", "b_ada_out", "b_down_out", "gain_one_out", "gain_two_out", "b_up_out", "time_out"]
        + list(buffers)
    )
    r = SimpleNamespace(**dict(zip(names, refs)))
    sem = SimpleNamespace(**dict(zip(semaphores, refs[len(names) :])))
    half = rows // 2
    part = half // 2
    block = size // 4
    planes, groups = n_wide // 2, n_wide // 8

    w = lax.axis_index("wide")
    z = lax.axis_index("narrow")
    c, bx, by, plane_at = w % 2, (w // 2) % 2, (w // 4) % 2, w // 2
    pair = (flip(w, c, 1), z)
    next_x, next_y = (flip(w, bx, 2), z), (flip(w, by, 4), z)
    mine = bx + 2 * by
    block_x, block_y, block_d = mine + 1 - 2 * bx, mine + 2 - 4 * by, 3 - mine
    far = [(z - 2 * c - q) % 4 for q in range(2)]
    home = c == z // 2
    odd = z % 2 == 1

    peers = [(w if same else pair[0], (z + dz) % 4) for same in (1, 0) for dz in range(4) if not (same and dz == 0)]
    peers += [((w + 2 * step) % n_wide, z) for step in range(1, planes)]
    barrier = pltpu.get_barrier_semaphore()
    for device in peers:
        pl.semaphore_signal(barrier, inc=1, device_id=device, device_id_type=MESH)

    w_ada = r.probs.at[2]
    loads = [pltpu.make_async_copy(r.x, r.raw.at[0], sem.load.at[0])]
    loads.append(pltpu.make_async_copy(r.dy, r.raw.at[1], sem.load.at[1]))
    for i, ref in enumerate((r.b_up, r.b_down, r.gain_one, r.gain_two)):
        loads.append(pltpu.make_async_copy(ref, r.small.at[i], sem.load.at[2 + i]))
    for i in range(6):
        piece = pl.ds(i * size, size)
        loads.append(pltpu.make_async_copy(r.b_ada.at[piece], r.small.at[ROW_B_ADA + i], sem.load.at[20 + i]))
    for i in range(6):
        loads.append(
            pltpu.make_async_copy(
                r.w_ada.at[:, pl.ds(i * size, size)], w_ada.at[pl.ds(i * cond, cond)], sem.load.at[7 + i]
            )
        )
    for load in loads:
        load.start()
    r.info[0] = jnp.zeros((8, 128), F32)
    time_load = pltpu.make_async_copy(r.times, r.info.at[0, pl.ds(0, slots)], sem.load.at[13])
    time_load.start()

    def w_block(t, q, index, start=0, count=block):
        if t == 0:
            return r.w_attn.at[index, pl.ds(q * block + start, count)]
        return r.w_ff.at[t - 1, q, pl.ds(pl.multiple_of(index * block + start, 32), count)]

    def home_copies(t, q):
        if t == 0:
            copies = [pltpu.make_async_copy(r.w_qkv.at[i], w_block(0, q, i), sem.home.at[0, i]) for i in range(3)]
            return copies + [pltpu.make_async_copy(r.w_out, w_block(0, q, 3), sem.home.at[0, 3])]
        return [pltpu.make_async_copy((r.w_up, r.w_down)[t - 1], r.w_ff.at[t - 1, q], sem.home.at[t, 0])]

    edge, middle = 3 - 3 * c, 2 - c

    def home_sends(t, q, source):
        return [
            remote(
                source, w_block(t, q, mine), sem.home_send.at[t, n], sem.z_in.at[t, q], (w, c + (c + q + n + 1) % 3)
            )
            for n in range(2)
        ]

    def home_each(t, q, action):
        if t == 0:

            @pl.when(mine == 3)
            def _():
                for copy in home_sends(t, q, r.w_out):
                    action(copy)

            @pl.when(mine != 3)
            def _():
                for copy in home_sends(t, q, r.w_qkv.at[jnp.minimum(mine, 2)]):
                    action(copy)

        else:
            for copy in home_sends(t, q, (r.w_up, r.w_down)[t - 1].at[pl.ds(pl.multiple_of(mine * block, 32), block)]):
                action(copy)

    def edge_copy(t, q):
        ref = w_block(t, q, mine)
        return remote(ref, ref, sem.edge_send.at[t, q], sem.z_in.at[t, q], (w, edge))

    def w_copy(t, q, n):
        index, start, count, device = (
            (mine, 0, block, next_x),
            (mine, 0, block, next_y),
            (block_x, 0, block // 2, next_y),
            (block_y, block // 2, block // 2, next_x),
        )[n]
        ref = w_block(t, q, index, start, count)
        return remote(ref, ref, sem.w_send.at[t, q, n], sem.w_in.at[t, q, n], device)

    def weights_start(t):
        for q in range(2):

            @pl.when(far[q] == 0)
            def _():
                home_each(t, q, lambda copy: copy.start())
                for copy in home_copies(t, q):
                    copy.start()

    def weights_own(t):
        for q in range(2):

            @pl.when(far[q] != 0)
            def _():
                landed(w_block(t, q, mine), sem.z_in.at[t, q])

                @pl.when(z == middle)
                def _():
                    edge_copy(t, q).start()

                w_copy(t, q, 0).start()
                w_copy(t, q, 1).start()

    def weights_pass(t):
        for q in range(2):

            @pl.when(far[q] != 0)
            def _():
                landed(w_block(t, q, block_x), sem.w_in.at[t, q, 0])
                w_copy(t, q, 2).start()
                landed(w_block(t, q, block_y), sem.w_in.at[t, q, 1])
                w_copy(t, q, 3).start()

    def weights_done(t):
        for q in range(2):

            @pl.when(far[q] != 0)
            def _():
                landed(w_block(t, q, block_d, 0, block // 2), sem.w_in.at[t, q, 2])
                landed(w_block(t, q, block_d, block // 2, block // 2), sem.w_in.at[t, q, 3])

            @pl.when(far[q] == 0)
            def _():
                for copy in home_copies(t, q):
                    copy.wait()

    def weights_sent(t):
        for q in range(2):

            @pl.when(far[q] == 0)
            def _():
                home_each(t, q, lambda copy: copy.wait_send())

            @pl.when(far[q] != 0)
            def _():
                for n in range(4):
                    w_copy(t, q, n).wait_send()

                @pl.when(z == middle)
                def _():
                    edge_copy(t, q).wait_send()

    stage = (r.probs.at[1], r.g_ff.at[0, 0])
    rests = 2 * 128

    def row_copies(kind, j):
        device = (w - c + j % 2, 2 * c + j // 2)
        own = (c == j % 2) & (2 * c + j // 2 == z)
        target = (r.x_low, r.dy_low)[kind]
        ends = (
            (
                stage[kind].at[pl.ds((j % 2) * part, part), pl.ds((j // 2) * 128, 128)],
                target.at[
                    pl.ds((j % 2) * part, part),
                    pl.ds(pl.multiple_of((z // 2) * (size // 2) + (z % 2) * 256, 128), 128),
                ],
            ),
            (stage[kind].at[pl.ds(j * (part // 2), part // 2), pl.ds(rests, 128)], r.rest.at[kind, z]),
        )
        here = [
            pltpu.make_async_copy(source, dest, sem.x_in.at[kind, z, n]) for n, (source, dest) in enumerate(ends)
        ]
        there = [
            remote(source, dest, sem.x_send.at[kind, j, n], sem.x_in.at[kind, z, n], device)
            for n, (source, dest) in enumerate(ends)
        ]
        return own, here, there

    spans_own = [r.lengths[0, i] for i in range(slots)]
    shift = jnp.where(
        (spans_own[0] >= spans_own[1]) & (spans_own[0] >= spans_own[2]),
        0,
        jnp.where(spans_own[1] >= spans_own[2], spans_own[0], spans_own[0] + spans_own[1]),
    )

    def unit(count, first=0, total=part):
        row = lax.broadcasted_iota(jnp.int32, (count, 1), 0) + first
        column = lax.broadcasted_iota(jnp.int32, (1, total), 1)
        return jnp.where(row == column, 1.0, 0.0).astype(BF16)

    def turn_rows(kind):
        back = jnp.where(shift == 0, 0, rows - shift)
        r.raw[kind] = pltpu.roll(r.raw[kind].astype(F32), back, 1).astype(BF16)
        same = unit(part)
        r.tail[...] = jnp.zeros_like(r.tail)
        for j in range(4):
            turned = nt(same, r.raw[kind, :, j * part : (j + 1) * part])
            main = turned[:, :128]
            r.tail[:, : width - 128] = turned[:, 128:]
            tail = r.tail[...]
            lane = lax.broadcasted_iota(jnp.int32, main.shape, 1)
            main_turned = pltpu.roll(main, 64, 1)
            tail_turned = pltpu.roll(tail, 64, 1)
            full = jnp.where(odd, jnp.where(lane < 64, main_turned, tail_turned), main)
            left = jnp.where(odd, jnp.where(lane < 64, 0.0, main_turned), tail)
            stage[kind][(j % 2) * part : (j % 2 + 1) * part, (j // 2) * 128 : (j // 2 + 1) * 128] = full.astype(BF16)
            packed = left[: part // 2] + pltpu.roll(left[part // 2 :], 64, 1)
            stage[kind][j * (part // 2) : (j + 1) * (part // 2), rests : rests + 128] = packed.astype(BF16)

    def rows_start(kind):
        for j in range(4):
            own, here, there = row_copies(kind, j)

            @pl.when(own)
            def _():
                for copy in here:
                    copy.start()

            @pl.when(jnp.logical_not(own))
            def _():
                for copy in there:
                    copy.start()

    def rows_sent(kind):
        for j in range(4):
            own, _, there = row_copies(kind, j)

            @pl.when(jnp.logical_not(own))
            def _():
                for copy in there:
                    copy.wait_send()

    own_rows = pl.ds(pl.multiple_of(c * part, 128), part)
    other_rows = pl.ds(pl.multiple_of((1 - c) * part, 128), part)

    def pair_rows(kind):
        target = (r.x_low, r.dy_low)[kind]
        return remote(target.at[own_rows], target.at[own_rows], sem.pair.at[kind], sem.pair_in.at[kind], pair)

    def rows_join(kind):
        target = (r.x_low, r.dy_low)[kind]
        for slot in range(4):
            at = (slot // 2) * (size // 2) + (slot % 2) * 256
            landed(target.at[own_rows, pl.ds(at, 128)], sem.x_in.at[kind, slot, 0])
            landed(r.rest.at[kind, slot], sem.x_in.at[kind, slot, 1])
        for g in range(2):
            even, odds = r.rest[kind, 2 * g].astype(F32), r.rest[kind, 2 * g + 1].astype(F32)
            lane = lax.broadcasted_iota(jnp.int32, even.shape, 1)
            upper = jnp.where(lane < 64, even, odds)
            lower = pltpu.roll(jnp.where(lane < 64, odds, even), 64, 1)
            at = pl.ds(g * (size // 2) + 128, 128)
            base = pl.multiple_of(c * part, 128)
            target[pl.ds(base, part // 2), at] = upper.astype(BF16)
            target[pl.ds(base + part // 2, part // 2), at] = lower.astype(BF16)
        pair_rows(kind).start()

    def rows_whole(kind):
        target = (r.x_low, r.dy_low)[kind]
        landed(target.at[other_rows], sem.pair_in.at[kind])

    def part_copy(n, ref, s, start):
        i = start // TILE
        return remote(ref.at[0, s], ref.at[1, s], sem.part_send.at[n, i], sem.part_in.at[n, i], pair)

    def sharing(n, ref):
        return lambda s, start: part_copy(n, ref, s, start).start()

    def arriving(n, ref):
        def wait(s, start):
            copy = part_copy(n, ref, s, start)
            copy.wait_recv()
            copy.wait_send()

        return wait

    def g_block(t, q, index, start=0, count=block):
        if t == 0:
            return r.g_attn.at[index, pl.ds(q * block + start, count)]
        return r.g_ff.at[t - 1, q, pl.ds(pl.multiple_of(index * block + start, 32), count)]

    def add_to(target, terms):
        def step(s, start):
            total = target[s, :].astype(F32)
            for term in terms:
                total = total + term[s, :].astype(F32)
            target[s, :] = total.astype(BF16)

        tiles(target.shape[0], step, 32)

    def g_copy(t, q, n):
        source, dest, device = (
            (g_block(t, q, block_d, 0, block // 2), r.near_half.at[t, q, 0], next_y),
            (g_block(t, q, block_d, block // 2, block // 2), r.near_half.at[t, q, 1], next_x),
            (g_block(t, q, block_x), r.near_full.at[t, q, 0], next_x),
            (g_block(t, q, block_y), r.near_full.at[t, q, 1], next_y),
        )[n]
        return remote(source, dest, sem.g_send.at[t, q, n], sem.g_in.at[t, q, n], device)

    def g_home(t, q, slot):
        return remote(
            g_block(t, q, mine), r.from_z.at[t, slot], sem.g_send.at[t, q, 4], sem.gz_in.at[t, slot], (w, 2 * c + q)
        )

    def g_edge(t, q):
        return remote(g_block(t, q, mine), r.from_z.at[t, q], sem.g_send.at[t, q, 4], sem.gz_in.at[t, q], (w, middle))

    def grads_start(t, q):
        g_copy(t, q, 0).start()
        g_copy(t, q, 1).start()

    def grads_second(t, q):
        g_copy(t, q, 0).wait_recv()
        add_to(g_block(t, q, block_x, 0, block // 2), [r.near_half.at[t, q, 0]])
        g_copy(t, q, 2).start()
        g_copy(t, q, 1).wait_recv()
        add_to(g_block(t, q, block_y, block // 2, block // 2), [r.near_half.at[t, q, 1]])
        g_copy(t, q, 3).start()

    def grads_third(t):
        for q in range(2):
            g_copy(t, q, 2).wait_recv()
            g_copy(t, q, 3).wait_recv()
            add_to(g_block(t, q, mine), [r.near_full.at[t, q, 0], r.near_full.at[t, q, 1]])

            if t == 0:

                @pl.when(far[q] != 0)
                def _():
                    g_home(t, q, far[q] - 1).start()

            else:

                @pl.when(z == edge)
                def _():
                    g_edge(t, q).start()

                @pl.when((far[q] != 0) & (z != edge) & (z != middle))
                def _():
                    g_home(t, q, 0).start()

    def grads_middle(t):
        @pl.when(z == middle)
        def _():
            for q in range(2):
                landed(r.from_z.at[t, q], sem.gz_in.at[t, q])
                add_to(g_block(t, q, mine), [r.from_z.at[t, q]])
                g_home(t, q, 1).start()

    def out_block(t, index, start=0, count=block):
        return r.g_out.at[t, pl.ds(pl.multiple_of(index * block + start, 32), count)]

    def end_local(t, q):
        return pltpu.make_async_copy(g_block(t, q, mine), out_block(t, mine), sem.end_in.at[t, 4])

    def end_copy(t, q, n):
        if n < 2:
            return remote(
                g_block(t, q, mine), out_block(t, mine), sem.end_send.at[t, n], sem.end_in.at[t, n],
                (next_x, next_y)[n],
            )
        ref = out_block(t, block_x, 0, block // 2) if n == 2 else out_block(t, block_y, block // 2, block // 2)
        return remote(ref, ref, sem.end_send.at[t, n], sem.end_in.at[t, n], (next_y, next_x)[n - 2])

    def end_pair(t, n):
        ref = out_block(t, (mine, block_x, block_y, block_d)[n])
        return remote(ref, ref, sem.end_send.at[t, 4 + n], sem.end_in.at[t, 5 + n], pair)

    def group_copy(t, q, step):
        return remote(
            g_block(t, q, mine), r.groups.at[t, step], sem.group_send.at[t, step], sem.group_in.at[t, step],
            ((w + 8 * step) % n_wide, z),
        )

    def grads_fourth(t):
        for q in range(2):

            @pl.when(far[q] == 0)
            def _():
                count = 3 if t == 0 else 2
                for slot in range(count):
                    landed(r.from_z.at[t, slot], sem.gz_in.at[t, slot])
                add_to(g_block(t, q, mine), [r.from_z.at[t, slot] for slot in range(count)])
                for step in range(1, groups):
                    group_copy(t, q, step).start()
                for step in range(1, groups):
                    group_copy(t, q, step).wait()
                for step in range(1, groups):
                    load = pltpu.make_async_copy(r.groups.at[t, step], r.from_z.at[t, 0], sem.group_load.at[t])
                    load.start()
                    load.wait()
                    add_to(g_block(t, q, mine), [r.from_z.at[t, 0]])
                end_local(t, q).start()
                end_copy(t, q, 0).start()
                end_copy(t, q, 1).start()

    def grads_fifth(t):
        for q in range(2):

            @pl.when(far[q] == 0)
            def _():
                landed(out_block(t, block_x), sem.end_in.at[t, 0])
                end_copy(t, q, 2).start()
                end_pair(t, 1).start()
                landed(out_block(t, block_y), sem.end_in.at[t, 1])
                end_copy(t, q, 3).start()
                end_pair(t, 2).start()
                end_local(t, q).wait()
                end_pair(t, 0).start()

    def grads_sixth(t):
        for q in range(2):

            @pl.when(far[q] == 0)
            def _():
                landed(out_block(t, block_d, 0, block // 2), sem.end_in.at[t, 2])
                landed(out_block(t, block_d, block // 2, block // 2), sem.end_in.at[t, 3])
                end_pair(t, 3).start()

    def grads_done(t):
        for q in range(2):
            for n in range(4):
                g_copy(t, q, n).wait_send()

            @pl.when(far[q] != 0)
            def _():
                g_home(t, q, 0).wait_send()

            @pl.when(far[q] == 0)
            def _():
                for n in range(4):
                    end_copy(t, q, n).wait_send()
                for n in range(4):
                    end_pair(t, n).wait_send()

        @pl.when(jnp.logical_not(home))
        def _():
            for index in range(4):
                landed(out_block(t, (mine, block_x, block_y, block_d)[index]), sem.end_in.at[t, 5 + index])

    def result_copies(kind, source, dest):
        window = pl.ds((dest // 2) * (size // 2) + (dest % 2) * 256, 128)
        slot = 2 * (z % 2) + c
        own = home & (z == dest)
        mains, rests_in = ((r.out_o, r.out_r), (r.in_o, r.in_r))[kind]
        ends = (
            (source.at[own_rows, window], mains.at[slot]),
            (r.result_rest.at[kind, dest], rests_in.at[slot]),
        )
        here = [
            pltpu.make_async_copy(ref, target, sem.out_in.at[kind, slot, n]) for n, (ref, target) in enumerate(ends)
        ]
        there = [
            remote(
                ref, target, sem.out_send.at[kind, dest, n], sem.out_in.at[kind, slot, n], (w - c + z // 2, dest)
            )
            for n, (ref, target) in enumerate(ends)
        ]
        return own, here, there

    def results_start(kind, source):
        for g in range(2):
            at = pl.ds(g * (size // 2) + 128, 128)
            base = pl.multiple_of(c * part, 128)
            upper = source[pl.ds(base, part // 2), at].astype(F32)
            lower = pltpu.roll(source[pl.ds(base + part // 2, part // 2), at].astype(F32), 64, 1)
            lane = lax.broadcasted_iota(jnp.int32, upper.shape, 1)
            r.result_rest[kind, 2 * g] = jnp.where(lane < 64, upper, lower).astype(BF16)
            r.result_rest[kind, 2 * g + 1] = jnp.where(lane < 64, lower, upper).astype(BF16)
        for dest in range(4):
            own, here, there = result_copies(kind, source, dest)

            @pl.when(own)
            def _():
                for copy in here:
                    copy.start()

            @pl.when(jnp.logical_not(own))
            def _():
                for copy in there:
                    copy.start()

    def results_done(kind, source):
        mains, rests_in = ((r.out_o, r.out_r), (r.in_o, r.in_r))[kind]
        for slot in range(4):
            landed(mains.at[slot], sem.out_in.at[kind, slot, 0])
            landed(rests_in.at[slot], sem.out_in.at[kind, slot, 1])
        for dest in range(4):
            own, _, there = result_copies(kind, source, dest)

            @pl.when(jnp.logical_not(own))
            def _():
                for copy in there:
                    copy.wait_send()

    def results_turn(kind, stage_at, target, stage_out):
        mains, rests_in = ((r.out_o, r.out_r), (r.in_o, r.in_r))[kind]
        loads = []
        for slot in range(4):
            main_at = stage_at.at[pl.ds((slot // 2) * part, part), pl.ds((slot % 2) * 128, 128)]
            rest_at = stage_at.at[pl.ds(slot * (part // 2), part // 2), pl.ds(256, 128)]
            loads.append(pltpu.make_async_copy(mains.at[slot], main_at, sem.load.at[14 + slot]))
            loads.append(pltpu.make_async_copy(rests_in.at[slot], rest_at, sem.load.at[20 + slot]))
        for load in loads:
            load.start()
        for load in loads:
            load.wait()
        same, upper, lower = unit(part), unit(part // 2), unit(part // 2, part // 2)
        pieces = []
        for slot in range(4):
            main = tn(stage_at[(slot // 2) * part : (slot // 2 + 1) * part, (slot % 2) * 128 : (slot % 2 + 1) * 128], same)
            packed = stage_at[slot * (part // 2) : (slot + 1) * (part // 2), 256:384]
            first, second = tn(packed, upper), tn(packed, lower)
            rest = jnp.where(odd, first[64:] + second[:64], first[:64] + second[64:])
            pieces.append(
                jnp.where(odd, jnp.concatenate([rest, main], axis=0), jnp.concatenate([main, rest], axis=0))
            )
        turned = pltpu.roll(jnp.concatenate(pieces, axis=1), shift, 1).astype(stage_out.dtype)
        stores = []
        for n in range(2):
            stage_out[n * width : (n + 1) * width, :] = turned[:, n * half : (n + 1) * half]
            stores.append(
                pltpu.make_async_copy(
                    stage_out.at[pl.ds(n * width, width)], target.at[:, pl.ds(n * half, half)], sem.load.at[18 + n]
                )
            )
            stores[-1].start()
        for store in stores:
            store.wait()

    w_ada_again = r.slope.at[0]
    ada_loads = [
        pltpu.make_async_copy(
            r.w_ada.at[:, pl.ds(i * size, size)], w_ada_again.at[pl.ds(i * cond, cond)], sem.load.at[7 + i]
        )
        for i in range(6)
    ]

    def finish_small():
        per_slab = half // (4 * MSG_ROWS)
        count = 2 * planes
        slabs = -(-count // per_slab)
        loads = []
        for i in range(count):
            place = r.probs.at[i // per_slab, pl.ds((i % per_slab) * 4 * MSG_ROWS, 4 * MSG_ROWS)]
            source = r.messages.at[i // planes, i % planes]
            loads += [
                pltpu.make_async_copy(source.at[j], place.at[pl.ds(j * MSG_ROWS, MSG_ROWS)], sem.msg_load.at[i, j])
                for j in range(4)
            ]
        for load in loads:
            load.start()
        for load in loads + ada_loads:
            load.wait()
        totals = [None, None]
        ada = [None] * 6
        for n in range(slabs):
            used = min(count - n * per_slab, per_slab) * 4 * MSG_ROWS
            every = r.probs[n, :used, :]
            column = lax.broadcasted_iota(jnp.int32, (MSG_ROWS, used), 1)
            row = lax.broadcasted_iota(jnp.int32, (MSG_ROWS, used), 0)
            early = column + n * half < planes * 4 * MSG_ROWS
            for part_of in range(2):
                wanted = (column % MSG_ROWS == row) & (early if part_of == 0 else jnp.logical_not(early))
                term = nn(jnp.where(wanted, 1.0, 0.0).astype(BF16), every)
                totals[part_of] = term if totals[part_of] is None else totals[part_of] + term
            contexts = every[:, :cond].astype(F32)
            at = lax.broadcasted_iota(jnp.int32, contexts.shape, 0) % MSG_ROWS
            contexts = jnp.where(at == MSG_CONTEXT, contexts, 0.0)
            for i in range(6):
                moved = pltpu.roll(contexts, used - MSG_CONTEXT + i, 0).astype(BF16)
                term = tn(moved, every)
                ada[i] = term if ada[i] is None else ada[i] + term
        for i in range(6):
            r.grad_one[i * cond : (i + 1) * cond, :] = ada[i]
        r.small[...] = totals[0] + totals[1]
        up_rows = jnp.where(z // 2 == 0, totals[0][MSG_B_UP : MSG_B_UP + 2], totals[1][MSG_B_UP : MSG_B_UP + 2])
        r.small[MSG_B_UP : MSG_B_UP + 1, :] = jnp.where(odd, up_rows[1:2], up_rows[0:1])
        own_slot = jnp.where(
            (spans_own[0] >= spans_own[1]) & (spans_own[0] >= spans_own[2]),
            0,
            jnp.where(spans_own[1] >= spans_own[2], 1, 2),
        )
        place = lax.broadcasted_iota(jnp.int32, (8, 1), 0)
        grads = jnp.zeros((8, cond), F32)
        for half_at, seg, after in ((0, 0, 0), (1, 0, 1), (1, 1, 2)):
            group_at = seg * planes + plane_at
            base = (group_at % per_slab) * 4 * MSG_ROWS + (2 * c + half_at) * MSG_ROWS
            rows_at = r.probs[group_at // per_slab, pl.ds(pl.multiple_of(base, MSG_ROWS), MSG_ROWS), :]
            row = lax.broadcasted_iota(jnp.int32, (MSG_ROWS, 1), 0)
            total = jnp.zeros((MSG_ROWS, cond), F32)
            for i in range(6):
                total = total + jnp.where(row == i, nt(rows_at, w_ada_again[i * cond : (i + 1) * cond, :]), 0.0)
            slot = own_slot + after
            slot = jnp.where(slot >= slots, slot - slots, slot)
            grads = grads + jnp.where(place == slot, jnp.sum(total, axis=0, keepdims=True), 0.0)
        times = r.info[0]
        gate = 1.0 / (1.0 + jnp.exp(-times))
        r.context[...] = grads * (gate + times * gate * (1.0 - gate))
        copies = [
            pltpu.make_async_copy(r.grad_one.at[pl.ds(i * cond, cond)], r.ada_out.at[:, pl.ds(i * size, size)], sem.end_small.at[i])
            for i in range(6)
        ]
        copies += [
            pltpu.make_async_copy(r.small.at[i], r.b_ada_out.at[pl.ds(i * size, size)], sem.end_small.at[6 + i])
            for i in range(6)
        ]
        for i, (row, ref) in enumerate(
            ((MSG_B_DOWN, r.b_down_out), (MSG_GAIN_ONE, r.gain_one_out), (MSG_GAIN_TWO, r.gain_two_out), (MSG_B_UP, r.b_up_out))
        ):
            copies.append(pltpu.make_async_copy(r.small.at[row], ref, sem.end_small.at[12 + i]))
        copies.append(pltpu.make_async_copy(r.context.at[pl.ds(0, slots)], r.time_out, sem.end_small.at[16]))
        for copy in copies:
            copy.start()
        return copies

    time_load.wait()
    lane = lax.broadcasted_iota(jnp.int32, (1, 128), 1)
    length_row = jnp.zeros((1, 128), F32)
    for i in range(slots):
        length_row = jnp.where(lane == i, r.lengths[0, i].astype(F32), length_row)
    r.info[0, slots : slots + 1, :] = length_row
    for load in loads[2:6]:
        load.wait()
    r.b_own[...] = r.small[0:8, :]

    pl.semaphore_wait(barrier, len(peers))
    weights_start(0)
    info_copy = remote(r.info.at[0], r.info.at[1], sem.pair.at[2], sem.pair_in.at[2], pair)
    info_copy.start()
    b_copies = [
        remote(r.b_own, r.b_all.at[z], sem.b_send.at[dz], sem.b_in.at[dz], (w, (z + dz) % 4)) for dz in range(1, 4)
    ]
    for copy in b_copies:
        copy.start()
    loads[0].wait()
    turn_rows(0)
    rows_start(0)

    info_copy.wait()
    info = jnp.where(home, r.info[0], r.info[1])
    context = info / (1.0 + jnp.exp(-info))
    context_low = context.astype(BF16)
    spans = [info[slots : slots + 1, i : i + 1] for i in range(slots)]
    longest = [
        (spans[0] >= spans[1]) & (spans[0] >= spans[2]),
        (spans[1] > spans[0]) & (spans[1] >= spans[2]),
        (spans[2] > spans[0]) & (spans[2] > spans[1]),
    ]

    def slot_after(shift):
        return [longest[(i - shift) % slots] for i in range(slots)]

    def pick(flags, values):
        total = None
        for flag, value in zip(flags, values):
            term = jnp.where(flag, value, 0.0)
            total = term if total is None else total + term
        return total

    flags_a = [jnp.where(odd, after.astype(F32), at.astype(F32)) > 0.5 for after, at in zip(slot_after(1), longest)]
    flags_b = [jnp.where(odd, after.astype(F32), at.astype(F32)) > 0.5 for after, at in zip(slot_after(2), longest)]
    bound = jnp.where(odd, pick(slot_after(1), spans), float(half))
    r.context[0:1, :] = pick(flags_a, [context[i : i + 1, :] for i in range(slots)])
    r.context[1:2, :] = pick(flags_b, [context[i : i + 1, :] for i in range(slots)])
    for load in loads[6:]:
        load.wait()
    rises = {}
    for i in range(6):
        modulation = nn(context_low, w_ada[i * cond : (i + 1) * cond, :]) + r.small[ROW_B_ADA + i : ROW_B_ADA + i + 1, :]
        for seg, flags in enumerate((flags_a, flags_b)):
            row = pick(flags, [modulation[n : n + 1, :] for n in range(slots)])
            if i in (1, 4):
                gain = r.small[ROW_GAIN_ONE : ROW_GAIN_ONE + 1, :] if i == 1 else r.small[ROW_GAIN_TWO : ROW_GAIN_TWO + 1, :]
                rise = 8 * seg + (RISE_ONE if i == 1 else RISE_TWO)
                r.mods[rise : rise + 1, :] = 1.0 + row
                row = gain * (1.0 + row)
            at = 8 * seg + (SHIFT_ONE, GAIN_ONE, GATE_ONE, SHIFT_TWO, GAIN_TWO, GATE_TWO)[i]
            r.mods[at : at + 1, :] = row
    inverse = jnp.exp((lane % (HD // 2)).astype(F32) * (-9.210340371976184 / (HD // 2)))
    signs = jnp.where(lane % HD < HD // 2, -1.0, 1.0)

    def tables(s, start):
        row = (lax.broadcasted_iota(jnp.int32, (TILE, 1), 0) + start).astype(F32)
        angles = jnp.where(row < bound, row, row - bound) * inverse
        r.cosine[s, :] = jnp.cos(angles)
        r.sine[s, :] = jnp.sin(angles) * signs

    tiles(half, tables)
    r.scales[...] = jnp.zeros_like(r.scales)
    r.sums[...] = jnp.zeros_like(r.sums)
    r.bias_up[...] = jnp.zeros_like(r.bias_up)
    weights_own(0)
    loads[1].wait()
    turn_rows(1)
    for n, copy in enumerate(b_copies):
        landed(r.b_all.at[(z + 3 - n) % 4], sem.b_in.at[n + 1])
    r.b_all[z] = r.b_own[...]
    weights_pass(0)
    weights_start(1)
    rows_join(0)
    weights_done(0)

    def project_some(i, carry):
        @pl.when(i == 2)
        def _():
            rows_whole(0)

        project(
            bound, ((2 * c + i) % 4) * (part // 2), part // 2, r.x_low, r.mods, r.cosine, r.sine, r.w_attn, r.in_one,
            r.q, r.k, r.v,
        )
        return carry

    lax.fori_loop(0, 4, project_some, 0)
    weights_start(2)
    weights_own(1)
    rows_sent(0)
    attend(bound, 0, r.q, r.k, r.v, r.probs, r.scales, r.mixed)
    weights_pass(1)
    rows_start(1)
    attend(bound, 1, r.q, r.k, r.v, r.probs, r.scales, r.mixed)
    weights_own(2)
    attend(bound, 2, r.q, r.k, r.v, r.probs, r.scales, r.mixed)
    mix_out(r.mixed, r.w_attn, r.attn_part, sharing(0, r.attn_part))
    weights_done(1)
    b_up = jnp.where(c == 0, r.b_all[0, 0:1, :], r.b_all[2, 0:1, :]), jnp.where(c == 0, r.b_all[1, 0:1, :], r.b_all[3, 0:1, :])
    feed_up(
        bound, r.x_low, r.mods, r.attn_part, r.w_ff.at[0], b_up, r.in_two, r.act, r.slope, arriving(0, r.attn_part)
    )
    weights_pass(2)
    rows_join(1)
    rows_whole(1)
    rows_sent(1)
    feed_grads(bound, r.dy_low, r.mods, r.feed_low, r.sums)
    for q in range(2):
        weight_grad(r.act.at[q], r.feed_low, r.g_ff.at[1, q])
        grads_start(2, q)
    weights_done(2)
    feed_down(r.act, r.w_ff.at[1], r.feed_part, sharing(1, r.feed_part))
    grads_second(2, 0)
    feed_back(
        r.feed_low, r.slope, r.w_ff.at[0], r.w_ff.at[1], r.bias_up, r.back_part, sharing(2, r.back_part)
    )
    grads_second(2, 1)
    for q in range(2):
        weight_grad(r.in_two, r.slope.at[q], r.g_ff.at[0, q])
        grads_start(1, q)
    b_down = r.small[ROW_B_DOWN : ROW_B_DOWN + 1, :]
    feed_out(
        bound, r.x_low, r.dy_low, r.mods, r.attn_part, r.feed_part, b_down, r.out_low, r.sums, arriving(1, r.feed_part)
    )
    results_start(0, r.out_low)
    norm_two_back(
        bound, r.x_low, r.dy_low, r.mods, r.back_part, r.attn_part, r.w_attn, r.grad_one, r.feed_low, r.grad_mixed,
        r.sums, arriving(2, r.back_part),
    )
    weight_grad(r.mixed, r.feed_low, r.g_attn.at[3])
    grads_third(2)
    grads_second(1, 0)
    for g in range(3):
        attend_back(
            g, r.q, r.k, r.v, r.probs, r.scales, r.mixed, r.grad_mixed, r.cosine, r.sine, r.total_k, r.total_v,
            r.grad_q, r.grad_k, r.grad_v,
        )
        for t, grads in enumerate((r.grad_q, r.grad_k, r.grad_v)):
            r.g_attn[t, g * 128 : (g + 1) * 128, :] = tn(grads[:, lanes(g)], r.in_one[...]).astype(BF16)
        if g == 0:
            grads_second(1, 1)
        if g == 1:
            grads_start(0, 0)
    grads_start(0, 1)
    grads_third(1)
    project_back(r.grad_q, r.grad_k, r.grad_v, r.w_attn, r.act, sharing(3, r.act))
    grads_second(0, 0)
    grads_second(0, 1)
    grads_middle(2)
    norm_one_back(
        bound, r.x_low, r.mods, r.act, r.grad_one, r.in_two, r.sums, arriving(3, r.act)
    )

    def sum_row(piece):
        return jnp.where(c == 0, r.sums[piece : piece + 1, :], r.sums[8 + piece : 9 + piece, :])

    def mod_row(piece):
        return jnp.where(c == 0, r.mods[piece : piece + 1, :], r.mods[8 + piece : 9 + piece, :])

    gain_one = r.small[ROW_GAIN_ONE : ROW_GAIN_ONE + 1, :]
    gain_two = r.small[ROW_GAIN_TWO : ROW_GAIN_TWO + 1, :]
    context_row = jnp.where(c == 0, r.context[0:1, :], r.context[1:2, :])
    message = [
        sum_row(SUM_G1),
        sum_row(SUM_G1N) * gain_one,
        sum_row(SUM_GATE_ONE),
        sum_row(SUM_G2),
        sum_row(SUM_G2N) * gain_two,
        sum_row(SUM_GATE_TWO),
        sum_row(SUM_DY) * mod_row(GATE_TWO),
        sum_row(SUM_G1N) * mod_row(RISE_ONE),
        sum_row(SUM_G2N) * mod_row(RISE_TWO),
        r.bias_up[0:1, :],
        r.bias_up[1:2, :],
        jnp.concatenate([context_row] + [jnp.zeros((1, 128), F32)] * (size // 128 - 1), axis=1),
        jnp.zeros((4, size), F32),
    ]
    r.message[...] = jnp.concatenate(message, axis=0).astype(BF16)
    message_at = r.messages.at[c, plane_at, z]
    message_local = pltpu.make_async_copy(r.message, message_at, sem.m_in.at[0])
    message_local.start()
    message_copies = [
        remote(r.message, message_at, sem.m_send.at[dz], sem.m_in.at[dz], (w, (z + dz) % 4)) for dz in range(1, 4)
    ]
    for copy in message_copies:
        copy.start()
    for load in ada_loads:
        load.start()
    results_start(1, r.in_two)
    results_done(0, r.out_low)
    results_turn(0, r.act.at[0], r.out_t, r.feed_low)
    grads_middle(1)
    grads_third(0)
    grads_fourth(2)
    grads_fourth(1)
    message_local.wait()
    for dz in range(1, 4):
        landed(r.messages.at[c, plane_at, (z + 4 - dz) % 4], sem.m_in.at[dz])
    plane_copies = []
    for step in range(1, planes):
        ref = r.messages.at[c, plane_at]
        plane_copies.append(
            remote(ref, ref, sem.mp_send.at[step], sem.mp_in.at[step], ((w + 2 * step) % n_wide, z))
        )
        plane_copies[-1].start()
    grads_fifth(2)
    results_done(1, r.in_two)
    results_turn(1, r.act.at[1], r.in_t, r.grad_one)
    for step in range(1, planes):
        landed(r.messages.at[c, (plane_at + planes - step) % planes], sem.mp_in.at[step])
    message_pair = remote(r.messages.at[c], r.messages.at[c], sem.m_send.at[4], sem.m_in.at[4], pair)
    message_pair.start()
    grads_fourth(0)
    grads_fifth(1)
    grads_sixth(2)
    landed(r.messages.at[1 - c], sem.m_in.at[4])
    small_ends = finish_small()
    grads_fifth(0)
    grads_sixth(1)
    grads_sixth(0)
    for copy in small_ends:
        copy.wait()

    for t in range(CHUNKS):
        weights_sent(t)
    for kind in range(2):
        pair_rows(kind).wait_send()
    for copy in b_copies + message_copies + plane_copies + [message_pair]:
        copy.wait_send()
    for t in range(CHUNKS):
        grads_done(t)


def layer(n_wide, lengths, x, *others):
    width, rows = x.shape
    w_up, times = others[3], others[-1]
    size = w_up.shape[0]
    slots, cond = times.shape
    buffers, semaphores = scratch_plan(n_wide, rows, width, size, cond)
    anywhere = pl.BlockSpec(memory_space=pl.ANY)
    part, planes, groups = rows // 4, n_wide // 2, n_wide // 8
    outs = (
        ((width, rows), BF16),
        ((width, rows), F32),
        ((4, part, 128), BF16),
        ((4, part, 128), BF16),
        ((4, part // 2, 128), BF16),
        ((4, part // 2, 128), BF16),
        ((CHUNKS, size, size), BF16),
        ((2, planes, 4, MSG_ROWS, size), BF16),
        ((CHUNKS, groups, size // 4, size), BF16),
        ((cond, 6 * size), F32),
        ((6 * size,), F32),
        ((size,), F32),
        ((size,), F32),
        ((size,), F32),
        ((size,), F32),
        ((slots, cond), F32),
    )
    return pl.pallas_call(
        functools.partial(layer_kernel, n_wide, rows, width, size, cond, slots),
        out_shape=tuple(jax.ShapeDtypeStruct(shape, kind) for shape, kind in outs),
        in_specs=[pl.BlockSpec(memory_space=pltpu.SMEM)] + [anywhere] * (1 + len(others)),
        out_specs=(anywhere,) * len(outs),
        scratch_shapes=[pltpu.VMEM(shape, kind) for shape, kind in buffers.values()]
        + [pltpu.SemaphoreType.DMA(shape) for shape in semaphores.values()],
        compiler_params=pltpu.CompilerParams(
            collective_id=0, has_side_effects=True, vmem_limit_bytes=63 * 1024 * 1024
        ),
        name="layer",
    )(lengths, x, *others)


def body(
    n_wide,
    block_input,
    time_embed,
    seq_lengths,
    w_qkv,
    w_out,
    w_up,
    b_up,
    w_down,
    b_down,
    gain_one,
    gain_two,
    w_ada,
    b_ada,
    out_grad,
):
    size = w_up.shape[0]
    quarter = w_qkv.shape[2]
    out_t, in_t, _, _, _, _, g_own, _, _, ada, b_ada_sum, b_down_sum, gain_one_sum, gain_two_sum, b_up_sum, times = layer(
        n_wide, seq_lengths, block_input.T, out_grad.T, jnp.swapaxes(w_qkv, 1, 2), w_out, w_up, w_down, b_up,
        b_down, gain_one, gain_two, w_ada, b_ada, time_embed,
    )
    g_attn = g_own[0].astype(F32)
    grad_qkv = jnp.swapaxes(g_attn[: 3 * quarter].reshape(3, quarter, size), 1, 2)
    return (
        out_t.T,
        in_t.T,
        times,
        grad_qkv,
        g_attn[3 * quarter :],
        g_own[1].astype(F32),
        b_up_sum,
        g_own[2].astype(F32),
        b_down_sum,
        gain_one_sum,
        gain_two_sum,
        ada,
        b_ada_sum,
    )


def solution(mesh):
    return jax.shard_map(
        functools.partial(body, mesh.shape["wide"]),
        mesh=mesh,
        in_specs=(
            P("wide", "narrow"),
            P("wide", None),
            P("wide", None),
            P(None, None, "narrow"),
            P("narrow", None),
            P(None, "narrow"),
            P("narrow"),
            P("narrow", None),
            P(),
            P(),
            P(),
            P(),
            P(),
            P("wide", "narrow"),
        ),
        out_specs=(
            P("wide", "narrow"),
            P("wide", "narrow"),
            P("wide", None),
            P(None, None, "narrow"),
            P("narrow", None),
            P(None, "narrow"),
            P("narrow"),
            P("narrow", None),
            P(),
            P(),
            P(),
            P(),
            P(),
        ),
        check_vma=False,
    )
```

```python
import functools
from types import SimpleNamespace

import jax
import jax.numpy as jnp
from jax import lax
from jax.experimental import pallas as pl
from jax.experimental.pallas import tpu as pltpu
from jax.sharding import PartitionSpec as P

HD = 64
LOG2_E = 1.4426950408889634
epsilon = 1e-05
MESH = pl.DeviceIdType.MESH
CHUNKS = 3
F32 = jnp.float32
BF16 = jnp.bfloat16


def flip(w, bit, step):
    return w + step * (1 - 2 * bit)


def remote(src, dst, send, recv, device):
    return pltpu.make_async_remote_copy(
        src_ref=src, dst_ref=dst, send_sem=send, recv_sem=recv, device_id=device, device_id_type=MESH
    )


def landed(ref, sem):
    pltpu.make_async_copy(ref, ref, sem).wait()


def dot(a, b, dims):
    return lax.dot_general(a, b, (dims, ((), ())), preferred_element_type=F32)


def nn(a, b):
    return dot(a, b, ((1,), (0,)))


def nt(a, b):
    return dot(a, b, ((1,), (1,)))


def tn(a, b):
    return dot(a, b, ((0,), (0,)))


TILE = 256
ATTEND = 384
ATTEND_BACK = 384


def tiles(count, step, size=TILE):
    def run(i, carry):
        step(pl.ds(pl.multiple_of(i * size, size), size), i * size)
        return carry

    lax.fori_loop(0, count // size, run, 0)


def norm_stats(inputs):
    row_mean = jnp.mean(inputs, axis=-1, keepdims=True)
    centered = inputs - row_mean
    variance = jnp.mean(centered * centered, axis=-1, keepdims=True)
    scaled = lax.rsqrt(variance + epsilon)
    return (centered * scaled, scaled)


def norm_back(grad_normed, normed, scaled):
    first_term = jnp.mean(grad_normed, axis=-1, keepdims=True)
    second_term = jnp.mean(grad_normed * normed, axis=-1, keepdims=True)
    return scaled * (grad_normed - first_term - normed * second_term)


GAIN_ONE, SHIFT_ONE, GATE_ONE, GAIN_TWO, SHIFT_TWO, GATE_TWO, RISE_ONE, RISE_TWO = range(8)
SUM_G1, SUM_G1N, SUM_GATE_ONE, SUM_G2, SUM_G2N, SUM_GATE_TWO, SUM_DY = range(7)


def chosen(mods, first, piece):
    return jnp.where(first, mods[piece : piece + 1, :], mods[8 + piece : 9 + piece, :])


def first_rows(bound, start, count):
    return (lax.broadcasted_iota(jnp.int32, (count, 1), 0) + start).astype(F32) < bound


def add_sums(sums, piece, first, values):
    total = jnp.sum(values, axis=0, keepdims=True)
    head = jnp.sum(jnp.where(first, values, 0.0), axis=0, keepdims=True)
    sums[piece : piece + 1, :] += head
    sums[8 + piece : 9 + piece, :] += total - head


def swapped(pair):
    lane = lax.broadcasted_iota(jnp.int32, pair.shape, 1)
    return jnp.where(lane % HD < HD // 2, pltpu.roll(pair, 128 - HD // 2, 1), pltpu.roll(pair, HD // 2, 1))


def lanes(g):
    return pl.ds(g * 128, 128)


def head_only(pair, hh):
    lane = lax.broadcasted_iota(jnp.int32, pair.shape, 1)
    return jnp.where((lane < HD) == (hh == 0), pair, jnp.zeros_like(pair))


def project(bound, start, rows, x, mods, cosine, sine, w_attn, in_one, q, k, v):
    s = pl.ds(pl.multiple_of(start, 64), rows)
    first = first_rows(bound, start, rows)
    normed, _ = norm_stats(x[s, :].astype(F32))
    low = (normed * chosen(mods, first, GAIN_ONE) + chosen(mods, first, SHIFT_ONE)).astype(BF16)
    in_one[s, :] = low
    cos_rows, sin_rows = cosine[s, :], sine[s, :]
    for t, target in enumerate((q, k)):
        raw = nt(low, w_attn[t])
        for g in range(raw.shape[1] // 128):
            pair = raw[:, g * 128 : (g + 1) * 128]
            turned = pair * cos_rows + swapped(pair) * sin_rows
            target[s, lanes(g)] = (turned * (0.125 * LOG2_E if t == 0 else 1.0)).astype(BF16)
    v[s, :] = nt(low, w_attn[2]).astype(BF16)


def attend(bound, g, q, k, v, probs, scales, mixed):
    rows = q.shape[0]

    def step(s, start):
        first = first_rows(bound, start, ATTEND)
        column = lax.broadcasted_iota(jnp.int32, (1, rows), 1).astype(F32) < bound
        bias = jnp.where(first == column, 0.0, -1e30)
        halves = []
        for hh in range(2):
            scores = nt(head_only(q[s, lanes(g)], hh), k[:, lanes(g)]) + bias
            expos = jnp.exp2(scores - jnp.max(scores, axis=-1, keepdims=True))
            low = expos.astype(BF16)
            probs[2 * g + hh, s, :] = low
            scale = 1.0 / jnp.sum(expos, axis=-1, keepdims=True)
            kept = scales[s, :]
            scales[s, :] = jnp.where(lax.broadcasted_iota(jnp.int32, kept.shape, 1) == 2 * g + hh, scale, kept)
            halves.append(nn(low, v[:, lanes(g)]) * scale)
        lane = lax.broadcasted_iota(jnp.int32, halves[0].shape, 1)
        mixed[s, lanes(g)] = jnp.where(lane < HD, halves[0], halves[1]).astype(BF16)

    tiles(rows, step, ATTEND)


def mix_out(mixed, w_attn, part, share):
    def step(s, start):
        part[0, s, :] = nn(mixed[s, :], w_attn[3]).astype(BF16)
        share(s, start)

    tiles(mixed.shape[0], step)


def both(part, s):
    return part[0, s, :].astype(F32) + part[1, s, :].astype(F32)


def hidden_rows(first, s, x, mods, attn_part):
    return x[s, :].astype(F32) + chosen(mods, first, GATE_ONE) * both(attn_part, s)


def feed_up(bound, x, mods, attn_part, w_up, b_up, in_two, act, slope, arrived):
    def step(s, start):
        arrived(s, start)
        first = first_rows(bound, start, TILE)
        normed, _ = norm_stats(hidden_rows(first, s, x, mods, attn_part))
        low = (normed * chosen(mods, first, GAIN_TWO) + chosen(mods, first, SHIFT_TWO)).astype(BF16)
        in_two[s, :] = low
        for n in range(2):
            pre = nn(low, w_up[n]) + b_up[n]
            square = pre * pre
            bent = jnp.tanh(0.7978845608028654 * pre * (1.0 + 0.044715 * square))
            rise = 0.5 * (1.0 + bent)
            act[n, s, :] = (pre * rise).astype(BF16)
            inner = 0.7978845608028654 + 0.10703222443 * square
            slope[n, s, :] = (rise + 0.5 * pre * (1.0 - bent * bent) * inner).astype(BF16)

    tiles(x.shape[0], step)


def feed_grads(bound, dy, mods, feed_low, sums):
    def step(s, start):
        first = first_rows(bound, start, TILE)
        grads = dy[s, :].astype(F32)
        add_sums(sums, SUM_DY, first, grads)
        feed_low[s, :] = (grads * chosen(mods, first, GATE_TWO)).astype(BF16)

    tiles(dy.shape[0], step)


def feed_down(act, w_down, part, share):
    def step(s, start):
        part[0, s, :] = (nn(act[0, s, :], w_down[0]) + nn(act[1, s, :], w_down[1])).astype(BF16)
        share(s, start)

    tiles(act.shape[1], step)


def feed_out(bound, x, dy, mods, attn_part, feed_part, b_down, out, sums, arrived):
    def step(s, start):
        arrived(s, start)
        first = first_rows(bound, start, TILE)
        rows = both(feed_part, s) + b_down
        out[s, :] = (hidden_rows(first, s, x, mods, attn_part) + chosen(mods, first, GATE_TWO) * rows).astype(BF16)
        add_sums(sums, SUM_GATE_TWO, first, dy[s, :].astype(F32) * rows)

    tiles(dy.shape[0], step)


def feed_back(feed_low, slope, w_down, bias_up):
    def step(s, start):
        low = feed_low[s, :]
        for n in range(2):
            grad_pre = nt(low, w_down[n]) * slope[n, s, :].astype(F32)
            bias_up[n : n + 1, :] += jnp.sum(grad_pre, axis=0, keepdims=True)
            slope[n, s, :] = grad_pre.astype(BF16)

    tiles(feed_low.shape[0], step)


def feed_in_back(pre_low, w_up, part, share):
    def step(s, start):
        part[0, s, :] = (nt(pre_low[0, s, :], w_up[0]) + nt(pre_low[1, s, :], w_up[1])).astype(BF16)
        share(s, start)

    tiles(pre_low.shape[1], step)


def weight_grad(left, right, target):
    def step(s, start):
        target[s, :] = tn(left[:, s], right[...]).astype(BF16)

    size = 384 if left.shape[1] % 384 == 0 else 128
    tiles(left.shape[1], step, size)


def norm_two_back(bound, x, dy, mods, back_part, attn_part, w_attn, grad_one, attn_low, grad_mixed, sums, arrived):
    def step(s, start):
        arrived(s, start)
        first = first_rows(bound, start, TILE)
        grads = both(back_part, s)
        normed, scaled = norm_stats(hidden_rows(first, s, x, mods, attn_part))
        add_sums(sums, SUM_G2, first, grads)
        add_sums(sums, SUM_G2N, first, grads * normed)
        rows = dy[s, :].astype(F32) + norm_back(grads * chosen(mods, first, GAIN_TWO), normed, scaled)
        grad_one[s, :] = rows
        add_sums(sums, SUM_GATE_ONE, first, rows * both(attn_part, s))
        low = (rows * chosen(mods, first, GATE_ONE)).astype(BF16)
        attn_low[s, :] = low
        grad_mixed[s, :] = nt(low, w_attn[3]).astype(BF16)

    tiles(dy.shape[0], step)


def attend_back(g, q, k, v, probs, scales, mixed, grad_mixed, cosine, sine, total_k, total_v, grad_q, grad_k, grad_v):
    rows = q.shape[0]

    def turned_back(pair, s):
        return pair * cosine[s, :] - swapped(pair) * sine[s, :]

    total_k[...] = jnp.zeros_like(total_k)
    total_v[...] = jnp.zeros_like(total_v)

    def step(s, start):
        upstream = grad_mixed[s, lanes(g)]
        product = upstream.astype(F32) * mixed[s, lanes(g)].astype(F32)
        halves = []
        for hh in range(2):
            kept = scales[s, :]
            here = lax.broadcasted_iota(jnp.int32, kept.shape, 1) == 2 * g + hh
            scale = jnp.sum(jnp.where(here, kept, 0.0), axis=-1, keepdims=True)
            row_dot = jnp.sum(head_only(product, hh), axis=-1, keepdims=True) * scale
            up_head = (head_only(upstream, hh).astype(F32) * scale).astype(BF16)
            low = probs[2 * g + hh, s, :]
            grad_weights = nt(up_head, v[:, lanes(g)])
            grad_scores = (low.astype(F32) * (grad_weights - row_dot)).astype(BF16)
            halves.append(nn(grad_scores, k[:, lanes(g)]))
            total_v[...] += tn(low, up_head)
            total_k[...] += tn(grad_scores, head_only(q[s, lanes(g)], hh))
        lane = lax.broadcasted_iota(jnp.int32, halves[0].shape, 1)
        pair = jnp.where(lane < HD, halves[0], halves[1]) * 0.125
        grad_q[s, lanes(g)] = turned_back(pair, s).astype(BF16)

    tiles(rows, step, ATTEND_BACK)

    def finish(s, start):
        grad_k[s, lanes(g)] = turned_back(total_k[s, :] * (1.0 / LOG2_E), s).astype(BF16)
        grad_v[s, lanes(g)] = total_v[s, :].astype(BF16)

    tiles(rows, finish)


def project_back(grad_q, grad_k, grad_v, w_attn, part, share):
    def step(s, start):
        total = nn(grad_q[s, :], w_attn[0]) + nn(grad_k[s, :], w_attn[1]) + nn(grad_v[s, :], w_attn[2])
        part[0, s, :] = total.astype(BF16)
        share(s, start)

    tiles(grad_q.shape[0], step)


def norm_one_back(bound, x, mods, back_part, grad_one, in_grad, sums, arrived):
    def step(s, start):
        arrived(s, start)
        first = first_rows(bound, start, TILE)
        grads = both(back_part, s)
        normed, scaled = norm_stats(x[s, :].astype(F32))
        add_sums(sums, SUM_G1, first, grads)
        add_sums(sums, SUM_G1N, first, grads * normed)
        rows = grad_one[s, :] + norm_back(grads * chosen(mods, first, GAIN_ONE), normed, scaled)
        in_grad[s, :] = rows.astype(BF16)

    tiles(x.shape[0], step)


ROW_B_UP, ROW_B_DOWN, ROW_GAIN_ONE, ROW_GAIN_TWO, ROW_B_ADA = 0, 1, 2, 3, 8
MSG_MOD, MSG_B_DOWN, MSG_GAIN_ONE, MSG_GAIN_TWO, MSG_B_UP, MSG_CONTEXT = 0, 6, 7, 8, 9, 11
MSG_ROWS = 16
Z_SLOT = (0, 3, 5)


def scratch_plan(n_wide, rows, width, size, cond):
    half, heads = rows // 2, 2 * width // HD
    block = size // 4
    buffers = {
        "tail": ((half // 2, 128), F32),
        "small": ((16, size), F32),
        "b_all": ((4, 8, size), F32),
        "b_own": ((8, size), F32),
        "info": ((2, 8, 128), F32),
        "context": ((8, 128), F32),
        "mods": ((16, size), F32),
        "sums": ((16, size), F32),
        "bias_up": ((8, size), F32),
        "message": ((MSG_ROWS, size), BF16),
        "rest": ((2, 4, half // 4, 128), BF16),
        "result_rest": ((2, 4, half // 4, 128), BF16),
        "x_low": ((half, size), BF16),
        "dy_low": ((half, size), BF16),
        "cosine": ((half, 128), F32),
        "sine": ((half, 128), F32),
        "w_attn": ((4, 2 * block, size), BF16),
        "w_ff": ((2, 2, size, size), BF16),
        "in_one": ((half, size), BF16),
        "q": ((half, 2 * width), BF16),
        "k": ((half, 2 * width), BF16),
        "v": ((half, 2 * width), BF16),
        "probs": ((heads, half, half), BF16),
        "scales": ((half, 128), F32),
        "mixed": ((half, 2 * width), BF16),
        "attn_part": ((2, half, size), BF16),
        "feed_part": ((2, half, size), BF16),
        "back_part": ((2, half, size), BF16),
        "in_two": ((half, size), BF16),
        "act": ((2, half, size), BF16),
        "slope": ((2, half, size), BF16),
        "out_low": ((half, size), BF16),
        "feed_low": ((half, size), BF16),
        "grad_one": ((half, size), F32),
        "grad_mixed": ((half, 2 * width), BF16),
        "total_k": ((half, 128), F32),
        "total_v": ((half, 128), F32),
        "grad_q": ((half, 2 * width), BF16),
        "grad_k": ((half, 2 * width), BF16),
        "grad_v": ((half, 2 * width), BF16),
        "g_attn": ((4, 2 * block, size), BF16),
        "g_ff": ((2, 2, size, size), BF16),
        "near_half": ((CHUNKS, 2, 2, block // 2, size), BF16),
        "near_full": ((CHUNKS, 2, 2, block, size), BF16),
        "from_z": ((7, block, size), BF16),
    }
    planes = n_wide // 2
    groups = n_wide // 8
    semaphores = {
        "load": (28,),
        "msg_load": (n_wide, 4),
        "end_small": (17,),
        "pair": (4,),
        "pair_in": (4,),
        "b_send": (4,),
        "b_in": (4,),
        "x_send": (2, 4, 2),
        "x_in": (2, 4, 2),
        "home": (CHUNKS, 4),
        "home_send": (CHUNKS, 2),
        "edge_send": (CHUNKS, 2),
        "z_in": (CHUNKS, 2),
        "w_send": (CHUNKS, 2, 4),
        "w_in": (CHUNKS, 2, 4),
        "part_send": (4, 4),
        "part_in": (4, 4),
        "out_send": (2, 4, 2),
        "out_in": (2, 4, 2),
        "g_send": (CHUNKS, 2, 5),
        "g_in": (CHUNKS, 2, 4),
        "gz_in": (CHUNKS, 3),
        "group_send": (CHUNKS, groups),
        "group_in": (CHUNKS, groups),
        "group_load": (CHUNKS,),
        "end_send": (CHUNKS, 8),
        "end_in": (CHUNKS, 9),
        "m_send": (5,),
        "m_in": (5,),
        "mp_send": (planes,),
        "mp_in": (planes,),
    }
    return buffers, semaphores


def layer_kernel(n_wide, rows, width, size, cond, slots, *refs):
    buffers, semaphores = scratch_plan(n_wide, rows, width, size, cond)
    names = (
        ["lengths", "x", "dy", "w_qkv", "w_out", "w_up", "w_down", "b_up", "b_down", "gain_one", "gain_two", "w_ada"]
        + ["b_ada", "times", "out_t", "in_t", "out_o", "in_o", "out_r", "in_r", "g_heads", "g_up", "g_down", "messages", "groups"]
        + ["ada_out", "b_ada_out", "b_down_out", "gain_one_out", "gain_two_out", "b_up_out", "time_out"]
        + list(buffers)
    )
    r = SimpleNamespace(**dict(zip(names, refs)))
    sem = SimpleNamespace(**dict(zip(semaphores, refs[len(names) :])))
    half = rows // 2
    part = half // 2
    block = size // 4
    planes, groups = n_wide // 2, n_wide // 8

    w = lax.axis_index("wide")
    z = lax.axis_index("narrow")
    c, bx, by, plane_at = w % 2, (w // 2) % 2, (w // 4) % 2, w // 2
    pair = (flip(w, c, 1), z)
    next_x, next_y = (flip(w, bx, 2), z), (flip(w, by, 4), z)
    mine = bx + 2 * by
    block_x, block_y, block_d = mine + 1 - 2 * bx, mine + 2 - 4 * by, 3 - mine
    far = [(z - 2 * c - q) % 4 for q in range(2)]
    home = c == z // 2
    odd = z % 2 == 1

    peers = [(w if same else pair[0], (z + dz) % 4) for same in (1, 0) for dz in range(4) if not (same and dz == 0)]
    peers += [((w + 2 * step) % n_wide, z) for step in range(1, planes)]
    barrier = pltpu.get_barrier_semaphore()
    for device in peers:
        pl.semaphore_signal(barrier, inc=1, device_id=device, device_id_type=MESH)

    w_ada = r.probs.at[2]
    raw = r.probs.at[3]
    loads = []
    for i in range(4):
        source = (r.x, r.dy)[i // 2].at[:, pl.ds((i % 2) * half, half)]
        loads.append(pltpu.make_async_copy(source, raw.at[pl.ds(i * width, width)], sem.load.at[(0, 1, 26, 27)[i]]))
    for i, ref in enumerate((r.b_up, r.b_down, r.gain_one, r.gain_two)):
        loads.append(pltpu.make_async_copy(ref, r.small.at[i], sem.load.at[2 + i]))
    for i in range(6):
        piece = pl.ds(i * size, size)
        loads.append(pltpu.make_async_copy(r.b_ada.at[piece], r.small.at[ROW_B_ADA + i], sem.load.at[20 + i]))
    for i in range(6):
        loads.append(
            pltpu.make_async_copy(
                r.w_ada.at[:, pl.ds(i * size, size)], w_ada.at[pl.ds(i * cond, cond)], sem.load.at[7 + i]
            )
        )
    for load in loads:
        load.start()
    r.info[0] = jnp.zeros((8, 128), F32)
    time_load = pltpu.make_async_copy(r.times, r.info.at[0, pl.ds(0, slots)], sem.load.at[13])
    time_load.start()

    def w_block(t, q, index, start=0, count=block):
        if t == 0:
            return r.w_attn.at[index, pl.ds(q * block + start, count)]
        return r.w_ff.at[t - 1, q, pl.ds(pl.multiple_of(index * block + start, 32), count)]

    def home_copies(t, q):
        if t == 0:
            copies = [pltpu.make_async_copy(r.w_qkv.at[i], w_block(0, q, i), sem.home.at[0, i]) for i in range(3)]
            return copies + [pltpu.make_async_copy(r.w_out, w_block(0, q, 3), sem.home.at[0, 3])]
        return [pltpu.make_async_copy((r.w_up, r.w_down)[t - 1], r.w_ff.at[t - 1, q], sem.home.at[t, 0])]

    edge, middle = 3 - 3 * c, 2 - c

    def home_sends(t, q, source):
        return [
            remote(
                source, w_block(t, q, mine), sem.home_send.at[t, n], sem.z_in.at[t, q], (w, c + (c + q + n + 1) % 3)
            )
            for n in range(2)
        ]

    def home_each(t, q, action):
        if t == 0:

            @pl.when(mine == 3)
            def _():
                for copy in home_sends(t, q, r.w_out):
                    action(copy)

            @pl.when(mine != 3)
            def _():
                for copy in home_sends(t, q, r.w_qkv.at[jnp.minimum(mine, 2)]):
                    action(copy)

        else:
            for copy in home_sends(t, q, (r.w_up, r.w_down)[t - 1].at[pl.ds(pl.multiple_of(mine * block, 32), block)]):
                action(copy)

    def edge_copy(t, q):
        ref = w_block(t, q, mine)
        return remote(ref, ref, sem.edge_send.at[t, q], sem.z_in.at[t, q], (w, edge))

    def w_copy(t, q, n):
        index, start, count, device = (
            (mine, 0, block, next_x),
            (mine, 0, block, next_y),
            (block_x, 0, block // 2, next_y),
            (block_y, block // 2, block // 2, next_x),
        )[n]
        ref = w_block(t, q, index, start, count)
        return remote(ref, ref, sem.w_send.at[t, q, n], sem.w_in.at[t, q, n], device)

    def weights_start(t):
        for q in range(2):

            @pl.when(far[q] == 0)
            def _():
                home_each(t, q, lambda copy: copy.start())
                for copy in home_copies(t, q):
                    copy.start()

    def weights_own(t, at_edge):
        for q in range(2):

            @pl.when((z == edge) if at_edge else (far[q] != 0) & (z != edge))
            def _():
                landed(w_block(t, q, mine), sem.z_in.at[t, q])

                @pl.when(z == middle)
                def _():
                    edge_copy(t, q).start()

                w_copy(t, q, 0).start()
                w_copy(t, q, 1).start()

    def weights_pass(t):
        for q in range(2):

            @pl.when(far[q] != 0)
            def _():
                landed(w_block(t, q, block_x), sem.w_in.at[t, q, 0])
                w_copy(t, q, 2).start()
                landed(w_block(t, q, block_y), sem.w_in.at[t, q, 1])
                w_copy(t, q, 3).start()

    def weights_done(t):
        for q in range(2):

            @pl.when(far[q] != 0)
            def _():
                landed(w_block(t, q, block_d, 0, block // 2), sem.w_in.at[t, q, 2])
                landed(w_block(t, q, block_d, block // 2, block // 2), sem.w_in.at[t, q, 3])

            @pl.when(far[q] == 0)
            def _():
                for copy in home_copies(t, q):
                    copy.wait()

    def weights_sent(t):
        for q in range(2):

            @pl.when(far[q] == 0)
            def _():
                home_each(t, q, lambda copy: copy.wait_send())

            @pl.when(far[q] != 0)
            def _():
                for n in range(4):
                    w_copy(t, q, n).wait_send()

                @pl.when(z == middle)
                def _():
                    edge_copy(t, q).wait_send()

    stage = (r.probs.at[1], r.g_ff.at[0, 0])
    rests = 2 * 128

    def row_copies(kind, j):
        device = (w - c + j % 2, 2 * c + j // 2)
        own = (c == j % 2) & (2 * c + j // 2 == z)
        target = (r.x_low, r.dy_low)[kind]
        ends = (
            (
                stage[kind].at[pl.ds((j % 2) * part, part), pl.ds((j // 2) * 128, 128)],
                target.at[
                    pl.ds((j % 2) * part, part),
                    pl.ds(pl.multiple_of((z // 2) * (size // 2) + (z % 2) * 256, 128), 128),
                ],
            ),
            (stage[kind].at[pl.ds(j * (part // 2), part // 2), pl.ds(rests, 128)], r.rest.at[kind, z]),
        )
        here = [
            pltpu.make_async_copy(source, dest, sem.x_in.at[kind, z, n]) for n, (source, dest) in enumerate(ends)
        ]
        there = [
            remote(source, dest, sem.x_send.at[kind, j, n], sem.x_in.at[kind, z, n], device)
            for n, (source, dest) in enumerate(ends)
        ]
        return own, here, there

    spans_own = [r.lengths[0, i] for i in range(slots)]
    shift = jnp.where(
        (spans_own[0] >= spans_own[1]) & (spans_own[0] >= spans_own[2]),
        0,
        jnp.where(spans_own[1] >= spans_own[2], spans_own[0], spans_own[0] + spans_own[1]),
    )

    def unit(count, first=0, total=part):
        row = lax.broadcasted_iota(jnp.int32, (count, 1), 0) + first
        column = lax.broadcasted_iota(jnp.int32, (1, total), 1)
        return jnp.where(row == column, 1.0, 0.0).astype(BF16)

    def turn_rows(kind):
        back = jnp.where(shift == 0, 0, rows - shift)
        at = 2 * kind * width
        columns = jnp.concatenate([raw[at : at + width, :], raw[at + width : at + 2 * width, :]], axis=1)
        columns = pltpu.roll(columns.astype(F32), back, 1).astype(BF16)
        raw[at : at + width, :] = columns[:, :half]
        raw[at + width : at + 2 * width, :] = columns[:, half:]
        same = unit(part)
        r.tail[...] = jnp.zeros_like(r.tail)
        for j in range(4):
            row, lane_at = at + (j // 2) * width, (j % 2) * part
            turned = nt(same, raw[row : row + width, lane_at : lane_at + part])
            main = turned[:, :128]
            r.tail[:, : width - 128] = turned[:, 128:]
            tail = r.tail[...]
            lane = lax.broadcasted_iota(jnp.int32, main.shape, 1)
            main_turned = pltpu.roll(main, 64, 1)
            tail_turned = pltpu.roll(tail, 64, 1)
            full = jnp.where(odd, jnp.where(lane < 64, main_turned, tail_turned), main)
            left = jnp.where(odd, jnp.where(lane < 64, 0.0, main_turned), tail)
            stage[kind][(j % 2) * part : (j % 2 + 1) * part, (j // 2) * 128 : (j // 2 + 1) * 128] = full.astype(BF16)
            packed = left[: part // 2] + pltpu.roll(left[part // 2 :], 64, 1)
            stage[kind][j * (part // 2) : (j + 1) * (part // 2), rests : rests + 128] = packed.astype(BF16)

    def rows_start(kind):
        for j in range(4):
            own, here, there = row_copies(kind, j)

            @pl.when(own)
            def _():
                for copy in here:
                    copy.start()

            @pl.when(jnp.logical_not(own))
            def _():
                for copy in there:
                    copy.start()

    def rows_sent(kind):
        for j in range(4):
            own, _, there = row_copies(kind, j)

            @pl.when(jnp.logical_not(own))
            def _():
                for copy in there:
                    copy.wait_send()

    own_rows = pl.ds(pl.multiple_of(c * part, 128), part)
    other_rows = pl.ds(pl.multiple_of((1 - c) * part, 128), part)

    def pair_rows(kind):
        target = (r.x_low, r.dy_low)[kind]
        return remote(target.at[own_rows], target.at[own_rows], sem.pair.at[kind], sem.pair_in.at[kind], pair)

    def rows_join(kind):
        target = (r.x_low, r.dy_low)[kind]
        for slot in range(4):
            at = (slot // 2) * (size // 2) + (slot % 2) * 256
            landed(target.at[own_rows, pl.ds(at, 128)], sem.x_in.at[kind, slot, 0])
            landed(r.rest.at[kind, slot], sem.x_in.at[kind, slot, 1])
        for g in range(2):
            even, odds = r.rest[kind, 2 * g].astype(F32), r.rest[kind, 2 * g + 1].astype(F32)
            lane = lax.broadcasted_iota(jnp.int32, even.shape, 1)
            upper = jnp.where(lane < 64, even, odds)
            lower = pltpu.roll(jnp.where(lane < 64, odds, even), 64, 1)
            at = pl.ds(g * (size // 2) + 128, 128)
            base = pl.multiple_of(c * part, 128)
            target[pl.ds(base, part // 2), at] = upper.astype(BF16)
            target[pl.ds(base + part // 2, part // 2), at] = lower.astype(BF16)
        pair_rows(kind).start()

    def rows_whole(kind):
        target = (r.x_low, r.dy_low)[kind]
        landed(target.at[other_rows], sem.pair_in.at[kind])

    def part_copy(n, ref, s, start):
        i = start // TILE
        return remote(ref.at[0, s], ref.at[1, s], sem.part_send.at[n, i], sem.part_in.at[n, i], pair)

    def sharing(n, ref):
        return lambda s, start: part_copy(n, ref, s, start).start()

    def arriving(n, ref):
        def wait(s, start):
            copy = part_copy(n, ref, s, start)
            copy.wait_recv()
            copy.wait_send()

        return wait

    def g_block(t, q, index, start=0, count=block):
        if t == 0:
            return r.g_attn.at[index, pl.ds(q * block + start, count)]
        return r.g_ff.at[t - 1, q, pl.ds(pl.multiple_of(index * block + start, 32), count)]

    def add_to(target, terms):
        def step(s, start):
            total = target[s, :].astype(F32)
            for term in terms:
                total = total + term[s, :].astype(F32)
            target[s, :] = total.astype(BF16)

        tiles(target.shape[0], step, 32)

    def g_copy(t, q, n):
        source, dest, device = (
            (g_block(t, q, block_d, 0, block // 2), r.near_half.at[t, q, 0], next_y),
            (g_block(t, q, block_d, block // 2, block // 2), r.near_half.at[t, q, 1], next_x),
            (g_block(t, q, block_x), r.near_full.at[t, q, 0], next_x),
            (g_block(t, q, block_y), r.near_full.at[t, q, 1], next_y),
        )[n]
        return remote(source, dest, sem.g_send.at[t, q, n], sem.g_in.at[t, q, n], device)

    def g_home(t, q, slot):
        return remote(
            g_block(t, q, mine), r.from_z.at[Z_SLOT[t] + slot], sem.g_send.at[t, q, 4], sem.gz_in.at[t, slot], (w, 2 * c + q)
        )

    def g_edge(t, q):
        return remote(g_block(t, q, mine), r.from_z.at[Z_SLOT[t] + q], sem.g_send.at[t, q, 4], sem.gz_in.at[t, q], (w, middle))

    def grads_start(t, q):
        g_copy(t, q, 0).start()
        g_copy(t, q, 1).start()

    def grads_second(t, q):
        g_copy(t, q, 0).wait_recv()
        add_to(g_block(t, q, block_x, 0, block // 2), [r.near_half.at[t, q, 0]])
        g_copy(t, q, 2).start()
        g_copy(t, q, 1).wait_recv()
        add_to(g_block(t, q, block_y, block // 2, block // 2), [r.near_half.at[t, q, 1]])
        g_copy(t, q, 3).start()

    def grads_third(t):
        for q in range(2):
            g_copy(t, q, 2).wait_recv()
            g_copy(t, q, 3).wait_recv()
            add_to(g_block(t, q, mine), [r.near_full.at[t, q, 0], r.near_full.at[t, q, 1]])

            if t == 0:

                @pl.when(far[q] != 0)
                def _():
                    g_home(t, q, far[q] - 1).start()

            else:

                @pl.when(z == edge)
                def _():
                    g_edge(t, q).start()

                @pl.when((far[q] != 0) & (z != edge) & (z != middle))
                def _():
                    g_home(t, q, 0).start()

    def grads_middle(t):
        @pl.when(z == middle)
        def _():
            for q in range(2):
                landed(r.from_z.at[Z_SLOT[t] + q], sem.gz_in.at[t, q])
                add_to(g_block(t, q, mine), [r.from_z.at[Z_SLOT[t] + q]])
                g_home(t, q, 1).start()

    def out_block(t, index, start=0, count=block):
        if t == 0:
            return r.g_heads.at[index, pl.ds(start, count)]
        return (r.g_up, r.g_down)[t - 1].at[pl.ds(pl.multiple_of(index * block + start, 32), count)]

    def end_local(t, q):
        return pltpu.make_async_copy(g_block(t, q, mine), out_block(t, mine), sem.end_in.at[t, 4])

    def end_copy(t, q, n):
        if n < 2:
            return remote(
                g_block(t, q, mine), out_block(t, mine), sem.end_send.at[t, n], sem.end_in.at[t, n],
                (next_x, next_y)[n],
            )
        if t == 0:
            return remote(
                g_block(t, q, mine), out_block(t, mine), sem.end_send.at[t, 2], sem.end_in.at[t, 2],
                (flip(next_x[0], by, 4), z),
            )
        ref = out_block(t, block_x, 0, block // 2) if n == 2 else out_block(t, block_y, block // 2, block // 2)
        return remote(ref, ref, sem.end_send.at[t, n], sem.end_in.at[t, n], (next_y, next_x)[n - 2])

    def end_pair(t, n):
        ref = out_block(t, (mine, block_x, block_y, block_d)[n])
        return remote(ref, ref, sem.end_send.at[t, 4 + n], sem.end_in.at[t, 5 + n], pair)

    def group_copy(t, q, step):
        return remote(
            g_block(t, q, mine), r.groups.at[t, step], sem.group_send.at[t, step], sem.group_in.at[t, step],
            ((w + 8 * step) % n_wide, z),
        )

    def grads_fourth(t):
        for q in range(2):

            @pl.when(far[q] == 0)
            def _():
                count = 3 if t == 0 else 2
                for slot in range(count):
                    landed(r.from_z.at[Z_SLOT[t] + slot], sem.gz_in.at[t, slot])
                add_to(g_block(t, q, mine), [r.from_z.at[Z_SLOT[t] + slot] for slot in range(count)])
                for step in range(1, groups):
                    group_copy(t, q, step).start()
                for step in range(1, groups):
                    group_copy(t, q, step).wait()
                for step in range(1, groups):
                    load = pltpu.make_async_copy(r.groups.at[t, step], r.from_z.at[Z_SLOT[t]], sem.group_load.at[t])
                    load.start()
                    load.wait()
                    add_to(g_block(t, q, mine), [r.from_z.at[Z_SLOT[t]]])
                end_local(t, q).start()
                end_copy(t, q, 0).start()
                end_copy(t, q, 1).start()
                if t == 0:
                    end_copy(t, q, 2).start()

    def grads_fifth(t):
        for q in range(2):

            @pl.when(far[q] == 0)
            def _():
                landed(out_block(t, block_x), sem.end_in.at[t, 0])
                if t > 0:
                    end_copy(t, q, 2).start()
                end_pair(t, 1).start()
                landed(out_block(t, block_y), sem.end_in.at[t, 1])
                if t > 0:
                    end_copy(t, q, 3).start()
                end_pair(t, 2).start()
                end_local(t, q).wait()
                end_pair(t, 0).start()

    def grads_sixth(t):
        for q in range(2):

            @pl.when(far[q] == 0)
            def _():
                if t == 0:
                    landed(out_block(t, block_d), sem.end_in.at[t, 2])
                else:
                    landed(out_block(t, block_d, 0, block // 2), sem.end_in.at[t, 2])
                    landed(out_block(t, block_d, block // 2, block // 2), sem.end_in.at[t, 3])
                end_pair(t, 3).start()

    def grads_done(t):
        for q in range(2):
            for n in range(4):
                g_copy(t, q, n).wait_send()

            @pl.when(far[q] != 0)
            def _():
                g_home(t, q, 0).wait_send()

            @pl.when(far[q] == 0)
            def _():
                for n in range(3 if t == 0 else 4):
                    end_copy(t, q, n).wait_send()
                for n in range(4):
                    end_pair(t, n).wait_send()

        @pl.when(jnp.logical_not(home))
        def _():
            for index in range(4):
                landed(out_block(t, (mine, block_x, block_y, block_d)[index]), sem.end_in.at[t, 5 + index])

    def result_copies(kind, source, dest):
        window = pl.ds((dest // 2) * (size // 2) + (dest % 2) * 256, 128)
        slot = 2 * (z % 2) + c
        own = home & (z == dest)
        mains, rests_in = ((r.out_o, r.out_r), (r.in_o, r.in_r))[kind]
        ends = (
            (source.at[own_rows, window], mains.at[slot]),
            (r.result_rest.at[kind, dest], rests_in.at[slot]),
        )
        here = [
            pltpu.make_async_copy(ref, target, sem.out_in.at[kind, slot, n]) for n, (ref, target) in enumerate(ends)
        ]
        there = [
            remote(
                ref, target, sem.out_send.at[kind, dest, n], sem.out_in.at[kind, slot, n], (w - c + z // 2, dest)
            )
            for n, (ref, target) in enumerate(ends)
        ]
        return own, here, there

    def results_start(kind, source):
        for g in range(2):
            at = pl.ds(g * (size // 2) + 128, 128)
            base = pl.multiple_of(c * part, 128)
            upper = source[pl.ds(base, part // 2), at].astype(F32)
            lower = pltpu.roll(source[pl.ds(base + part // 2, part // 2), at].astype(F32), 64, 1)
            lane = lax.broadcasted_iota(jnp.int32, upper.shape, 1)
            r.result_rest[kind, 2 * g] = jnp.where(lane < 64, upper, lower).astype(BF16)
            r.result_rest[kind, 2 * g + 1] = jnp.where(lane < 64, lower, upper).astype(BF16)
        for dest in range(4):
            own, here, there = result_copies(kind, source, dest)

            @pl.when(own)
            def _():
                for copy in here:
                    copy.start()

            @pl.when(jnp.logical_not(own))
            def _():
                for copy in there:
                    copy.start()

    def results_done(kind, source):
        mains, rests_in = ((r.out_o, r.out_r), (r.in_o, r.in_r))[kind]
        for slot in range(4):
            landed(mains.at[slot], sem.out_in.at[kind, slot, 0])
            landed(rests_in.at[slot], sem.out_in.at[kind, slot, 1])
        for dest in range(4):
            own, _, there = result_copies(kind, source, dest)

            @pl.when(jnp.logical_not(own))
            def _():
                for copy in there:
                    copy.wait_send()

    def results_turn(kind, stage_at, target, stage_out):
        mains, rests_in = ((r.out_o, r.out_r), (r.in_o, r.in_r))[kind]
        loads = []
        for slot in range(4):
            main_at = stage_at.at[pl.ds((slot // 2) * part, part), pl.ds((slot % 2) * 128, 128)]
            rest_at = stage_at.at[pl.ds(slot * (part // 2), part // 2), pl.ds(256, 128)]
            loads.append(pltpu.make_async_copy(mains.at[slot], main_at, sem.load.at[14 + slot]))
            loads.append(pltpu.make_async_copy(rests_in.at[slot], rest_at, sem.load.at[20 + slot]))
        for load in loads:
            load.start()
        for load in loads:
            load.wait()
        same, upper, lower = unit(part), unit(part // 2), unit(part // 2, part // 2)
        pieces = []
        for slot in range(4):
            main = tn(stage_at[(slot // 2) * part : (slot // 2 + 1) * part, (slot % 2) * 128 : (slot % 2 + 1) * 128], same)
            packed = stage_at[slot * (part // 2) : (slot + 1) * (part // 2), 256:384]
            first, second = tn(packed, upper), tn(packed, lower)
            rest = jnp.where(odd, first[64:] + second[:64], first[:64] + second[64:])
            pieces.append(
                jnp.where(odd, jnp.concatenate([rest, main], axis=0), jnp.concatenate([main, rest], axis=0))
            )
        turned = pltpu.roll(jnp.concatenate(pieces, axis=1), shift, 1).astype(stage_out.dtype)
        stores = []
        for n in range(2):
            stage_out[n * width : (n + 1) * width, :] = turned[:, n * half : (n + 1) * half]
            stores.append(
                pltpu.make_async_copy(
                    stage_out.at[pl.ds(n * width, width)], target.at[:, pl.ds(n * half, half)], sem.load.at[18 + n]
                )
            )
            stores[-1].start()
        for store in stores:
            store.wait()

    w_ada_again = r.slope.at[0]
    ada_loads = [
        pltpu.make_async_copy(
            r.w_ada.at[:, pl.ds(i * size, size)], w_ada_again.at[pl.ds(i * cond, cond)], sem.load.at[7 + i]
        )
        for i in range(6)
    ]

    def finish_small():
        per_slab = half // (4 * MSG_ROWS)
        count = 2 * planes
        slabs = -(-count // per_slab)
        loads = []
        for i in range(count):
            place = r.probs.at[i // per_slab, pl.ds((i % per_slab) * 4 * MSG_ROWS, 4 * MSG_ROWS)]
            source = r.messages.at[i // planes, i % planes]
            loads += [
                pltpu.make_async_copy(source.at[j], place.at[pl.ds(j * MSG_ROWS, MSG_ROWS)], sem.msg_load.at[i, j])
                for j in range(4)
            ]
        for load in loads:
            load.start()
        for load in loads + ada_loads:
            load.wait()
        totals = [None, None]
        ada = [None] * 6
        for n in range(slabs):
            used = min(count - n * per_slab, per_slab) * 4 * MSG_ROWS
            every = r.probs[n, :used, :]
            column = lax.broadcasted_iota(jnp.int32, (MSG_ROWS, used), 1)
            row = lax.broadcasted_iota(jnp.int32, (MSG_ROWS, used), 0)
            early = column + n * half < planes * 4 * MSG_ROWS
            for part_of in range(2):
                wanted = (column % MSG_ROWS == row) & (early if part_of == 0 else jnp.logical_not(early))
                term = nn(jnp.where(wanted, 1.0, 0.0).astype(BF16), every)
                totals[part_of] = term if totals[part_of] is None else totals[part_of] + term
            contexts = every[:, :cond].astype(F32)
            at = lax.broadcasted_iota(jnp.int32, contexts.shape, 0) % MSG_ROWS
            contexts = jnp.where(at == MSG_CONTEXT, contexts, 0.0)
            for i in range(6):
                moved = pltpu.roll(contexts, used - MSG_CONTEXT + i, 0).astype(BF16)
                term = tn(moved, every)
                ada[i] = term if ada[i] is None else ada[i] + term
        for i in range(6):
            r.grad_one[i * cond : (i + 1) * cond, :] = ada[i]
        r.small[...] = totals[0] + totals[1]
        up_rows = jnp.where(z // 2 == 0, totals[0][MSG_B_UP : MSG_B_UP + 2], totals[1][MSG_B_UP : MSG_B_UP + 2])
        r.small[MSG_B_UP : MSG_B_UP + 1, :] = jnp.where(odd, up_rows[1:2], up_rows[0:1])
        own_slot = jnp.where(
            (spans_own[0] >= spans_own[1]) & (spans_own[0] >= spans_own[2]),
            0,
            jnp.where(spans_own[1] >= spans_own[2], 1, 2),
        )
        place = lax.broadcasted_iota(jnp.int32, (8, 1), 0)
        grads = jnp.zeros((8, cond), F32)
        for half_at, seg, after in ((0, 0, 0), (1, 0, 1), (1, 1, 2)):
            group_at = seg * planes + plane_at
            base = (group_at % per_slab) * 4 * MSG_ROWS + (2 * c + half_at) * MSG_ROWS
            rows_at = r.probs[group_at // per_slab, pl.ds(pl.multiple_of(base, MSG_ROWS), MSG_ROWS), :]
            row = lax.broadcasted_iota(jnp.int32, (MSG_ROWS, 1), 0)
            total = jnp.zeros((MSG_ROWS, cond), F32)
            for i in range(6):
                total = total + jnp.where(row == i, nt(rows_at, w_ada_again[i * cond : (i + 1) * cond, :]), 0.0)
            slot = own_slot + after
            slot = jnp.where(slot >= slots, slot - slots, slot)
            grads = grads + jnp.where(place == slot, jnp.sum(total, axis=0, keepdims=True), 0.0)
        times = r.info[0]
        gate = 1.0 / (1.0 + jnp.exp(-times))
        r.context[...] = grads * (gate + times * gate * (1.0 - gate))
        copies = []
        for i in range(6):
            ends = (r.grad_one.at[pl.ds(i * cond, cond)], r.ada_out.at[:, pl.ds(i * size, size)])
            copies.append(pltpu.make_async_copy(*ends, sem.end_small.at[i]))
            ends = (r.small.at[i], r.b_ada_out.at[pl.ds(i * size, size)])
            copies.append(pltpu.make_async_copy(*ends, sem.end_small.at[6 + i]))
        rows_out = (
            (MSG_B_DOWN, r.b_down_out), (MSG_GAIN_ONE, r.gain_one_out), (MSG_GAIN_TWO, r.gain_two_out),
            (MSG_B_UP, r.b_up_out),
        )
        for i, (row, ref) in enumerate(rows_out):
            copies.append(pltpu.make_async_copy(r.small.at[row], ref, sem.end_small.at[12 + i]))
        copies.append(pltpu.make_async_copy(r.context.at[pl.ds(0, slots)], r.time_out, sem.end_small.at[16]))
        for copy in copies:
            copy.start()
        return copies

    time_load.wait()
    lane = lax.broadcasted_iota(jnp.int32, (1, 128), 1)
    length_row = jnp.zeros((1, 128), F32)
    for i in range(slots):
        length_row = jnp.where(lane == i, r.lengths[0, i].astype(F32), length_row)
    r.info[0, slots : slots + 1, :] = length_row
    for load in loads[4:8]:
        load.wait()
    r.b_own[...] = r.small[0:8, :]

    pl.semaphore_wait(barrier, len(peers))
    weights_start(0)
    info_copy = remote(r.info.at[0], r.info.at[1], sem.pair.at[2], sem.pair_in.at[2], pair)
    info_copy.start()
    b_copies = [
        remote(r.b_own, r.b_all.at[z], sem.b_send.at[dz], sem.b_in.at[dz], (w, (z + dz) % 4)) for dz in range(1, 4)
    ]
    for copy in b_copies:
        copy.start()

    info_copy.wait()
    info = jnp.where(home, r.info[0], r.info[1])
    context = info / (1.0 + jnp.exp(-info))
    context_low = context.astype(BF16)
    spans = [info[slots : slots + 1, i : i + 1] for i in range(slots)]
    longest = [
        (spans[0] >= spans[1]) & (spans[0] >= spans[2]),
        (spans[1] > spans[0]) & (spans[1] >= spans[2]),
        (spans[2] > spans[0]) & (spans[2] > spans[1]),
    ]

    def slot_after(shift):
        return [longest[(i - shift) % slots] for i in range(slots)]

    def pick(flags, values):
        total = None
        for flag, value in zip(flags, values):
            term = jnp.where(flag, value, 0.0)
            total = term if total is None else total + term
        return total

    flags_a = [jnp.where(odd, after.astype(F32), at.astype(F32)) > 0.5 for after, at in zip(slot_after(1), longest)]
    flags_b = [jnp.where(odd, after.astype(F32), at.astype(F32)) > 0.5 for after, at in zip(slot_after(2), longest)]
    bound = jnp.where(odd, pick(slot_after(1), spans), float(half))
    r.context[0:1, :] = pick(flags_a, [context[i : i + 1, :] for i in range(slots)])
    r.context[1:2, :] = pick(flags_b, [context[i : i + 1, :] for i in range(slots)])
    for load in loads[8:]:
        load.wait()
    rises = {}
    for i in range(6):
        modulation = nn(context_low, w_ada[i * cond : (i + 1) * cond, :]) + r.small[ROW_B_ADA + i : ROW_B_ADA + i + 1, :]
        for seg, flags in enumerate((flags_a, flags_b)):
            row = pick(flags, [modulation[n : n + 1, :] for n in range(slots)])
            if i in (1, 4):
                gain = r.small[ROW_GAIN_ONE : ROW_GAIN_ONE + 1, :] if i == 1 else r.small[ROW_GAIN_TWO : ROW_GAIN_TWO + 1, :]
                rise = 8 * seg + (RISE_ONE if i == 1 else RISE_TWO)
                r.mods[rise : rise + 1, :] = 1.0 + row
                row = gain * (1.0 + row)
            at = 8 * seg + (SHIFT_ONE, GAIN_ONE, GATE_ONE, SHIFT_TWO, GAIN_TWO, GATE_TWO)[i]
            r.mods[at : at + 1, :] = row
    inverse = jnp.exp((lane % (HD // 2)).astype(F32) * (-9.210340371976184 / (HD // 2)))
    signs = jnp.where(lane % HD < HD // 2, -1.0, 1.0)

    def tables(s, start):
        row = (lax.broadcasted_iota(jnp.int32, (TILE, 1), 0) + start).astype(F32)
        angles = jnp.where(row < bound, row, row - bound) * inverse
        r.cosine[s, :] = jnp.cos(angles)
        r.sine[s, :] = jnp.sin(angles) * signs

    tiles(half, tables)
    r.scales[...] = jnp.zeros_like(r.scales)
    r.sums[...] = jnp.zeros_like(r.sums)
    r.bias_up[...] = jnp.zeros_like(r.bias_up)
    loads[0].wait()
    loads[1].wait()
    turn_rows(0)
    rows_start(0)
    weights_own(0, False)
    loads[2].wait()
    loads[3].wait()
    turn_rows(1)
    weights_own(0, True)
    for n, copy in enumerate(b_copies):
        landed(r.b_all.at[(z + 3 - n) % 4], sem.b_in.at[n + 1])
    r.b_all[z] = r.b_own[...]
    weights_pass(0)
    rows_join(0)
    weights_start(1)
    weights_done(0)

    def project_some(i, carry):
        @pl.when(i == 2)
        def _():
            rows_whole(0)

        project(
            bound, ((2 * c + i) % 4) * (part // 2), part // 2, r.x_low, r.mods, r.cosine, r.sine, r.w_attn, r.in_one,
            r.q, r.k, r.v,
        )
        return carry

    lax.fori_loop(0, 4, project_some, 0)
    weights_start(2)
    weights_own(1, False)
    rows_sent(0)
    attend(bound, 0, r.q, r.k, r.v, r.probs, r.scales, r.mixed)
    weights_own(1, True)
    rows_start(1)
    attend(bound, 1, r.q, r.k, r.v, r.probs, r.scales, r.mixed)
    weights_pass(1)
    weights_own(2, False)
    attend(bound, 2, r.q, r.k, r.v, r.probs, r.scales, r.mixed)
    weights_own(2, True)
    mix_out(r.mixed, r.w_attn, r.attn_part, sharing(0, r.attn_part))
    weights_done(1)
    b_up = jnp.where(c == 0, r.b_all[0, 0:1, :], r.b_all[2, 0:1, :]), jnp.where(c == 0, r.b_all[1, 0:1, :], r.b_all[3, 0:1, :])
    feed_up(
        bound, r.x_low, r.mods, r.attn_part, r.w_ff.at[0], b_up, r.in_two, r.act, r.slope, arriving(0, r.attn_part)
    )
    weights_pass(2)
    rows_join(1)
    rows_whole(1)
    rows_sent(1)
    feed_grads(bound, r.dy_low, r.mods, r.feed_low, r.sums)
    for q in range(2):
        weight_grad(r.act.at[q], r.feed_low, r.g_ff.at[1, q])
        grads_start(2, q)
    weights_done(2)
    feed_down(r.act, r.w_ff.at[1], r.feed_part, sharing(1, r.feed_part))
    grads_second(2, 0)
    feed_back(r.feed_low, r.slope, r.w_ff.at[1], r.bias_up)
    grads_second(2, 1)
    for q in range(2):
        weight_grad(r.in_two, r.slope.at[q], r.g_ff.at[0, q])
        grads_start(1, q)
    feed_in_back(r.slope, r.w_ff.at[0], r.back_part, sharing(2, r.back_part))
    b_down = r.small[ROW_B_DOWN : ROW_B_DOWN + 1, :]
    feed_out(
        bound, r.x_low, r.dy_low, r.mods, r.attn_part, r.feed_part, b_down, r.out_low, r.sums, arriving(1, r.feed_part)
    )
    results_start(0, r.out_low)
    norm_two_back(
        bound, r.x_low, r.dy_low, r.mods, r.back_part, r.attn_part, r.w_attn, r.grad_one, r.feed_low, r.grad_mixed,
        r.sums, arriving(2, r.back_part),
    )
    weight_grad(r.mixed, r.feed_low, r.g_attn.at[3])
    grads_third(2)
    grads_second(1, 0)
    for g in range(3):
        attend_back(
            g, r.q, r.k, r.v, r.probs, r.scales, r.mixed, r.grad_mixed, r.cosine, r.sine, r.total_k, r.total_v,
            r.grad_q, r.grad_k, r.grad_v,
        )
        for t, grads in enumerate((r.grad_q, r.grad_k, r.grad_v)):
            r.g_attn[t, g * 128 : (g + 1) * 128, :] = tn(grads[:, lanes(g)], r.in_one[...]).astype(BF16)
        if g == 0:
            grads_second(1, 1)
        if g == 1:
            grads_start(0, 0)
    grads_start(0, 1)
    grads_third(1)
    project_back(r.grad_q, r.grad_k, r.grad_v, r.w_attn, r.act, sharing(3, r.act))
    grads_second(0, 0)
    grads_second(0, 1)
    grads_middle(2)
    norm_one_back(
        bound, r.x_low, r.mods, r.act, r.grad_one, r.in_two, r.sums, arriving(3, r.act)
    )

    def sum_row(piece):
        return jnp.where(c == 0, r.sums[piece : piece + 1, :], r.sums[8 + piece : 9 + piece, :])

    def mod_row(piece):
        return jnp.where(c == 0, r.mods[piece : piece + 1, :], r.mods[8 + piece : 9 + piece, :])

    gain_one = r.small[ROW_GAIN_ONE : ROW_GAIN_ONE + 1, :]
    gain_two = r.small[ROW_GAIN_TWO : ROW_GAIN_TWO + 1, :]
    context_row = jnp.where(c == 0, r.context[0:1, :], r.context[1:2, :])
    message = [
        sum_row(SUM_G1),
        sum_row(SUM_G1N) * gain_one,
        sum_row(SUM_GATE_ONE),
        sum_row(SUM_G2),
        sum_row(SUM_G2N) * gain_two,
        sum_row(SUM_GATE_TWO),
        sum_row(SUM_DY) * mod_row(GATE_TWO),
        sum_row(SUM_G1N) * mod_row(RISE_ONE),
        sum_row(SUM_G2N) * mod_row(RISE_TWO),
        r.bias_up[0:1, :],
        r.bias_up[1:2, :],
        jnp.concatenate([context_row] + [jnp.zeros((1, 128), F32)] * (size // 128 - 1), axis=1),
        jnp.zeros((4, size), F32),
    ]
    r.message[...] = jnp.concatenate(message, axis=0).astype(BF16)
    message_at = r.messages.at[c, plane_at, z]
    message_local = pltpu.make_async_copy(r.message, message_at, sem.m_in.at[0])
    message_local.start()
    message_copies = [
        remote(r.message, message_at, sem.m_send.at[dz], sem.m_in.at[dz], (w, (z + dz) % 4)) for dz in range(1, 4)
    ]
    for copy in message_copies:
        copy.start()
    for load in ada_loads:
        load.start()
    results_done(0, r.out_low)
    results_turn(0, r.act.at[0], r.out_t, r.feed_low)
    grads_middle(1)
    grads_third(0)
    grads_fourth(2)
    grads_fourth(1)
    results_start(1, r.in_two)
    message_local.wait()
    for dz in range(1, 4):
        landed(r.messages.at[c, plane_at, (z + 4 - dz) % 4], sem.m_in.at[dz])
    plane_copies = []
    for step in range(1, planes):
        ref = r.messages.at[c, plane_at]
        plane_copies.append(
            remote(ref, ref, sem.mp_send.at[step], sem.mp_in.at[step], ((w + 2 * step) % n_wide, z))
        )
        plane_copies[-1].start()
    grads_fifth(2)
    grads_fifth(1)
    for step in range(1, planes):
        landed(r.messages.at[c, (plane_at + planes - step) % planes], sem.mp_in.at[step])
    message_pair = remote(r.messages.at[c], r.messages.at[c], sem.m_send.at[4], sem.m_in.at[4], pair)
    message_pair.start()
    grads_fourth(0)
    grads_sixth(2)
    grads_sixth(1)
    landed(r.messages.at[1 - c], sem.m_in.at[4])
    small_ends = finish_small()
    grads_fifth(0)
    for copy in small_ends:
        copy.wait()
    results_done(1, r.in_two)
    results_turn(1, r.act.at[1], r.in_t, r.grad_one)
    grads_sixth(0)

    for t in range(CHUNKS):
        weights_sent(t)
    for kind in range(2):
        pair_rows(kind).wait_send()
    for copy in b_copies + message_copies + plane_copies + [message_pair]:
        copy.wait_send()
    for t in range(CHUNKS):
        grads_done(t)


def layer(n_wide, lengths, x, *others):
    width, rows = x.shape
    w_up, times = others[3], others[-1]
    size = w_up.shape[0]
    slots, cond = times.shape
    buffers, semaphores = scratch_plan(n_wide, rows, width, size, cond)
    anywhere = pl.BlockSpec(memory_space=pl.ANY)
    part, planes, groups = rows // 4, n_wide // 2, n_wide // 8
    outs = (
        ((width, rows), BF16),
        ((width, rows), F32),
        ((4, part, 128), BF16),
        ((4, part, 128), BF16),
        ((4, part // 2, 128), BF16),
        ((4, part // 2, 128), BF16),
        ((4, size // 4, size), BF16),
        ((size, size), BF16),
        ((size, size), BF16),
        ((2, planes, 4, MSG_ROWS, size), BF16),
        ((CHUNKS, groups, size // 4, size), BF16),
        ((cond, 6 * size), F32),
        ((6 * size,), F32),
        ((size,), F32),
        ((size,), F32),
        ((size,), F32),
        ((size,), F32),
        ((slots, cond), F32),
    )
    return pl.pallas_call(
        functools.partial(layer_kernel, n_wide, rows, width, size, cond, slots),
        out_shape=tuple(jax.ShapeDtypeStruct(shape, kind) for shape, kind in outs),
        in_specs=[pl.BlockSpec(memory_space=pltpu.SMEM)] + [anywhere] * (1 + len(others)),
        out_specs=(anywhere,) * len(outs),
        scratch_shapes=[pltpu.VMEM(shape, kind) for shape, kind in buffers.values()]
        + [pltpu.SemaphoreType.DMA(shape) for shape in semaphores.values()],
        compiler_params=pltpu.CompilerParams(
            collective_id=0, has_side_effects=True, vmem_limit_bytes=63 * 1024 * 1024
        ),
        name="layer",
    )(lengths, x, *others)


def body(
    n_wide,
    block_input,
    time_embed,
    seq_lengths,
    w_qkv,
    w_out,
    w_up,
    b_up,
    w_down,
    b_down,
    gain_one,
    gain_two,
    w_ada,
    b_ada,
    out_grad,
):
    results = layer(
        n_wide, seq_lengths, block_input.T, out_grad.T, jnp.swapaxes(w_qkv, 1, 2), w_out, w_up, w_down, b_up,
        b_down, gain_one, gain_two, w_ada, b_ada, time_embed,
    )
    out_t, in_t, _, _, _, _, g_heads, g_up, g_down, _, _ = results[:11]
    ada, b_ada_sum, b_down_sum, gain_one_sum, gain_two_sum, b_up_sum, times = results[11:18]
    return (
        out_t.T,
        in_t.T,
        times,
        jnp.swapaxes(g_heads[:3].astype(F32), 1, 2),
        g_heads[3].astype(F32),
        g_up.astype(F32),
        b_up_sum,
        g_down.astype(F32),
        b_down_sum,
        gain_one_sum,
        gain_two_sum,
        ada,
        b_ada_sum,
    )


def solution(mesh):
    return jax.shard_map(
        functools.partial(body, mesh.shape["wide"]),
        mesh=mesh,
        in_specs=(
            P("wide", "narrow"),
            P("wide", None),
            P("wide", None),
            P(None, None, "narrow"),
            P("narrow", None),
            P(None, "narrow"),
            P("narrow"),
            P("narrow", None),
            P(),
            P(),
            P(),
            P(),
            P(),
            P("wide", "narrow"),
        ),
        out_specs=(
            P("wide", "narrow"),
            P("wide", "narrow"),
            P("wide", None),
            P(None, None, "narrow"),
            P("narrow", None),
            P(None, "narrow"),
            P("narrow"),
            P("narrow", None),
            P(),
            P(),
            P(),
            P(),
            P(),
        ),
        check_vma=False,
    )
```

```python
import functools
from types import SimpleNamespace

import jax
import jax.numpy as jnp
from jax import lax
from jax.experimental import pallas as pl
from jax.experimental.pallas import tpu as pltpu
from jax.sharding import PartitionSpec as P

HD = 64
LOG2_E = 1.4426950408889634
epsilon = 1e-05
MESH = pl.DeviceIdType.MESH
CHUNKS = 3
F32 = jnp.float32
BF16 = jnp.bfloat16


def flip(w, bit, step):
    return w + step * (1 - 2 * bit)


def remote(src, dst, send, recv, device):
    return pltpu.make_async_remote_copy(
        src_ref=src, dst_ref=dst, send_sem=send, recv_sem=recv, device_id=device, device_id_type=MESH
    )


def landed(ref, sem):
    pltpu.make_async_copy(ref, ref, sem).wait()


def dot(a, b, dims):
    return lax.dot_general(a, b, (dims, ((), ())), preferred_element_type=F32)


def nn(a, b):
    return dot(a, b, ((1,), (0,)))


def nt(a, b):
    return dot(a, b, ((1,), (1,)))


def tn(a, b):
    return dot(a, b, ((0,), (0,)))


TILE = 256
ATTEND = 384
ATTEND_BACK = 384


def tiles(count, step, size=TILE):
    def run(i, carry):
        step(pl.ds(pl.multiple_of(i * size, size), size), i * size)
        return carry

    lax.fori_loop(0, count // size, run, 0)


def norm_stats(inputs):
    row_mean = jnp.mean(inputs, axis=-1, keepdims=True)
    centered = inputs - row_mean
    variance = jnp.mean(centered * centered, axis=-1, keepdims=True)
    scaled = lax.rsqrt(variance + epsilon)
    return (centered * scaled, scaled)


def norm_back(grad_normed, normed, scaled):
    first_term = jnp.mean(grad_normed, axis=-1, keepdims=True)
    second_term = jnp.mean(grad_normed * normed, axis=-1, keepdims=True)
    return scaled * (grad_normed - first_term - normed * second_term)


GAIN_ONE, SHIFT_ONE, GATE_ONE, GAIN_TWO, SHIFT_TWO, GATE_TWO, RISE_ONE, RISE_TWO = range(8)
SUM_G1, SUM_G1N, SUM_GATE_ONE, SUM_G2, SUM_G2N, SUM_GATE_TWO, SUM_DY = range(7)


def chosen(mods, first, piece):
    return jnp.where(first, mods[piece : piece + 1, :], mods[8 + piece : 9 + piece, :])


def first_rows(bound, start, count):
    return (lax.broadcasted_iota(jnp.int32, (count, 1), 0) + start).astype(F32) < bound


def add_sums(sums, piece, first, values):
    total = jnp.sum(values, axis=0, keepdims=True)
    head = jnp.sum(jnp.where(first, values, 0.0), axis=0, keepdims=True)
    sums[piece : piece + 1, :] += head
    sums[8 + piece : 9 + piece, :] += total - head


def swapped(pair):
    lane = lax.broadcasted_iota(jnp.int32, pair.shape, 1)
    return jnp.where(lane % HD < HD // 2, pltpu.roll(pair, 128 - HD // 2, 1), pltpu.roll(pair, HD // 2, 1))


def lanes(g):
    return pl.ds(g * 128, 128)


def head_only(pair, hh):
    lane = lax.broadcasted_iota(jnp.int32, pair.shape, 1)
    return jnp.where((lane < HD) == (hh == 0), pair, jnp.zeros_like(pair))


def project(bound, start, rows, x, mods, cosine, sine, w_attn, in_one, q, k, v):
    s = pl.ds(pl.multiple_of(start, 64), rows)
    first = first_rows(bound, start, rows)
    normed, _ = norm_stats(x[s, :].astype(F32))
    low = (normed * chosen(mods, first, GAIN_ONE) + chosen(mods, first, SHIFT_ONE)).astype(BF16)
    in_one[s, :] = low
    cos_rows, sin_rows = cosine[s, :], sine[s, :]
    for t, target in enumerate((q, k)):
        raw = nt(low, w_attn[t])
        for g in range(raw.shape[1] // 128):
            pair = raw[:, g * 128 : (g + 1) * 128]
            turned = pair * cos_rows + swapped(pair) * sin_rows
            target[s, lanes(g)] = (turned * (0.125 * LOG2_E if t == 0 else 1.0)).astype(BF16)
    v[s, :] = nt(low, w_attn[2]).astype(BF16)


def attend(bound, g, q, k, v, probs, scales, mixed):
    rows = q.shape[0]

    def step(s, start):
        first = first_rows(bound, start, ATTEND)
        column = lax.broadcasted_iota(jnp.int32, (1, rows), 1).astype(F32) < bound
        bias = jnp.where(first == column, 0.0, -1e30)
        halves = []
        for hh in range(2):
            scores = nt(head_only(q[s, lanes(g)], hh), k[:, lanes(g)]) + bias
            expos = jnp.exp2(scores - jnp.max(scores, axis=-1, keepdims=True))
            low = expos.astype(BF16)
            probs[2 * g + hh, s, :] = low
            scale = 1.0 / jnp.sum(expos, axis=-1, keepdims=True)
            kept = scales[s, :]
            scales[s, :] = jnp.where(lax.broadcasted_iota(jnp.int32, kept.shape, 1) == 2 * g + hh, scale, kept)
            halves.append(nn(low, v[:, lanes(g)]) * scale)
        lane = lax.broadcasted_iota(jnp.int32, halves[0].shape, 1)
        mixed[s, lanes(g)] = jnp.where(lane < HD, halves[0], halves[1]).astype(BF16)

    tiles(rows, step, ATTEND)


def mix_out(mixed, w_attn, part, share):
    def step(s, start):
        part[0, s, :] = nn(mixed[s, :], w_attn[3]).astype(BF16)
        share(s, start)

    tiles(mixed.shape[0], step)


def both(part, s):
    return part[0, s, :].astype(F32) + part[1, s, :].astype(F32)


def hidden_rows(first, s, x, mods, attn_part):
    return x[s, :].astype(F32) + chosen(mods, first, GATE_ONE) * both(attn_part, s)


def feed_up(bound, x, mods, attn_part, w_up, b_up, in_two, act, slope, arrived):
    def step(s, start):
        arrived(s, start)
        first = first_rows(bound, start, TILE)
        normed, _ = norm_stats(hidden_rows(first, s, x, mods, attn_part))
        low = (normed * chosen(mods, first, GAIN_TWO) + chosen(mods, first, SHIFT_TWO)).astype(BF16)
        in_two[s, :] = low
        for n in range(2):
            pre = nn(low, w_up[n]) + b_up[n]
            square = pre * pre
            bent = jnp.tanh(0.7978845608028654 * pre * (1.0 + 0.044715 * square))
            rise = 0.5 * (1.0 + bent)
            act[n, s, :] = (pre * rise).astype(BF16)
            inner = 0.7978845608028654 + 0.10703222443 * square
            slope[n, s, :] = (rise + 0.5 * pre * (1.0 - bent * bent) * inner).astype(BF16)

    tiles(x.shape[0], step)


def feed_grads(bound, dy, mods, feed_low, sums):
    def step(s, start):
        first = first_rows(bound, start, TILE)
        grads = dy[s, :].astype(F32)
        add_sums(sums, SUM_DY, first, grads)
        feed_low[s, :] = (grads * chosen(mods, first, GATE_TWO)).astype(BF16)

    tiles(dy.shape[0], step)


def feed_down(act, w_down, part, share):
    def step(s, start):
        part[0, s, :] = (nn(act[0, s, :], w_down[0]) + nn(act[1, s, :], w_down[1])).astype(BF16)
        share(s, start)

    tiles(act.shape[1], step)


def feed_out(bound, x, dy, mods, attn_part, feed_part, b_down, out, sums, arrived):
    def step(s, start):
        arrived(s, start)
        first = first_rows(bound, start, TILE)
        rows = both(feed_part, s) + b_down
        out[s, :] = (hidden_rows(first, s, x, mods, attn_part) + chosen(mods, first, GATE_TWO) * rows).astype(BF16)
        add_sums(sums, SUM_GATE_TWO, first, dy[s, :].astype(F32) * rows)

    tiles(dy.shape[0], step)


def feed_back(feed_low, slope, w_down, bias_up):
    def step(s, start):
        low = feed_low[s, :]
        for n in range(2):
            grad_pre = nt(low, w_down[n]) * slope[n, s, :].astype(F32)
            bias_up[n : n + 1, :] += jnp.sum(grad_pre, axis=0, keepdims=True)
            slope[n, s, :] = grad_pre.astype(BF16)

    tiles(feed_low.shape[0], step)


def feed_in_back(pre_low, w_up, part, share):
    def step(s, start):
        part[0, s, :] = (nt(pre_low[0, s, :], w_up[0]) + nt(pre_low[1, s, :], w_up[1])).astype(BF16)
        share(s, start)

    tiles(pre_low.shape[1], step)


def weight_grad(left, right, target):
    def step(s, start):
        target[s, :] = tn(left[:, s], right[...]).astype(BF16)

    size = 384 if left.shape[1] % 384 == 0 else 128
    tiles(left.shape[1], step, size)


def norm_two_back(bound, x, dy, mods, back_part, attn_part, w_attn, grad_one, attn_low, grad_mixed, sums, arrived):
    def step(s, start):
        arrived(s, start)
        first = first_rows(bound, start, TILE)
        grads = both(back_part, s)
        normed, scaled = norm_stats(hidden_rows(first, s, x, mods, attn_part))
        add_sums(sums, SUM_G2, first, grads)
        add_sums(sums, SUM_G2N, first, grads * normed)
        rows = dy[s, :].astype(F32) + norm_back(grads * chosen(mods, first, GAIN_TWO), normed, scaled)
        grad_one[s, :] = rows
        add_sums(sums, SUM_GATE_ONE, first, rows * both(attn_part, s))
        low = (rows * chosen(mods, first, GATE_ONE)).astype(BF16)
        attn_low[s, :] = low
        grad_mixed[s, :] = nt(low, w_attn[3]).astype(BF16)

    tiles(dy.shape[0], step)


def attend_back(g, q, k, v, probs, scales, mixed, grad_mixed, cosine, sine, total_k, total_v, grad_q, grad_k, grad_v):
    rows = q.shape[0]

    def turned_back(pair, s):
        return pair * cosine[s, :] - swapped(pair) * sine[s, :]

    total_k[...] = jnp.zeros_like(total_k)
    total_v[...] = jnp.zeros_like(total_v)

    def step(s, start):
        upstream = grad_mixed[s, lanes(g)]
        product = upstream.astype(F32) * mixed[s, lanes(g)].astype(F32)
        halves = []
        for hh in range(2):
            kept = scales[s, :]
            here = lax.broadcasted_iota(jnp.int32, kept.shape, 1) == 2 * g + hh
            scale = jnp.sum(jnp.where(here, kept, 0.0), axis=-1, keepdims=True)
            row_dot = jnp.sum(head_only(product, hh), axis=-1, keepdims=True) * scale
            up_head = (head_only(upstream, hh).astype(F32) * scale).astype(BF16)
            low = probs[2 * g + hh, s, :]
            grad_weights = nt(up_head, v[:, lanes(g)])
            grad_scores = (low.astype(F32) * (grad_weights - row_dot)).astype(BF16)
            halves.append(nn(grad_scores, k[:, lanes(g)]))
            total_v[...] += tn(low, up_head)
            total_k[...] += tn(grad_scores, head_only(q[s, lanes(g)], hh))
        lane = lax.broadcasted_iota(jnp.int32, halves[0].shape, 1)
        pair = jnp.where(lane < HD, halves[0], halves[1]) * 0.125
        grad_q[s, lanes(g)] = turned_back(pair, s).astype(BF16)

    tiles(rows, step, ATTEND_BACK)

    def finish(s, start):
        grad_k[s, lanes(g)] = turned_back(total_k[s, :] * (1.0 / LOG2_E), s).astype(BF16)
        grad_v[s, lanes(g)] = total_v[s, :].astype(BF16)

    tiles(rows, finish)


def project_back(grad_q, grad_k, grad_v, w_attn, part, share):
    def step(s, start):
        total = nn(grad_q[s, :], w_attn[0]) + nn(grad_k[s, :], w_attn[1]) + nn(grad_v[s, :], w_attn[2])
        part[0, s, :] = total.astype(BF16)
        share(s, start)

    tiles(grad_q.shape[0], step)


def norm_one_back(bound, x, mods, back_part, grad_one, in_grad, sums, arrived):
    def step(s, start):
        arrived(s, start)
        first = first_rows(bound, start, TILE)
        grads = both(back_part, s)
        normed, scaled = norm_stats(x[s, :].astype(F32))
        add_sums(sums, SUM_G1, first, grads)
        add_sums(sums, SUM_G1N, first, grads * normed)
        rows = grad_one[s, :] + norm_back(grads * chosen(mods, first, GAIN_ONE), normed, scaled)
        in_grad[s, :] = rows.astype(BF16)

    tiles(x.shape[0], step)


ROW_B_UP, ROW_B_DOWN, ROW_GAIN_ONE, ROW_GAIN_TWO, ROW_B_ADA = 0, 1, 2, 3, 8
MSG_MOD, MSG_B_DOWN, MSG_GAIN_ONE, MSG_GAIN_TWO, MSG_B_UP, MSG_CONTEXT = 0, 6, 7, 8, 9, 11
MSG_ROWS = 16
Z_SLOT = (0, 3, 5)


def scratch_plan(n_wide, rows, width, size, cond):
    half, heads = rows // 2, 2 * width // HD
    block = size // 4
    buffers = {
        "tail": ((half // 2, 128), F32),
        "small": ((16, size), F32),
        "b_all": ((4, 8, size), F32),
        "b_own": ((8, size), F32),
        "info": ((2, 8, 128), F32),
        "context": ((8, 128), F32),
        "mods": ((16, size), F32),
        "sums": ((16, size), F32),
        "bias_up": ((8, size), F32),
        "message": ((MSG_ROWS, size), BF16),
        "rest": ((2, 4, half // 4, 128), BF16),
        "result_rest": ((2, 4, half // 4, 128), BF16),
        "x_low": ((half, size), BF16),
        "dy_low": ((half, size), BF16),
        "cosine": ((half, 128), F32),
        "sine": ((half, 128), F32),
        "w_attn": ((4, 2 * block, size), BF16),
        "w_ff": ((2, 2, size, size), BF16),
        "in_one": ((half, size), BF16),
        "q": ((half, 2 * width), BF16),
        "k": ((half, 2 * width), BF16),
        "v": ((half, 2 * width), BF16),
        "probs": ((heads, half, half), BF16),
        "scales": ((half, 128), F32),
        "mixed": ((half, 2 * width), BF16),
        "attn_part": ((2, half, size), BF16),
        "feed_part": ((2, half, size), BF16),
        "back_part": ((2, half, size), BF16),
        "in_two": ((half, size), BF16),
        "act": ((2, half, size), BF16),
        "slope": ((2, half, size), BF16),
        "out_low": ((half, size), BF16),
        "feed_low": ((half, size), BF16),
        "grad_one": ((half, size), F32),
        "grad_mixed": ((half, 2 * width), BF16),
        "total_k": ((half, 128), F32),
        "total_v": ((half, 128), F32),
        "grad_q": ((half, 2 * width), BF16),
        "grad_k": ((half, 2 * width), BF16),
        "grad_v": ((half, 2 * width), BF16),
        "g_attn": ((4, 2 * block, size), BF16),
        "g_ff": ((2, 2, size, size), BF16),
        "near_half": ((CHUNKS, 2, 2, block // 2, size), BF16),
        "near_full": ((CHUNKS, 2, 2, block, size), BF16),
        "from_z": ((7, block, size), BF16),
    }
    planes = n_wide // 2
    groups = n_wide // 8
    semaphores = {
        "load": (28,),
        "msg_load": (n_wide, 4),
        "end_small": (17,),
        "pair": (4,),
        "pair_in": (4,),
        "b_send": (4,),
        "b_in": (4,),
        "x_send": (2, 4, 2),
        "x_in": (2, 4, 2),
        "home": (CHUNKS, 4),
        "home_send": (CHUNKS, 2),
        "edge_send": (CHUNKS, 2),
        "z_in": (CHUNKS, 2),
        "w_send": (CHUNKS, 2, 4),
        "w_in": (CHUNKS, 2, 4),
        "part_send": (4, 4),
        "part_in": (4, 4),
        "out_send": (2, 4, 2),
        "out_in": (2, 4, 2),
        "g_send": (CHUNKS, 2, 5),
        "g_in": (CHUNKS, 2, 4),
        "gz_in": (CHUNKS, 3),
        "group_send": (CHUNKS, groups),
        "group_in": (CHUNKS, groups),
        "group_load": (CHUNKS,),
        "end_send": (CHUNKS, 8),
        "end_in": (CHUNKS, 9),
        "m_send": (5,),
        "m_in": (5,),
        "mp_send": (planes,),
        "mp_in": (planes,),
    }
    return buffers, semaphores


def layer_kernel(n_wide, rows, width, size, cond, slots, *refs):
    buffers, semaphores = scratch_plan(n_wide, rows, width, size, cond)
    names = (
        ["lengths", "x", "dy", "w_qkv", "w_out", "w_up", "w_down", "b_up", "b_down", "gain_one", "gain_two", "w_ada"]
        + ["b_ada", "times", "out_t", "in_t", "out_o", "in_o", "out_r", "in_r", "g_heads", "g_up", "g_down", "messages", "groups"]
        + ["ada_out", "b_ada_out", "b_down_out", "gain_one_out", "gain_two_out", "b_up_out", "time_out"]
        + list(buffers)
    )
    r = SimpleNamespace(**dict(zip(names, refs)))
    sem = SimpleNamespace(**dict(zip(semaphores, refs[len(names) :])))
    half = rows // 2
    part = half // 2
    block = size // 4
    planes, groups = n_wide // 2, n_wide // 8

    w = lax.axis_index("wide")
    z = lax.axis_index("narrow")
    c, bx, by, plane_at = w % 2, (w // 2) % 2, (w // 4) % 2, w // 2
    pair = (flip(w, c, 1), z)
    next_x, next_y = (flip(w, bx, 2), z), (flip(w, by, 4), z)
    mine = bx + 2 * by
    block_x, block_y, block_d = mine + 1 - 2 * bx, mine + 2 - 4 * by, 3 - mine
    far = [(z - 2 * c - q) % 4 for q in range(2)]
    home = c == z // 2
    odd = z % 2 == 1

    peers = [(w if same else pair[0], (z + dz) % 4) for same in (1, 0) for dz in range(4) if not (same and dz == 0)]
    peers += [((w + 2 * step) % n_wide, z) for step in range(1, planes)]
    barrier = pltpu.get_barrier_semaphore()
    for device in peers:
        pl.semaphore_signal(barrier, inc=1, device_id=device, device_id_type=MESH)

    w_ada = r.probs.at[2]
    raw = r.probs.at[3]
    loads = []
    for i in range(4):
        source = (r.x, r.dy)[i // 2].at[:, pl.ds((i % 2) * half, half)]
        loads.append(pltpu.make_async_copy(source, raw.at[pl.ds(i * width, width)], sem.load.at[(0, 1, 26, 27)[i]]))
    for i, ref in enumerate((r.b_up, r.b_down, r.gain_one, r.gain_two)):
        loads.append(pltpu.make_async_copy(ref, r.small.at[i], sem.load.at[2 + i]))
    for i in range(6):
        piece = pl.ds(i * size, size)
        loads.append(pltpu.make_async_copy(r.b_ada.at[piece], r.small.at[ROW_B_ADA + i], sem.load.at[20 + i]))
    for i in range(6):
        loads.append(
            pltpu.make_async_copy(
                r.w_ada.at[:, pl.ds(i * size, size)], w_ada.at[pl.ds(i * cond, cond)], sem.load.at[7 + i]
            )
        )
    for load in loads:
        load.start()
    r.info[0] = jnp.zeros((8, 128), F32)
    time_load = pltpu.make_async_copy(r.times, r.info.at[0, pl.ds(0, slots)], sem.load.at[13])
    time_load.start()

    def w_block(t, q, index, start=0, count=block):
        if t == 0:
            return r.w_attn.at[index, pl.ds(q * block + start, count)]
        return r.w_ff.at[t - 1, q, pl.ds(pl.multiple_of(index * block + start, 32), count)]

    def home_copies(t, q):
        if t == 0:
            copies = [pltpu.make_async_copy(r.w_qkv.at[i], w_block(0, q, i), sem.home.at[0, i]) for i in range(3)]
            return copies + [pltpu.make_async_copy(r.w_out, w_block(0, q, 3), sem.home.at[0, 3])]
        return [pltpu.make_async_copy((r.w_up, r.w_down)[t - 1], r.w_ff.at[t - 1, q], sem.home.at[t, 0])]

    edge, middle = 3 - 3 * c, 2 - c

    def home_sends(t, q, source):
        return [
            remote(
                source, w_block(t, q, mine), sem.home_send.at[t, n], sem.z_in.at[t, q], (w, c + (c + q + n + 1) % 3)
            )
            for n in range(2)
        ]

    def home_each(t, q, action):
        if t == 0:

            @pl.when(mine == 3)
            def _():
                for copy in home_sends(t, q, r.w_out):
                    action(copy)

            @pl.when(mine != 3)
            def _():
                for copy in home_sends(t, q, r.w_qkv.at[jnp.minimum(mine, 2)]):
                    action(copy)

        else:
            for copy in home_sends(t, q, (r.w_up, r.w_down)[t - 1].at[pl.ds(pl.multiple_of(mine * block, 32), block)]):
                action(copy)

    def edge_copy(t, q):
        ref = w_block(t, q, mine)
        return remote(ref, ref, sem.edge_send.at[t, q], sem.z_in.at[t, q], (w, edge))

    def w_copy(t, q, n):
        index, start, count, device = (
            (mine, 0, block, next_x),
            (mine, 0, block, next_y),
            (block_x, 0, block // 2, next_y),
            (block_y, block // 2, block // 2, next_x),
        )[n]
        ref = w_block(t, q, index, start, count)
        return remote(ref, ref, sem.w_send.at[t, q, n], sem.w_in.at[t, q, n], device)

    def weights_start(t):
        for q in range(2):

            @pl.when(far[q] == 0)
            def _():
                home_each(t, q, lambda copy: copy.start())
                for copy in home_copies(t, q):
                    copy.start()

    def weights_own(t, at_edge):
        for q in range(2):

            @pl.when((z == edge) if at_edge else (far[q] != 0) & (z != edge))
            def _():
                landed(w_block(t, q, mine), sem.z_in.at[t, q])

                @pl.when(z == middle)
                def _():
                    edge_copy(t, q).start()

                w_copy(t, q, 0).start()
                w_copy(t, q, 1).start()

    def weights_pass(t):
        for q in range(2):

            @pl.when(far[q] != 0)
            def _():
                landed(w_block(t, q, block_x), sem.w_in.at[t, q, 0])
                w_copy(t, q, 2).start()
                landed(w_block(t, q, block_y), sem.w_in.at[t, q, 1])
                w_copy(t, q, 3).start()

    def weights_done(t):
        for q in range(2):

            @pl.when(far[q] != 0)
            def _():
                landed(w_block(t, q, block_d, 0, block // 2), sem.w_in.at[t, q, 2])
                landed(w_block(t, q, block_d, block // 2, block // 2), sem.w_in.at[t, q, 3])

            @pl.when(far[q] == 0)
            def _():
                for copy in home_copies(t, q):
                    copy.wait()

    def weights_sent(t):
        for q in range(2):

            @pl.when(far[q] == 0)
            def _():
                home_each(t, q, lambda copy: copy.wait_send())

            @pl.when(far[q] != 0)
            def _():
                for n in range(4):
                    w_copy(t, q, n).wait_send()

                @pl.when(z == middle)
                def _():
                    edge_copy(t, q).wait_send()

    stage = (r.probs.at[1], r.g_ff.at[0, 0])
    rests = 2 * 128

    def row_copies(kind, j):
        device = (w - c + j % 2, 2 * c + j // 2)
        own = (c == j % 2) & (2 * c + j // 2 == z)
        target = (r.x_low, r.dy_low)[kind]
        ends = (
            (
                stage[kind].at[pl.ds((j % 2) * part, part), pl.ds((j // 2) * 128, 128)],
                target.at[
                    pl.ds((j % 2) * part, part),
                    pl.ds(pl.multiple_of((z // 2) * (size // 2) + (z % 2) * 256, 128), 128),
                ],
            ),
            (stage[kind].at[pl.ds(j * (part // 2), part // 2), pl.ds(rests, 128)], r.rest.at[kind, z]),
        )
        here = [
            pltpu.make_async_copy(source, dest, sem.x_in.at[kind, z, n]) for n, (source, dest) in enumerate(ends)
        ]
        there = [
            remote(source, dest, sem.x_send.at[kind, j, n], sem.x_in.at[kind, z, n], device)
            for n, (source, dest) in enumerate(ends)
        ]
        return own, here, there

    spans_own = [r.lengths[0, i] for i in range(slots)]
    shift = jnp.where(
        (spans_own[0] >= spans_own[1]) & (spans_own[0] >= spans_own[2]),
        0,
        jnp.where(spans_own[1] >= spans_own[2], spans_own[0], spans_own[0] + spans_own[1]),
    )

    def unit(count, first=0, total=part):
        row = lax.broadcasted_iota(jnp.int32, (count, 1), 0) + first
        column = lax.broadcasted_iota(jnp.int32, (1, total), 1)
        return jnp.where(row == column, 1.0, 0.0).astype(BF16)

    def turn_rows(kind):
        back = jnp.where(shift == 0, 0, rows - shift)
        at = 2 * kind * width
        columns = jnp.concatenate([raw[at : at + width, :], raw[at + width : at + 2 * width, :]], axis=1)
        columns = pltpu.roll(columns.astype(F32), back, 1).astype(BF16)
        raw[at : at + width, :] = columns[:, :half]
        raw[at + width : at + 2 * width, :] = columns[:, half:]
        same = unit(part)
        r.tail[...] = jnp.zeros_like(r.tail)
        for j in range(4):
            row, lane_at = at + (j // 2) * width, (j % 2) * part
            turned = nt(same, raw[row : row + width, lane_at : lane_at + part])
            main = turned[:, :128]
            r.tail[:, : width - 128] = turned[:, 128:]
            tail = r.tail[...]
            lane = lax.broadcasted_iota(jnp.int32, main.shape, 1)
            main_turned = pltpu.roll(main, 64, 1)
            tail_turned = pltpu.roll(tail, 64, 1)
            full = jnp.where(odd, jnp.where(lane < 64, main_turned, tail_turned), main)
            left = jnp.where(odd, jnp.where(lane < 64, 0.0, main_turned), tail)
            stage[kind][(j % 2) * part : (j % 2 + 1) * part, (j // 2) * 128 : (j // 2 + 1) * 128] = full.astype(BF16)
            packed = left[: part // 2] + pltpu.roll(left[part // 2 :], 64, 1)
            stage[kind][j * (part // 2) : (j + 1) * (part // 2), rests : rests + 128] = packed.astype(BF16)

    def rows_start(kind, outer):
        for j in range(4):
            own, here, there = row_copies(kind, j)
            wanted = (c == j // 2) == outer

            @pl.when(wanted & own)
            def _():
                for copy in here:
                    copy.start()

            @pl.when(wanted & jnp.logical_not(own))
            def _():
                for copy in there:
                    copy.start()

    def rows_sent(kind):
        for j in range(4):
            own, _, there = row_copies(kind, j)

            @pl.when(jnp.logical_not(own))
            def _():
                for copy in there:
                    copy.wait_send()

    own_rows = pl.ds(pl.multiple_of(c * part, 128), part)
    other_rows = pl.ds(pl.multiple_of((1 - c) * part, 128), part)

    def pair_rows(kind):
        target = (r.x_low, r.dy_low)[kind]
        return remote(target.at[own_rows], target.at[own_rows], sem.pair.at[kind], sem.pair_in.at[kind], pair)

    def rows_join(kind):
        target = (r.x_low, r.dy_low)[kind]
        for slot in range(4):
            at = (slot // 2) * (size // 2) + (slot % 2) * 256
            landed(target.at[own_rows, pl.ds(at, 128)], sem.x_in.at[kind, slot, 0])
            landed(r.rest.at[kind, slot], sem.x_in.at[kind, slot, 1])
        for g in range(2):
            even, odds = r.rest[kind, 2 * g].astype(F32), r.rest[kind, 2 * g + 1].astype(F32)
            lane = lax.broadcasted_iota(jnp.int32, even.shape, 1)
            upper = jnp.where(lane < 64, even, odds)
            lower = pltpu.roll(jnp.where(lane < 64, odds, even), 64, 1)
            at = pl.ds(g * (size // 2) + 128, 128)
            base = pl.multiple_of(c * part, 128)
            target[pl.ds(base, part // 2), at] = upper.astype(BF16)
            target[pl.ds(base + part // 2, part // 2), at] = lower.astype(BF16)
        pair_rows(kind).start()

    def rows_whole(kind):
        target = (r.x_low, r.dy_low)[kind]
        landed(target.at[other_rows], sem.pair_in.at[kind])

    def part_copy(n, ref, s, start):
        i = start // TILE
        return remote(ref.at[0, s], ref.at[1, s], sem.part_send.at[n, i], sem.part_in.at[n, i], pair)

    def sharing(n, ref):
        return lambda s, start: part_copy(n, ref, s, start).start()

    def arriving(n, ref):
        def wait(s, start):
            copy = part_copy(n, ref, s, start)
            copy.wait_recv()
            copy.wait_send()

        return wait

    def g_block(t, q, index, start=0, count=block):
        if t == 0:
            return r.g_attn.at[index, pl.ds(q * block + start, count)]
        return r.g_ff.at[t - 1, q, pl.ds(pl.multiple_of(index * block + start, 32), count)]

    def add_to(target, terms):
        def step(s, start):
            total = target[s, :].astype(F32)
            for term in terms:
                total = total + term[s, :].astype(F32)
            target[s, :] = total.astype(BF16)

        tiles(target.shape[0], step, 32)

    def g_copy(t, q, n):
        source, dest, device = (
            (g_block(t, q, block_d, 0, block // 2), r.near_half.at[t, q, 0], next_y),
            (g_block(t, q, block_d, block // 2, block // 2), r.near_half.at[t, q, 1], next_x),
            (g_block(t, q, block_x), r.near_full.at[t, q, 0], next_x),
            (g_block(t, q, block_y), r.near_full.at[t, q, 1], next_y),
        )[n]
        return remote(source, dest, sem.g_send.at[t, q, n], sem.g_in.at[t, q, n], device)

    def g_home(t, q, slot):
        return remote(
            g_block(t, q, mine), r.from_z.at[Z_SLOT[t] + slot], sem.g_send.at[t, q, 4], sem.gz_in.at[t, slot], (w, 2 * c + q)
        )

    def g_edge(t, q):
        return remote(g_block(t, q, mine), r.from_z.at[Z_SLOT[t] + q], sem.g_send.at[t, q, 4], sem.gz_in.at[t, q], (w, middle))

    def grads_start(t, q):
        g_copy(t, q, 0).start()
        g_copy(t, q, 1).start()

    def grads_second(t, q):
        g_copy(t, q, 0).wait_recv()
        add_to(g_block(t, q, block_x, 0, block // 2), [r.near_half.at[t, q, 0]])
        g_copy(t, q, 2).start()
        g_copy(t, q, 1).wait_recv()
        add_to(g_block(t, q, block_y, block // 2, block // 2), [r.near_half.at[t, q, 1]])
        g_copy(t, q, 3).start()

    def grads_third(t):
        for q in range(2):
            g_copy(t, q, 2).wait_recv()
            g_copy(t, q, 3).wait_recv()
            add_to(g_block(t, q, mine), [r.near_full.at[t, q, 0], r.near_full.at[t, q, 1]])

            if t == 0:

                @pl.when(far[q] != 0)
                def _():
                    g_home(t, q, far[q] - 1).start()

            else:

                @pl.when(z == edge)
                def _():
                    g_edge(t, q).start()

                @pl.when((far[q] != 0) & (z != edge) & (z != middle))
                def _():
                    g_home(t, q, 0).start()

    def grads_middle(t):
        @pl.when(z == middle)
        def _():
            for q in range(2):
                landed(r.from_z.at[Z_SLOT[t] + q], sem.gz_in.at[t, q])
                add_to(g_block(t, q, mine), [r.from_z.at[Z_SLOT[t] + q]])
                g_home(t, q, 1).start()

    def out_block(t, index, start=0, count=block):
        if t == 0:
            return r.g_heads.at[index, pl.ds(start, count)]
        return (r.g_up, r.g_down)[t - 1].at[pl.ds(pl.multiple_of(index * block + start, 32), count)]

    def end_local(t, q):
        return pltpu.make_async_copy(g_block(t, q, mine), out_block(t, mine), sem.end_in.at[t, 4])

    def end_copy(t, q, n):
        if n < 2:
            return remote(
                g_block(t, q, mine), out_block(t, mine), sem.end_send.at[t, n], sem.end_in.at[t, n],
                (next_x, next_y)[n],
            )
        if t == 0:
            return remote(
                g_block(t, q, mine), out_block(t, mine), sem.end_send.at[t, 2], sem.end_in.at[t, 2],
                (flip(next_x[0], by, 4), z),
            )
        ref = out_block(t, block_x, 0, block // 2) if n == 2 else out_block(t, block_y, block // 2, block // 2)
        return remote(ref, ref, sem.end_send.at[t, n], sem.end_in.at[t, n], (next_y, next_x)[n - 2])

    def end_pair(t, n):
        ref = out_block(t, (mine, block_x, block_y, block_d)[n])
        return remote(ref, ref, sem.end_send.at[t, 4 + n], sem.end_in.at[t, 5 + n], pair)

    def group_copy(t, q, step):
        return remote(
            g_block(t, q, mine), r.groups.at[t, step], sem.group_send.at[t, step], sem.group_in.at[t, step],
            ((w + 8 * step) % n_wide, z),
        )

    def grads_fourth(t):
        for q in range(2):

            @pl.when(far[q] == 0)
            def _():
                count = 3 if t == 0 else 2
                for slot in range(count):
                    landed(r.from_z.at[Z_SLOT[t] + slot], sem.gz_in.at[t, slot])
                add_to(g_block(t, q, mine), [r.from_z.at[Z_SLOT[t] + slot] for slot in range(count)])
                for step in range(1, groups):
                    group_copy(t, q, step).start()
                for step in range(1, groups):
                    group_copy(t, q, step).wait()
                for step in range(1, groups):
                    load = pltpu.make_async_copy(r.groups.at[t, step], r.from_z.at[Z_SLOT[t]], sem.group_load.at[t])
                    load.start()
                    load.wait()
                    add_to(g_block(t, q, mine), [r.from_z.at[Z_SLOT[t]]])
                end_local(t, q).start()
                end_copy(t, q, 0).start()
                end_copy(t, q, 1).start()
                if t == 0:
                    end_copy(t, q, 2).start()

    def grads_fifth(t):
        for q in range(2):

            @pl.when(far[q] == 0)
            def _():
                landed(out_block(t, block_x), sem.end_in.at[t, 0])
                if t > 0:
                    end_copy(t, q, 2).start()
                end_pair(t, 1).start()
                landed(out_block(t, block_y), sem.end_in.at[t, 1])
                if t > 0:
                    end_copy(t, q, 3).start()
                end_pair(t, 2).start()
                end_local(t, q).wait()
                end_pair(t, 0).start()

    def grads_sixth(t):
        for q in range(2):

            @pl.when(far[q] == 0)
            def _():
                if t == 0:
                    landed(out_block(t, block_d), sem.end_in.at[t, 2])
                else:
                    landed(out_block(t, block_d, 0, block // 2), sem.end_in.at[t, 2])
                    landed(out_block(t, block_d, block // 2, block // 2), sem.end_in.at[t, 3])
                end_pair(t, 3).start()

    def grads_done(t):
        for q in range(2):
            for n in range(4):
                g_copy(t, q, n).wait_send()

            @pl.when(far[q] != 0)
            def _():
                g_home(t, q, 0).wait_send()

            @pl.when(far[q] == 0)
            def _():
                for n in range(3 if t == 0 else 4):
                    end_copy(t, q, n).wait_send()
                for n in range(4):
                    end_pair(t, n).wait_send()

        @pl.when(jnp.logical_not(home))
        def _():
            for index in range(4):
                landed(out_block(t, (mine, block_x, block_y, block_d)[index]), sem.end_in.at[t, 5 + index])

    def result_copies(kind, source, dest):
        window = pl.ds((dest // 2) * (size // 2) + (dest % 2) * 256, 128)
        slot = 2 * (z % 2) + c
        own = home & (z == dest)
        mains, rests_in = ((r.out_o, r.out_r), (r.in_o, r.in_r))[kind]
        ends = (
            (source.at[own_rows, window], mains.at[slot]),
            (r.result_rest.at[kind, dest], rests_in.at[slot]),
        )
        here = [
            pltpu.make_async_copy(ref, target, sem.out_in.at[kind, slot, n]) for n, (ref, target) in enumerate(ends)
        ]
        there = [
            remote(
                ref, target, sem.out_send.at[kind, dest, n], sem.out_in.at[kind, slot, n], (w - c + z // 2, dest)
            )
            for n, (ref, target) in enumerate(ends)
        ]
        return own, here, there

    def results_start(kind, source):
        for g in range(2):
            at = pl.ds(g * (size // 2) + 128, 128)
            base = pl.multiple_of(c * part, 128)
            upper = source[pl.ds(base, part // 2), at].astype(F32)
            lower = pltpu.roll(source[pl.ds(base + part // 2, part // 2), at].astype(F32), 64, 1)
            lane = lax.broadcasted_iota(jnp.int32, upper.shape, 1)
            r.result_rest[kind, 2 * g] = jnp.where(lane < 64, upper, lower).astype(BF16)
            r.result_rest[kind, 2 * g + 1] = jnp.where(lane < 64, lower, upper).astype(BF16)
        for dest in range(4):
            own, here, there = result_copies(kind, source, dest)

            @pl.when(own)
            def _():
                for copy in here:
                    copy.start()

            @pl.when(jnp.logical_not(own))
            def _():
                for copy in there:
                    copy.start()

    def results_done(kind, source):
        mains, rests_in = ((r.out_o, r.out_r), (r.in_o, r.in_r))[kind]
        for slot in range(4):
            landed(mains.at[slot], sem.out_in.at[kind, slot, 0])
            landed(rests_in.at[slot], sem.out_in.at[kind, slot, 1])
        for dest in range(4):
            own, _, there = result_copies(kind, source, dest)

            @pl.when(jnp.logical_not(own))
            def _():
                for copy in there:
                    copy.wait_send()

    def results_turn(kind, stage_at, target, stage_out):
        mains, rests_in = ((r.out_o, r.out_r), (r.in_o, r.in_r))[kind]
        loads = []
        for slot in range(4):
            main_at = stage_at.at[pl.ds((slot // 2) * part, part), pl.ds((slot % 2) * 128, 128)]
            rest_at = stage_at.at[pl.ds(slot * (part // 2), part // 2), pl.ds(256, 128)]
            loads.append(pltpu.make_async_copy(mains.at[slot], main_at, sem.load.at[14 + slot]))
            loads.append(pltpu.make_async_copy(rests_in.at[slot], rest_at, sem.load.at[20 + slot]))
        for load in loads:
            load.start()
        for load in loads:
            load.wait()
        same, upper, lower = unit(part), unit(part // 2), unit(part // 2, part // 2)
        pieces = []
        for slot in range(4):
            main = tn(stage_at[(slot // 2) * part : (slot // 2 + 1) * part, (slot % 2) * 128 : (slot % 2 + 1) * 128], same)
            packed = stage_at[slot * (part // 2) : (slot + 1) * (part // 2), 256:384]
            first, second = tn(packed, upper), tn(packed, lower)
            rest = jnp.where(odd, first[64:] + second[:64], first[:64] + second[64:])
            pieces.append(
                jnp.where(odd, jnp.concatenate([rest, main], axis=0), jnp.concatenate([main, rest], axis=0))
            )
        turned = pltpu.roll(jnp.concatenate(pieces, axis=1), shift, 1).astype(stage_out.dtype)
        stores = []
        for n in range(2):
            stage_out[n * width : (n + 1) * width, :] = turned[:, n * half : (n + 1) * half]
            stores.append(
                pltpu.make_async_copy(
                    stage_out.at[pl.ds(n * width, width)], target.at[:, pl.ds(n * half, half)], sem.load.at[18 + n]
                )
            )
            stores[-1].start()
        for store in stores:
            store.wait()

    w_ada_again = r.slope.at[0]
    ada_loads = [
        pltpu.make_async_copy(
            r.w_ada.at[:, pl.ds(i * size, size)], w_ada_again.at[pl.ds(i * cond, cond)], sem.load.at[7 + i]
        )
        for i in range(6)
    ]

    def finish_small():
        per_slab = half // (4 * MSG_ROWS)
        count = 2 * planes
        slabs = -(-count // per_slab)
        loads = []
        for i in range(count):
            place = r.probs.at[i // per_slab, pl.ds((i % per_slab) * 4 * MSG_ROWS, 4 * MSG_ROWS)]
            source = r.messages.at[i // planes, i % planes]
            loads += [
                pltpu.make_async_copy(source.at[j], place.at[pl.ds(j * MSG_ROWS, MSG_ROWS)], sem.msg_load.at[i, j])
                for j in range(4)
            ]
        for load in loads:
            load.start()
        for load in loads + ada_loads:
            load.wait()
        totals = [None, None]
        ada = [None] * 6
        for n in range(slabs):
            used = min(count - n * per_slab, per_slab) * 4 * MSG_ROWS
            every = r.probs[n, :used, :]
            column = lax.broadcasted_iota(jnp.int32, (MSG_ROWS, used), 1)
            row = lax.broadcasted_iota(jnp.int32, (MSG_ROWS, used), 0)
            early = column + n * half < planes * 4 * MSG_ROWS
            for part_of in range(2):
                wanted = (column % MSG_ROWS == row) & (early if part_of == 0 else jnp.logical_not(early))
                term = nn(jnp.where(wanted, 1.0, 0.0).astype(BF16), every)
                totals[part_of] = term if totals[part_of] is None else totals[part_of] + term
            contexts = every[:, :cond].astype(F32)
            at = lax.broadcasted_iota(jnp.int32, contexts.shape, 0) % MSG_ROWS
            contexts = jnp.where(at == MSG_CONTEXT, contexts, 0.0)
            for i in range(6):
                moved = pltpu.roll(contexts, used - MSG_CONTEXT + i, 0).astype(BF16)
                term = tn(moved, every)
                ada[i] = term if ada[i] is None else ada[i] + term
        for i in range(6):
            r.grad_one[i * cond : (i + 1) * cond, :] = ada[i]
        r.small[...] = totals[0] + totals[1]
        up_rows = jnp.where(z // 2 == 0, totals[0][MSG_B_UP : MSG_B_UP + 2], totals[1][MSG_B_UP : MSG_B_UP + 2])
        r.small[MSG_B_UP : MSG_B_UP + 1, :] = jnp.where(odd, up_rows[1:2], up_rows[0:1])
        own_slot = jnp.where(
            (spans_own[0] >= spans_own[1]) & (spans_own[0] >= spans_own[2]),
            0,
            jnp.where(spans_own[1] >= spans_own[2], 1, 2),
        )
        place = lax.broadcasted_iota(jnp.int32, (8, 1), 0)
        grads = jnp.zeros((8, cond), F32)
        for half_at, seg, after in ((0, 0, 0), (1, 0, 1), (1, 1, 2)):
            group_at = seg * planes + plane_at
            base = (group_at % per_slab) * 4 * MSG_ROWS + (2 * c + half_at) * MSG_ROWS
            rows_at = r.probs[group_at // per_slab, pl.ds(pl.multiple_of(base, MSG_ROWS), MSG_ROWS), :]
            row = lax.broadcasted_iota(jnp.int32, (MSG_ROWS, 1), 0)
            total = jnp.zeros((MSG_ROWS, cond), F32)
            for i in range(6):
                total = total + jnp.where(row == i, nt(rows_at, w_ada_again[i * cond : (i + 1) * cond, :]), 0.0)
            slot = own_slot + after
            slot = jnp.where(slot >= slots, slot - slots, slot)
            grads = grads + jnp.where(place == slot, jnp.sum(total, axis=0, keepdims=True), 0.0)
        times = r.info[0]
        gate = 1.0 / (1.0 + jnp.exp(-times))
        r.context[...] = grads * (gate + times * gate * (1.0 - gate))
        copies = []
        for i in range(6):
            ends = (r.grad_one.at[pl.ds(i * cond, cond)], r.ada_out.at[:, pl.ds(i * size, size)])
            copies.append(pltpu.make_async_copy(*ends, sem.end_small.at[i]))
            ends = (r.small.at[i], r.b_ada_out.at[pl.ds(i * size, size)])
            copies.append(pltpu.make_async_copy(*ends, sem.end_small.at[6 + i]))
        rows_out = (
            (MSG_B_DOWN, r.b_down_out), (MSG_GAIN_ONE, r.gain_one_out), (MSG_GAIN_TWO, r.gain_two_out),
            (MSG_B_UP, r.b_up_out),
        )
        for i, (row, ref) in enumerate(rows_out):
            copies.append(pltpu.make_async_copy(r.small.at[row], ref, sem.end_small.at[12 + i]))
        copies.append(pltpu.make_async_copy(r.context.at[pl.ds(0, slots)], r.time_out, sem.end_small.at[16]))
        for copy in copies:
            copy.start()
        return copies

    time_load.wait()
    lane = lax.broadcasted_iota(jnp.int32, (1, 128), 1)
    length_row = jnp.zeros((1, 128), F32)
    for i in range(slots):
        length_row = jnp.where(lane == i, r.lengths[0, i].astype(F32), length_row)
    r.info[0, slots : slots + 1, :] = length_row
    for load in loads[4:8]:
        load.wait()
    r.b_own[...] = r.small[0:8, :]

    pl.semaphore_wait(barrier, len(peers))
    weights_start(0)
    info_copy = remote(r.info.at[0], r.info.at[1], sem.pair.at[2], sem.pair_in.at[2], pair)
    info_copy.start()
    b_copies = [
        remote(r.b_own, r.b_all.at[z], sem.b_send.at[dz], sem.b_in.at[dz], (w, (z + dz) % 4)) for dz in range(1, 4)
    ]
    for copy in b_copies:
        copy.start()

    info_copy.wait()
    info = jnp.where(home, r.info[0], r.info[1])
    context = info / (1.0 + jnp.exp(-info))
    context_low = context.astype(BF16)
    spans = [info[slots : slots + 1, i : i + 1] for i in range(slots)]
    longest = [
        (spans[0] >= spans[1]) & (spans[0] >= spans[2]),
        (spans[1] > spans[0]) & (spans[1] >= spans[2]),
        (spans[2] > spans[0]) & (spans[2] > spans[1]),
    ]

    def slot_after(shift):
        return [longest[(i - shift) % slots] for i in range(slots)]

    def pick(flags, values):
        total = None
        for flag, value in zip(flags, values):
            term = jnp.where(flag, value, 0.0)
            total = term if total is None else total + term
        return total

    flags_a = [jnp.where(odd, after.astype(F32), at.astype(F32)) > 0.5 for after, at in zip(slot_after(1), longest)]
    flags_b = [jnp.where(odd, after.astype(F32), at.astype(F32)) > 0.5 for after, at in zip(slot_after(2), longest)]
    bound = jnp.where(odd, pick(slot_after(1), spans), float(half))
    r.context[0:1, :] = pick(flags_a, [context[i : i + 1, :] for i in range(slots)])
    r.context[1:2, :] = pick(flags_b, [context[i : i + 1, :] for i in range(slots)])
    for load in loads[8:]:
        load.wait()
    rises = {}
    for i in range(6):
        modulation = nn(context_low, w_ada[i * cond : (i + 1) * cond, :]) + r.small[ROW_B_ADA + i : ROW_B_ADA + i + 1, :]
        for seg, flags in enumerate((flags_a, flags_b)):
            row = pick(flags, [modulation[n : n + 1, :] for n in range(slots)])
            if i in (1, 4):
                gain = r.small[ROW_GAIN_ONE : ROW_GAIN_ONE + 1, :] if i == 1 else r.small[ROW_GAIN_TWO : ROW_GAIN_TWO + 1, :]
                rise = 8 * seg + (RISE_ONE if i == 1 else RISE_TWO)
                r.mods[rise : rise + 1, :] = 1.0 + row
                row = gain * (1.0 + row)
            at = 8 * seg + (SHIFT_ONE, GAIN_ONE, GATE_ONE, SHIFT_TWO, GAIN_TWO, GATE_TWO)[i]
            r.mods[at : at + 1, :] = row
    inverse = jnp.exp((lane % (HD // 2)).astype(F32) * (-9.210340371976184 / (HD // 2)))
    signs = jnp.where(lane % HD < HD // 2, -1.0, 1.0)

    def tables(s, start):
        row = (lax.broadcasted_iota(jnp.int32, (TILE, 1), 0) + start).astype(F32)
        angles = jnp.where(row < bound, row, row - bound) * inverse
        r.cosine[s, :] = jnp.cos(angles)
        r.sine[s, :] = jnp.sin(angles) * signs

    tiles(half, tables)
    r.scales[...] = jnp.zeros_like(r.scales)
    r.sums[...] = jnp.zeros_like(r.sums)
    r.bias_up[...] = jnp.zeros_like(r.bias_up)
    loads[0].wait()
    loads[1].wait()
    turn_rows(0)
    rows_start(0, True)
    weights_own(0, False)
    rows_start(0, False)
    loads[2].wait()
    loads[3].wait()
    turn_rows(1)
    weights_own(0, True)
    for n, copy in enumerate(b_copies):
        landed(r.b_all.at[(z + 3 - n) % 4], sem.b_in.at[n + 1])
    r.b_all[z] = r.b_own[...]
    weights_pass(0)
    rows_join(0)
    weights_start(1)
    weights_done(0)

    def project_some(i, carry):
        @pl.when(i == 2)
        def _():
            rows_whole(0)

        project(
            bound, ((2 * c + i) % 4) * (part // 2), part // 2, r.x_low, r.mods, r.cosine, r.sine, r.w_attn, r.in_one,
            r.q, r.k, r.v,
        )
        return carry

    lax.fori_loop(0, 4, project_some, 0)
    weights_start(2)
    weights_own(1, False)
    rows_sent(0)
    attend(bound, 0, r.q, r.k, r.v, r.probs, r.scales, r.mixed)
    weights_own(1, True)
    rows_start(1, True)
    rows_start(1, False)
    attend(bound, 1, r.q, r.k, r.v, r.probs, r.scales, r.mixed)
    weights_pass(1)
    weights_own(2, False)
    attend(bound, 2, r.q, r.k, r.v, r.probs, r.scales, r.mixed)
    weights_own(2, True)
    mix_out(r.mixed, r.w_attn, r.attn_part, sharing(0, r.attn_part))
    weights_done(1)
    b_up = jnp.where(c == 0, r.b_all[0, 0:1, :], r.b_all[2, 0:1, :]), jnp.where(c == 0, r.b_all[1, 0:1, :], r.b_all[3, 0:1, :])
    feed_up(
        bound, r.x_low, r.mods, r.attn_part, r.w_ff.at[0], b_up, r.in_two, r.act, r.slope, arriving(0, r.attn_part)
    )
    weights_pass(2)
    rows_join(1)
    rows_whole(1)
    rows_sent(1)
    feed_grads(bound, r.dy_low, r.mods, r.feed_low, r.sums)
    for q in range(2):
        weight_grad(r.act.at[q], r.feed_low, r.g_ff.at[1, q])
        grads_start(2, q)
    weights_done(2)
    feed_down(r.act, r.w_ff.at[1], r.feed_part, sharing(1, r.feed_part))
    grads_second(2, 0)
    feed_back(r.feed_low, r.slope, r.w_ff.at[1], r.bias_up)
    grads_second(2, 1)
    for q in range(2):
        weight_grad(r.in_two, r.slope.at[q], r.g_ff.at[0, q])
        grads_start(1, q)
    feed_in_back(r.slope, r.w_ff.at[0], r.back_part, sharing(2, r.back_part))
    b_down = r.small[ROW_B_DOWN : ROW_B_DOWN + 1, :]
    feed_out(
        bound, r.x_low, r.dy_low, r.mods, r.attn_part, r.feed_part, b_down, r.out_low, r.sums, arriving(1, r.feed_part)
    )
    results_start(0, r.out_low)
    norm_two_back(
        bound, r.x_low, r.dy_low, r.mods, r.back_part, r.attn_part, r.w_attn, r.grad_one, r.feed_low, r.grad_mixed,
        r.sums, arriving(2, r.back_part),
    )
    weight_grad(r.mixed, r.feed_low, r.g_attn.at[3])
    grads_third(2)
    grads_second(1, 0)
    for g in range(3):
        attend_back(
            g, r.q, r.k, r.v, r.probs, r.scales, r.mixed, r.grad_mixed, r.cosine, r.sine, r.total_k, r.total_v,
            r.grad_q, r.grad_k, r.grad_v,
        )
        for t, grads in enumerate((r.grad_q, r.grad_k, r.grad_v)):
            r.g_attn[t, g * 128 : (g + 1) * 128, :] = tn(grads[:, lanes(g)], r.in_one[...]).astype(BF16)
        if g == 0:
            grads_second(1, 1)
        if g == 1:
            grads_start(0, 0)
    grads_start(0, 1)
    grads_third(1)
    project_back(r.grad_q, r.grad_k, r.grad_v, r.w_attn, r.act, sharing(3, r.act))
    grads_second(0, 0)
    grads_second(0, 1)
    grads_middle(2)
    norm_one_back(
        bound, r.x_low, r.mods, r.act, r.grad_one, r.in_two, r.sums, arriving(3, r.act)
    )

    def sum_row(piece):
        return jnp.where(c == 0, r.sums[piece : piece + 1, :], r.sums[8 + piece : 9 + piece, :])

    def mod_row(piece):
        return jnp.where(c == 0, r.mods[piece : piece + 1, :], r.mods[8 + piece : 9 + piece, :])

    gain_one = r.small[ROW_GAIN_ONE : ROW_GAIN_ONE + 1, :]
    gain_two = r.small[ROW_GAIN_TWO : ROW_GAIN_TWO + 1, :]
    context_row = jnp.where(c == 0, r.context[0:1, :], r.context[1:2, :])
    message = [
        sum_row(SUM_G1),
        sum_row(SUM_G1N) * gain_one,
        sum_row(SUM_GATE_ONE),
        sum_row(SUM_G2),
        sum_row(SUM_G2N) * gain_two,
        sum_row(SUM_GATE_TWO),
        sum_row(SUM_DY) * mod_row(GATE_TWO),
        sum_row(SUM_G1N) * mod_row(RISE_ONE),
        sum_row(SUM_G2N) * mod_row(RISE_TWO),
        r.bias_up[0:1, :],
        r.bias_up[1:2, :],
        jnp.concatenate([context_row] + [jnp.zeros((1, 128), F32)] * (size // 128 - 1), axis=1),
        jnp.zeros((4, size), F32),
    ]
    r.message[...] = jnp.concatenate(message, axis=0).astype(BF16)
    message_at = r.messages.at[c, plane_at, z]
    message_local = pltpu.make_async_copy(r.message, message_at, sem.m_in.at[0])
    message_local.start()
    message_copies = [
        remote(r.message, message_at, sem.m_send.at[dz], sem.m_in.at[dz], (w, (z + dz) % 4)) for dz in range(1, 4)
    ]
    for copy in message_copies:
        copy.start()
    for load in ada_loads:
        load.start()
    results_done(0, r.out_low)
    results_turn(0, r.act.at[0], r.out_t, r.feed_low)
    grads_middle(1)
    grads_third(0)
    grads_fourth(2)
    grads_fourth(1)
    results_start(1, r.in_two)
    message_local.wait()
    for dz in range(1, 4):
        landed(r.messages.at[c, plane_at, (z + 4 - dz) % 4], sem.m_in.at[dz])
    plane_copies = []
    for step in range(1, planes):
        ref = r.messages.at[c, plane_at]
        plane_copies.append(
            remote(ref, ref, sem.mp_send.at[step], sem.mp_in.at[step], ((w + 2 * step) % n_wide, z))
        )
        plane_copies[-1].start()
    grads_fifth(2)
    grads_fifth(1)
    for step in range(1, planes):
        landed(r.messages.at[c, (plane_at + planes - step) % planes], sem.mp_in.at[step])
    message_pair = remote(r.messages.at[c], r.messages.at[c], sem.m_send.at[4], sem.m_in.at[4], pair)
    message_pair.start()
    grads_fourth(0)
    grads_sixth(2)
    grads_sixth(1)
    landed(r.messages.at[1 - c], sem.m_in.at[4])
    small_ends = finish_small()
    grads_fifth(0)
    for copy in small_ends:
        copy.wait()
    results_done(1, r.in_two)
    results_turn(1, r.act.at[1], r.in_t, r.grad_one)
    grads_sixth(0)

    for t in range(CHUNKS):
        weights_sent(t)
    for kind in range(2):
        pair_rows(kind).wait_send()
    for copy in b_copies + message_copies + plane_copies + [message_pair]:
        copy.wait_send()
    for t in range(CHUNKS):
        grads_done(t)


def layer(n_wide, lengths, x, *others):
    width, rows = x.shape
    w_up, times = others[3], others[-1]
    size = w_up.shape[0]
    slots, cond = times.shape
    buffers, semaphores = scratch_plan(n_wide, rows, width, size, cond)
    anywhere = pl.BlockSpec(memory_space=pl.ANY)
    part, planes, groups = rows // 4, n_wide // 2, n_wide // 8
    outs = (
        ((width, rows), BF16),
        ((width, rows), F32),
        ((4, part, 128), BF16),
        ((4, part, 128), BF16),
        ((4, part // 2, 128), BF16),
        ((4, part // 2, 128), BF16),
        ((4, size // 4, size), BF16),
        ((size, size), BF16),
        ((size, size), BF16),
        ((2, planes, 4, MSG_ROWS, size), BF16),
        ((CHUNKS, groups, size // 4, size), BF16),
        ((cond, 6 * size), F32),
        ((6 * size,), F32),
        ((size,), F32),
        ((size,), F32),
        ((size,), F32),
        ((size,), F32),
        ((slots, cond), F32),
    )
    return pl.pallas_call(
        functools.partial(layer_kernel, n_wide, rows, width, size, cond, slots),
        out_shape=tuple(jax.ShapeDtypeStruct(shape, kind) for shape, kind in outs),
        in_specs=[pl.BlockSpec(memory_space=pltpu.SMEM)] + [anywhere] * (1 + len(others)),
        out_specs=(anywhere,) * len(outs),
        scratch_shapes=[pltpu.VMEM(shape, kind) for shape, kind in buffers.values()]
        + [pltpu.SemaphoreType.DMA(shape) for shape in semaphores.values()],
        compiler_params=pltpu.CompilerParams(
            collective_id=0, has_side_effects=True, vmem_limit_bytes=63 * 1024 * 1024
        ),
        name="layer",
    )(lengths, x, *others)


def body(
    n_wide,
    block_input,
    time_embed,
    seq_lengths,
    w_qkv,
    w_out,
    w_up,
    b_up,
    w_down,
    b_down,
    gain_one,
    gain_two,
    w_ada,
    b_ada,
    out_grad,
):
    results = layer(
        n_wide, seq_lengths, block_input.T, out_grad.T, jnp.swapaxes(w_qkv, 1, 2), w_out, w_up, w_down, b_up,
        b_down, gain_one, gain_two, w_ada, b_ada, time_embed,
    )
    out_t, in_t, _, _, _, _, g_heads, g_up, g_down, _, _ = results[:11]
    ada, b_ada_sum, b_down_sum, gain_one_sum, gain_two_sum, b_up_sum, times = results[11:18]
    return (
        out_t.T,
        in_t.T,
        times,
        jnp.swapaxes(g_heads[:3].astype(F32), 1, 2),
        g_heads[3].astype(F32),
        g_up.astype(F32),
        b_up_sum,
        g_down.astype(F32),
        b_down_sum,
        gain_one_sum,
        gain_two_sum,
        ada,
        b_ada_sum,
    )


def solution(mesh):
    return jax.shard_map(
        functools.partial(body, mesh.shape["wide"]),
        mesh=mesh,
        in_specs=(
            P("wide", "narrow"),
            P("wide", None),
            P("wide", None),
            P(None, None, "narrow"),
            P("narrow", None),
            P(None, "narrow"),
            P("narrow"),
            P("narrow", None),
            P(),
            P(),
            P(),
            P(),
            P(),
            P("wide", "narrow"),
        ),
        out_specs=(
            P("wide", "narrow"),
            P("wide", "narrow"),
            P("wide", None),
            P(None, None, "narrow"),
            P("narrow", None),
            P(None, "narrow"),
            P("narrow"),
            P("narrow", None),
            P(),
            P(),
            P(),
            P(),
            P(),
        ),
        check_vma=False,
    )
```

```python
import functools
from types import SimpleNamespace

import jax
import jax.numpy as jnp
from jax import lax
from jax.experimental import pallas as pl
from jax.experimental.pallas import tpu as pltpu
from jax.sharding import PartitionSpec as P

HD = 64
LOG2_E = 1.4426950408889634
epsilon = 1e-05
MESH = pl.DeviceIdType.MESH
CHUNKS = 3
F32 = jnp.float32
BF16 = jnp.bfloat16


def flip(w, bit, step):
    return w + step * (1 - 2 * bit)


def remote(src, dst, send, recv, device):
    return pltpu.make_async_remote_copy(
        src_ref=src, dst_ref=dst, send_sem=send, recv_sem=recv, device_id=device, device_id_type=MESH
    )


def landed(ref, sem):
    pltpu.make_async_copy(ref, ref, sem).wait()


def dot(a, b, dims):
    return lax.dot_general(a, b, (dims, ((), ())), preferred_element_type=F32)


def nn(a, b):
    return dot(a, b, ((1,), (0,)))


def nt(a, b):
    return dot(a, b, ((1,), (1,)))


def tn(a, b):
    return dot(a, b, ((0,), (0,)))


TILE = 256
ATTEND = 384
ATTEND_BACK = 384


def tiles(count, step, size=TILE):
    def run(i, carry):
        step(pl.ds(pl.multiple_of(i * size, size), size), i * size)
        return carry

    lax.fori_loop(0, count // size, run, 0)


def norm_stats(inputs):
    row_mean = jnp.mean(inputs, axis=-1, keepdims=True)
    centered = inputs - row_mean
    variance = jnp.mean(centered * centered, axis=-1, keepdims=True)
    scaled = lax.rsqrt(variance + epsilon)
    return (centered * scaled, scaled)


def norm_back(grad_normed, normed, scaled):
    first_term = jnp.mean(grad_normed, axis=-1, keepdims=True)
    second_term = jnp.mean(grad_normed * normed, axis=-1, keepdims=True)
    return scaled * (grad_normed - first_term - normed * second_term)


GAIN_ONE, SHIFT_ONE, GATE_ONE, GAIN_TWO, SHIFT_TWO, GATE_TWO, RISE_ONE, RISE_TWO = range(8)
SUM_G1, SUM_G1N, SUM_GATE_ONE, SUM_G2, SUM_G2N, SUM_GATE_TWO, SUM_DY = range(7)


def chosen(mods, first, piece):
    return jnp.where(first, mods[piece : piece + 1, :], mods[8 + piece : 9 + piece, :])


def first_rows(bound, start, count):
    return (lax.broadcasted_iota(jnp.int32, (count, 1), 0) + start).astype(F32) < bound


def add_sums(sums, piece, first, values):
    total = jnp.sum(values, axis=0, keepdims=True)
    head = jnp.sum(jnp.where(first, values, 0.0), axis=0, keepdims=True)
    sums[piece : piece + 1, :] += head
    sums[8 + piece : 9 + piece, :] += total - head


def swapped(pair):
    lane = lax.broadcasted_iota(jnp.int32, pair.shape, 1)
    return jnp.where(lane % HD < HD // 2, pltpu.roll(pair, 128 - HD // 2, 1), pltpu.roll(pair, HD // 2, 1))


def lanes(g):
    return pl.ds(g * 128, 128)


def head_only(pair, hh):
    lane = lax.broadcasted_iota(jnp.int32, pair.shape, 1)
    return jnp.where((lane < HD) == (hh == 0), pair, jnp.zeros_like(pair))


def project(bound, start, rows, x, mods, cosine, sine, w_attn, in_one, q, k, v):
    s = pl.ds(pl.multiple_of(start, 64), rows)
    first = first_rows(bound, start, rows)
    normed, _ = norm_stats(x[s, :].astype(F32))
    low = (normed * chosen(mods, first, GAIN_ONE) + chosen(mods, first, SHIFT_ONE)).astype(BF16)
    in_one[s, :] = low
    cos_rows, sin_rows = cosine[s, :], sine[s, :]
    for t, target in enumerate((q, k)):
        raw = nt(low, w_attn[t])
        for g in range(raw.shape[1] // 128):
            pair = raw[:, g * 128 : (g + 1) * 128]
            turned = pair * cos_rows + swapped(pair) * sin_rows
            target[s, lanes(g)] = (turned * (0.125 * LOG2_E if t == 0 else 1.0)).astype(BF16)
    v[s, :] = nt(low, w_attn[2]).astype(BF16)


def attend(bound, g, q, k, v, probs, scales, mixed):
    rows = q.shape[0]

    def step(s, start):
        first = first_rows(bound, start, ATTEND)
        column = lax.broadcasted_iota(jnp.int32, (1, rows), 1).astype(F32) < bound
        bias = jnp.where(first == column, 0.0, -1e30)
        halves = []
        for hh in range(2):
            scores = nt(head_only(q[s, lanes(g)], hh), k[:, lanes(g)]) + bias
            expos = jnp.exp2(scores - jnp.max(scores, axis=-1, keepdims=True))
            low = expos.astype(BF16)
            probs[2 * g + hh, s, :] = low
            scale = 1.0 / jnp.sum(expos, axis=-1, keepdims=True)
            kept = scales[s, :]
            scales[s, :] = jnp.where(lax.broadcasted_iota(jnp.int32, kept.shape, 1) == 2 * g + hh, scale, kept)
            halves.append(nn(low, v[:, lanes(g)]) * scale)
        lane = lax.broadcasted_iota(jnp.int32, halves[0].shape, 1)
        mixed[s, lanes(g)] = jnp.where(lane < HD, halves[0], halves[1]).astype(BF16)

    tiles(rows, step, ATTEND)


def mix_out(mixed, w_attn, part, share):
    def step(s, start):
        part[0, s, :] = nn(mixed[s, :], w_attn[3]).astype(BF16)
        share(s, start)

    tiles(mixed.shape[0], step)


def both(part, s):
    return part[0, s, :].astype(F32) + part[1, s, :].astype(F32)


def hidden_rows(first, s, x, mods, attn_part):
    return x[s, :].astype(F32) + chosen(mods, first, GATE_ONE) * both(attn_part, s)


def feed_up(bound, x, mods, attn_part, w_up, b_up, in_two, act, slope, arrived):
    def step(s, start):
        arrived(s, start)
        first = first_rows(bound, start, TILE)
        normed, _ = norm_stats(hidden_rows(first, s, x, mods, attn_part))
        low = (normed * chosen(mods, first, GAIN_TWO) + chosen(mods, first, SHIFT_TWO)).astype(BF16)
        in_two[s, :] = low
        for n in range(2):
            pre = nn(low, w_up[n]) + b_up[n]
            square = pre * pre
            bent = jnp.tanh(0.7978845608028654 * pre * (1.0 + 0.044715 * square))
            rise = 0.5 * (1.0 + bent)
            act[n, s, :] = (pre * rise).astype(BF16)
            inner = 0.7978845608028654 + 0.10703222443 * square
            slope[n, s, :] = (rise + 0.5 * pre * (1.0 - bent * bent) * inner).astype(BF16)

    tiles(x.shape[0], step)


def feed_grads(bound, dy, mods, feed_low, sums):
    def step(s, start):
        first = first_rows(bound, start, TILE)
        grads = dy[s, :].astype(F32)
        add_sums(sums, SUM_DY, first, grads)
        feed_low[s, :] = (grads * chosen(mods, first, GATE_TWO)).astype(BF16)

    tiles(dy.shape[0], step)


def feed_down(act, w_down, part, share):
    def step(s, start):
        part[0, s, :] = (nn(act[0, s, :], w_down[0]) + nn(act[1, s, :], w_down[1])).astype(BF16)
        share(s, start)

    tiles(act.shape[1], step)


def feed_out(bound, x, dy, mods, attn_part, feed_part, b_down, out, sums, arrived):
    def step(s, start):
        arrived(s, start)
        first = first_rows(bound, start, TILE)
        rows = both(feed_part, s) + b_down
        out[s, :] = (hidden_rows(first, s, x, mods, attn_part) + chosen(mods, first, GATE_TWO) * rows).astype(BF16)
        add_sums(sums, SUM_GATE_TWO, first, dy[s, :].astype(F32) * rows)

    tiles(dy.shape[0], step)


def feed_back(feed_low, slope, w_down, bias_up):
    def step(s, start):
        low = feed_low[s, :]
        for n in range(2):
            grad_pre = nt(low, w_down[n]) * slope[n, s, :].astype(F32)
            bias_up[n : n + 1, :] += jnp.sum(grad_pre, axis=0, keepdims=True)
            slope[n, s, :] = grad_pre.astype(BF16)

    tiles(feed_low.shape[0], step)


def feed_in_back(pre_low, w_up, part, share):
    def step(s, start):
        part[0, s, :] = (nt(pre_low[0, s, :], w_up[0]) + nt(pre_low[1, s, :], w_up[1])).astype(BF16)
        share(s, start)

    tiles(pre_low.shape[1], step)


def weight_grad(left, right, target):
    def step(s, start):
        target[s, :] = tn(left[:, s], right[...]).astype(BF16)

    size = 384 if left.shape[1] % 384 == 0 else 128
    tiles(left.shape[1], step, size)


def norm_two_back(bound, x, dy, mods, back_part, attn_part, w_attn, grad_one, attn_low, grad_mixed, sums, arrived):
    def step(s, start):
        arrived(s, start)
        first = first_rows(bound, start, TILE)
        grads = both(back_part, s)
        normed, scaled = norm_stats(hidden_rows(first, s, x, mods, attn_part))
        add_sums(sums, SUM_G2, first, grads)
        add_sums(sums, SUM_G2N, first, grads * normed)
        rows = dy[s, :].astype(F32) + norm_back(grads * chosen(mods, first, GAIN_TWO), normed, scaled)
        grad_one[s, :] = rows
        add_sums(sums, SUM_GATE_ONE, first, rows * both(attn_part, s))
        low = (rows * chosen(mods, first, GATE_ONE)).astype(BF16)
        attn_low[s, :] = low
        grad_mixed[s, :] = nt(low, w_attn[3]).astype(BF16)

    tiles(dy.shape[0], step)


def attend_back(g, q, k, v, probs, scales, mixed, grad_mixed, cosine, sine, total_k, total_v, grad_q, grad_k, grad_v):
    rows = q.shape[0]

    def turned_back(pair, s):
        return pair * cosine[s, :] - swapped(pair) * sine[s, :]

    total_k[...] = jnp.zeros_like(total_k)
    total_v[...] = jnp.zeros_like(total_v)

    def step(s, start):
        upstream = grad_mixed[s, lanes(g)]
        product = upstream.astype(F32) * mixed[s, lanes(g)].astype(F32)
        halves = []
        for hh in range(2):
            kept = scales[s, :]
            here = lax.broadcasted_iota(jnp.int32, kept.shape, 1) == 2 * g + hh
            scale = jnp.sum(jnp.where(here, kept, 0.0), axis=-1, keepdims=True)
            row_dot = jnp.sum(head_only(product, hh), axis=-1, keepdims=True) * scale
            up_head = (head_only(upstream, hh).astype(F32) * scale).astype(BF16)
            low = probs[2 * g + hh, s, :]
            grad_weights = nt(up_head, v[:, lanes(g)])
            grad_scores = (low.astype(F32) * (grad_weights - row_dot)).astype(BF16)
            halves.append(nn(grad_scores, k[:, lanes(g)]))
            total_v[...] += tn(low, up_head)
            total_k[...] += tn(grad_scores, head_only(q[s, lanes(g)], hh))
        lane = lax.broadcasted_iota(jnp.int32, halves[0].shape, 1)
        pair = jnp.where(lane < HD, halves[0], halves[1]) * 0.125
        grad_q[s, lanes(g)] = turned_back(pair, s).astype(BF16)

    tiles(rows, step, ATTEND_BACK)

    def finish(s, start):
        grad_k[s, lanes(g)] = turned_back(total_k[s, :] * (1.0 / LOG2_E), s).astype(BF16)
        grad_v[s, lanes(g)] = total_v[s, :].astype(BF16)

    tiles(rows, finish)


def project_back(grad_q, grad_k, grad_v, w_attn, part, share):
    def step(s, start):
        total = nn(grad_q[s, :], w_attn[0]) + nn(grad_k[s, :], w_attn[1]) + nn(grad_v[s, :], w_attn[2])
        part[0, s, :] = total.astype(BF16)
        share(s, start)

    tiles(grad_q.shape[0], step)


def norm_one_back(bound, x, mods, back_part, grad_one, in_grad, sums, arrived):
    def step(s, start):
        arrived(s, start)
        first = first_rows(bound, start, TILE)
        grads = both(back_part, s)
        normed, scaled = norm_stats(x[s, :].astype(F32))
        add_sums(sums, SUM_G1, first, grads)
        add_sums(sums, SUM_G1N, first, grads * normed)
        rows = grad_one[s, :] + norm_back(grads * chosen(mods, first, GAIN_ONE), normed, scaled)
        in_grad[s, :] = rows.astype(BF16)

    tiles(x.shape[0], step)


ROW_B_UP, ROW_B_DOWN, ROW_GAIN_ONE, ROW_GAIN_TWO, ROW_B_ADA = 0, 1, 2, 3, 8
MSG_MOD, MSG_B_DOWN, MSG_GAIN_ONE, MSG_GAIN_TWO, MSG_B_UP, MSG_CONTEXT = 0, 6, 7, 8, 9, 11
MSG_ROWS = 16
Z_SLOT = (0, 3, 5)


def scratch_plan(n_wide, rows, width, size, cond):
    half, heads = rows // 2, 2 * width // HD
    block = size // 4
    buffers = {
        "tail": ((half // 2, 128), F32),
        "small": ((16, size), F32),
        "b_all": ((4, 8, size), F32),
        "b_own": ((8, size), F32),
        "info": ((2, 8, 128), F32),
        "context": ((8, 128), F32),
        "mods": ((16, size), F32),
        "sums": ((16, size), F32),
        "bias_up": ((8, size), F32),
        "message": ((MSG_ROWS, size), BF16),
        "rest": ((2, 4, half // 4, 128), BF16),
        "result_rest": ((2, 4, half // 4, 128), BF16),
        "x_low": ((half, size), BF16),
        "dy_low": ((half, size), BF16),
        "cosine": ((half, 128), F32),
        "sine": ((half, 128), F32),
        "w_attn": ((4, 2 * block, size), BF16),
        "w_ff": ((2, 2, size, size), BF16),
        "in_one": ((half, size), BF16),
        "q": ((half, 2 * width), BF16),
        "k": ((half, 2 * width), BF16),
        "v": ((half, 2 * width), BF16),
        "probs": ((heads, half, half), BF16),
        "scales": ((half, 128), F32),
        "mixed": ((half, 2 * width), BF16),
        "attn_part": ((2, half, size), BF16),
        "feed_part": ((2, half, size), BF16),
        "back_part": ((2, half, size), BF16),
        "in_two": ((half, size), BF16),
        "act": ((2, half, size), BF16),
        "slope": ((2, half, size), BF16),
        "out_low": ((half, size), BF16),
        "feed_low": ((half, size), BF16),
        "grad_one": ((half, size), F32),
        "grad_mixed": ((half, 2 * width), BF16),
        "total_k": ((half, 128), F32),
        "total_v": ((half, 128), F32),
        "grad_q": ((half, 2 * width), BF16),
        "grad_k": ((half, 2 * width), BF16),
        "grad_v": ((half, 2 * width), BF16),
        "g_attn": ((4, 2 * block, size), BF16),
        "g_ff": ((2, 2, size, size), BF16),
        "near_half": ((CHUNKS, 2, 2, block // 2, size), BF16),
        "near_full": ((CHUNKS, 2, 2, block, size), BF16),
        "from_z": ((7, block, size), BF16),
    }
    planes = n_wide // 2
    groups = n_wide // 8
    semaphores = {
        "load": (28,),
        "msg_load": (n_wide, 4),
        "end_small": (17,),
        "pair": (4,),
        "pair_in": (4,),
        "b_send": (4,),
        "b_in": (4,),
        "x_send": (2, 4, 2),
        "x_in": (2, 4, 2),
        "home": (CHUNKS, 4),
        "home_send": (CHUNKS, 2),
        "edge_send": (CHUNKS, 2),
        "z_in": (CHUNKS, 2),
        "w_send": (CHUNKS, 2, 4),
        "w_in": (CHUNKS, 2, 4),
        "part_send": (4, 4),
        "part_in": (4, 4),
        "out_send": (2, 4, 2),
        "out_in": (2, 4, 2),
        "g_send": (CHUNKS, 2, 5),
        "g_in": (CHUNKS, 2, 4),
        "gz_in": (CHUNKS, 3),
        "group_send": (CHUNKS, groups),
        "group_in": (CHUNKS, groups),
        "group_load": (CHUNKS,),
        "end_send": (CHUNKS, 8),
        "end_in": (CHUNKS, 9),
        "m_send": (5,),
        "m_in": (5,),
        "mp_send": (planes,),
        "mp_in": (planes,),
    }
    return buffers, semaphores


def layer_kernel(n_wide, rows, width, size, cond, slots, *refs):
    buffers, semaphores = scratch_plan(n_wide, rows, width, size, cond)
    names = (
        ["lengths", "x", "dy", "w_qkv", "w_out", "w_up", "w_down", "b_up", "b_down", "gain_one", "gain_two", "w_ada"]
        + ["b_ada", "times", "out_t", "in_t", "out_o", "in_o", "out_r", "in_r", "g_qkv", "g_o", "g_up", "g_down", "messages", "groups"]
        + ["ada_out", "b_ada_out", "b_down_out", "gain_one_out", "gain_two_out", "b_up_out", "time_out"]
        + list(buffers)
    )
    r = SimpleNamespace(**dict(zip(names, refs)))
    sem = SimpleNamespace(**dict(zip(semaphores, refs[len(names) :])))
    half = rows // 2
    part = half // 2
    block = size // 4
    planes, groups = n_wide // 2, n_wide // 8

    w = lax.axis_index("wide")
    z = lax.axis_index("narrow")
    c, bx, by, plane_at = w % 2, (w // 2) % 2, (w // 4) % 2, w // 2
    pair = (flip(w, c, 1), z)
    next_x, next_y = (flip(w, bx, 2), z), (flip(w, by, 4), z)
    mine = bx + 2 * by
    block_x, block_y, block_d = mine + 1 - 2 * bx, mine + 2 - 4 * by, 3 - mine
    far = [(z - 2 * c - q) % 4 for q in range(2)]
    home = c == z // 2
    odd = z % 2 == 1

    peers = [(w if same else pair[0], (z + dz) % 4) for same in (1, 0) for dz in range(4) if not (same and dz == 0)]
    peers += [((w + 2 * step) % n_wide, z) for step in range(1, planes)]
    barrier = pltpu.get_barrier_semaphore()
    for device in peers:
        pl.semaphore_signal(barrier, inc=1, device_id=device, device_id_type=MESH)

    w_ada = r.probs.at[2]
    raw = r.probs.at[3]
    loads = []
    for i in range(4):
        source = (r.x, r.dy)[i // 2].at[:, pl.ds((i % 2) * half, half)]
        loads.append(pltpu.make_async_copy(source, raw.at[pl.ds(i * width, width)], sem.load.at[(0, 1, 26, 27)[i]]))
    for i, ref in enumerate((r.b_up, r.b_down, r.gain_one, r.gain_two)):
        loads.append(pltpu.make_async_copy(ref, r.small.at[i], sem.load.at[2 + i]))
    for i in range(6):
        piece = pl.ds(i * size, size)
        loads.append(pltpu.make_async_copy(r.b_ada.at[piece], r.small.at[ROW_B_ADA + i], sem.load.at[20 + i]))
    for i in range(6):
        loads.append(
            pltpu.make_async_copy(
                r.w_ada.at[:, pl.ds(i * size, size)], w_ada.at[pl.ds(i * cond, cond)], sem.load.at[7 + i]
            )
        )
    for load in loads:
        load.start()
    r.info[0] = jnp.zeros((8, 128), F32)
    time_load = pltpu.make_async_copy(r.times, r.info.at[0, pl.ds(0, slots)], sem.load.at[13])
    time_load.start()

    def w_block(t, q, index, start=0, count=block):
        if t == 0:
            return r.w_attn.at[index, pl.ds(q * block + start, count)]
        return r.w_ff.at[t - 1, q, pl.ds(pl.multiple_of(index * block + start, 32), count)]

    def home_copies(t, q):
        if t == 0:
            copies = [pltpu.make_async_copy(r.w_qkv.at[i], w_block(0, q, i), sem.home.at[0, i]) for i in range(3)]
            return copies + [pltpu.make_async_copy(r.w_out, w_block(0, q, 3), sem.home.at[0, 3])]
        return [pltpu.make_async_copy((r.w_up, r.w_down)[t - 1], r.w_ff.at[t - 1, q], sem.home.at[t, 0])]

    edge, middle = 3 - 3 * c, 2 - c

    def home_sends(t, q, source):
        return [
            remote(
                source, w_block(t, q, mine), sem.home_send.at[t, n], sem.z_in.at[t, q], (w, c + (c + q + n + 1) % 3)
            )
            for n in range(2)
        ]

    def home_each(t, q, action):
        if t == 0:

            @pl.when(mine == 3)
            def _():
                for copy in home_sends(t, q, r.w_out):
                    action(copy)

            @pl.when(mine != 3)
            def _():
                for copy in home_sends(t, q, r.w_qkv.at[jnp.minimum(mine, 2)]):
                    action(copy)

        else:
            for copy in home_sends(t, q, (r.w_up, r.w_down)[t - 1].at[pl.ds(pl.multiple_of(mine * block, 32), block)]):
                action(copy)

    def edge_copy(t, q):
        ref = w_block(t, q, mine)
        return remote(ref, ref, sem.edge_send.at[t, q], sem.z_in.at[t, q], (w, edge))

    def w_copy(t, q, n):
        index, start, count, device = (
            (mine, 0, block, next_x),
            (mine, 0, block, next_y),
            (block_x, 0, block // 2, next_y),
            (block_y, block // 2, block // 2, next_x),
        )[n]
        ref = w_block(t, q, index, start, count)
        return remote(ref, ref, sem.w_send.at[t, q, n], sem.w_in.at[t, q, n], device)

    def weights_start(t):
        for q in range(2):

            @pl.when(far[q] == 0)
            def _():
                home_each(t, q, lambda copy: copy.start())
                for copy in home_copies(t, q):
                    copy.start()

    def weights_own(t, at_edge):
        for q in range(2):

            @pl.when((z == edge) if at_edge else (far[q] != 0) & (z != edge))
            def _():
                landed(w_block(t, q, mine), sem.z_in.at[t, q])

                @pl.when(z == middle)
                def _():
                    edge_copy(t, q).start()

                w_copy(t, q, 0).start()
                w_copy(t, q, 1).start()

    def weights_pass(t):
        for q in range(2):

            @pl.when(far[q] != 0)
            def _():
                landed(w_block(t, q, block_x), sem.w_in.at[t, q, 0])
                w_copy(t, q, 2).start()
                landed(w_block(t, q, block_y), sem.w_in.at[t, q, 1])
                w_copy(t, q, 3).start()

    def weights_done(t):
        for q in range(2):

            @pl.when(far[q] != 0)
            def _():
                landed(w_block(t, q, block_d, 0, block // 2), sem.w_in.at[t, q, 2])
                landed(w_block(t, q, block_d, block // 2, block // 2), sem.w_in.at[t, q, 3])

            @pl.when(far[q] == 0)
            def _():
                for copy in home_copies(t, q):
                    copy.wait()

    def weights_sent(t):
        for q in range(2):

            @pl.when(far[q] == 0)
            def _():
                home_each(t, q, lambda copy: copy.wait_send())

            @pl.when(far[q] != 0)
            def _():
                for n in range(4):
                    w_copy(t, q, n).wait_send()

                @pl.when(z == middle)
                def _():
                    edge_copy(t, q).wait_send()

    stage = (r.probs.at[1], r.g_ff.at[0, 0])
    rests = 2 * 128

    def row_copies(kind, j):
        device = (w - c + j % 2, 2 * c + j // 2)
        own = (c == j % 2) & (2 * c + j // 2 == z)
        target = (r.x_low, r.dy_low)[kind]
        ends = (
            (
                stage[kind].at[pl.ds((j % 2) * part, part), pl.ds((j // 2) * 128, 128)],
                target.at[
                    pl.ds((j % 2) * part, part),
                    pl.ds(pl.multiple_of((z // 2) * (size // 2) + (z % 2) * 256, 128), 128),
                ],
            ),
            (stage[kind].at[pl.ds(j * (part // 2), part // 2), pl.ds(rests, 128)], r.rest.at[kind, z]),
        )
        here = [
            pltpu.make_async_copy(source, dest, sem.x_in.at[kind, z, n]) for n, (source, dest) in enumerate(ends)
        ]
        there = [
            remote(source, dest, sem.x_send.at[kind, j, n], sem.x_in.at[kind, z, n], device)
            for n, (source, dest) in enumerate(ends)
        ]
        return own, here, there

    spans_own = [r.lengths[0, i] for i in range(slots)]
    shift = jnp.where(
        (spans_own[0] >= spans_own[1]) & (spans_own[0] >= spans_own[2]),
        0,
        jnp.where(spans_own[1] >= spans_own[2], spans_own[0], spans_own[0] + spans_own[1]),
    )

    def unit(count, first=0, total=part):
        row = lax.broadcasted_iota(jnp.int32, (count, 1), 0) + first
        column = lax.broadcasted_iota(jnp.int32, (1, total), 1)
        return jnp.where(row == column, 1.0, 0.0).astype(BF16)

    def turn_rows(kind):
        back = jnp.where(shift == 0, 0, rows - shift)
        at = 2 * kind * width
        columns = jnp.concatenate([raw[at : at + width, :], raw[at + width : at + 2 * width, :]], axis=1)
        columns = pltpu.roll(columns.astype(F32), back, 1).astype(BF16)
        raw[at : at + width, :] = columns[:, :half]
        raw[at + width : at + 2 * width, :] = columns[:, half:]
        same = unit(part)
        r.tail[...] = jnp.zeros_like(r.tail)
        for j in range(4):
            row, lane_at = at + (j // 2) * width, (j % 2) * part
            turned = nt(same, raw[row : row + width, lane_at : lane_at + part])
            main = turned[:, :128]
            r.tail[:, : width - 128] = turned[:, 128:]
            tail = r.tail[...]
            lane = lax.broadcasted_iota(jnp.int32, main.shape, 1)
            main_turned = pltpu.roll(main, 64, 1)
            tail_turned = pltpu.roll(tail, 64, 1)
            full = jnp.where(odd, jnp.where(lane < 64, main_turned, tail_turned), main)
            left = jnp.where(odd, jnp.where(lane < 64, 0.0, main_turned), tail)
            stage[kind][(j % 2) * part : (j % 2 + 1) * part, (j // 2) * 128 : (j // 2 + 1) * 128] = full.astype(BF16)
            packed = left[: part // 2] + pltpu.roll(left[part // 2 :], 64, 1)
            stage[kind][j * (part // 2) : (j + 1) * (part // 2), rests : rests + 128] = packed.astype(BF16)

    def rows_start(kind, outer):
        for j in range(4):
            own, here, there = row_copies(kind, j)
            wanted = (c == j // 2) == outer

            @pl.when(wanted & own)
            def _():
                for copy in here:
                    copy.start()

            @pl.when(wanted & jnp.logical_not(own))
            def _():
                for copy in there:
                    copy.start()

    def rows_sent(kind):
        for j in range(4):
            own, _, there = row_copies(kind, j)

            @pl.when(jnp.logical_not(own))
            def _():
                for copy in there:
                    copy.wait_send()

    own_rows = pl.ds(pl.multiple_of(c * part, 128), part)
    other_rows = pl.ds(pl.multiple_of((1 - c) * part, 128), part)

    def pair_rows(kind):
        target = (r.x_low, r.dy_low)[kind]
        return remote(target.at[own_rows], target.at[own_rows], sem.pair.at[kind], sem.pair_in.at[kind], pair)

    def rows_join(kind):
        target = (r.x_low, r.dy_low)[kind]
        for slot in range(4):
            at = (slot // 2) * (size // 2) + (slot % 2) * 256
            landed(target.at[own_rows, pl.ds(at, 128)], sem.x_in.at[kind, slot, 0])
            landed(r.rest.at[kind, slot], sem.x_in.at[kind, slot, 1])
        for g in range(2):
            even, odds = r.rest[kind, 2 * g].astype(F32), r.rest[kind, 2 * g + 1].astype(F32)
            lane = lax.broadcasted_iota(jnp.int32, even.shape, 1)
            upper = jnp.where(lane < 64, even, odds)
            lower = pltpu.roll(jnp.where(lane < 64, odds, even), 64, 1)
            at = pl.ds(g * (size // 2) + 128, 128)
            base = pl.multiple_of(c * part, 128)
            target[pl.ds(base, part // 2), at] = upper.astype(BF16)
            target[pl.ds(base + part // 2, part // 2), at] = lower.astype(BF16)
        pair_rows(kind).start()

    def rows_whole(kind):
        target = (r.x_low, r.dy_low)[kind]
        landed(target.at[other_rows], sem.pair_in.at[kind])

    def part_copy(n, ref, s, start):
        i = start // TILE
        return remote(ref.at[0, s], ref.at[1, s], sem.part_send.at[n, i], sem.part_in.at[n, i], pair)

    def sharing(n, ref):
        return lambda s, start: part_copy(n, ref, s, start).start()

    def arriving(n, ref):
        def wait(s, start):
            copy = part_copy(n, ref, s, start)
            copy.wait_recv()
            copy.wait_send()

        return wait

    def g_block(t, q, index, start=0, count=block):
        if t == 0:
            return r.g_attn.at[index, pl.ds(q * block + start, count)]
        return r.g_ff.at[t - 1, q, pl.ds(pl.multiple_of(index * block + start, 32), count)]

    def add_to(target, terms):
        def step(s, start):
            total = target[s, :].astype(F32)
            for term in terms:
                total = total + term[s, :].astype(F32)
            target[s, :] = total.astype(BF16)

        tiles(target.shape[0], step, 32)

    def g_copy(t, q, n):
        source, dest, device = (
            (g_block(t, q, block_d, 0, block // 2), r.near_half.at[t, q, 0], next_y),
            (g_block(t, q, block_d, block // 2, block // 2), r.near_half.at[t, q, 1], next_x),
            (g_block(t, q, block_x), r.near_full.at[t, q, 0], next_x),
            (g_block(t, q, block_y), r.near_full.at[t, q, 1], next_y),
        )[n]
        return remote(source, dest, sem.g_send.at[t, q, n], sem.g_in.at[t, q, n], device)

    def g_home(t, q, slot):
        return remote(
            g_block(t, q, mine), r.from_z.at[Z_SLOT[t] + slot], sem.g_send.at[t, q, 4], sem.gz_in.at[t, slot], (w, 2 * c + q)
        )

    def g_edge(t, q):
        return remote(g_block(t, q, mine), r.from_z.at[Z_SLOT[t] + q], sem.g_send.at[t, q, 4], sem.gz_in.at[t, q], (w, middle))

    def grads_start(t, q):
        g_copy(t, q, 0).start()
        g_copy(t, q, 1).start()

    def grads_second(t, q):
        g_copy(t, q, 0).wait_recv()
        add_to(g_block(t, q, block_x, 0, block // 2), [r.near_half.at[t, q, 0]])
        g_copy(t, q, 2).start()
        g_copy(t, q, 1).wait_recv()
        add_to(g_block(t, q, block_y, block // 2, block // 2), [r.near_half.at[t, q, 1]])
        g_copy(t, q, 3).start()

    def grads_third(t):
        for q in range(2):
            g_copy(t, q, 2).wait_recv()
            g_copy(t, q, 3).wait_recv()
            add_to(g_block(t, q, mine), [r.near_full.at[t, q, 0], r.near_full.at[t, q, 1]])

            if t == 0:

                @pl.when(far[q] != 0)
                def _():
                    g_home(t, q, far[q] - 1).start()

            else:

                @pl.when(z == edge)
                def _():
                    g_edge(t, q).start()

                @pl.when((far[q] != 0) & (z != edge) & (z != middle))
                def _():
                    g_home(t, q, 0).start()

    def grads_middle(t):
        @pl.when(z == middle)
        def _():
            for q in range(2):
                landed(r.from_z.at[Z_SLOT[t] + q], sem.gz_in.at[t, q])
                add_to(g_block(t, q, mine), [r.from_z.at[Z_SLOT[t] + q]])
                g_home(t, q, 1).start()

    def out_block(t, index, start=0, count=block):
        if t == 0:
            return r.g_o
        return (r.g_up, r.g_down)[t - 1].at[pl.ds(pl.multiple_of(index * block + start, 32), count)]

    def heads_each(index, action):
        @pl.when(index == 3)
        def _():
            action(r.g_o)

        @pl.when(index != 3)
        def _():
            action(r.g_qkv.at[jnp.minimum(index, 2)])

    def heads_leave(q):
        def action(place):
            pltpu.make_async_copy(g_block(0, q, mine), place, sem.end_in.at[0, 4]).start()
            for n, device in enumerate((next_x, next_y, (flip(next_x[0], by, 4), z))):
                remote(g_block(0, q, mine), place, sem.end_send.at[0, n], sem.end_in.at[0, n], device).start()

        heads_each(mine, action)

    def pair_start(t, n):
        if t > 0:
            end_pair(t, n).start()
            return
        heads_each(
            (mine, block_x, block_y, block_d)[n],
            lambda place: remote(place, place, sem.end_send.at[0, 4 + n], sem.end_in.at[0, 5 + n], pair).start(),
        )

    def end_local(t, q):
        return pltpu.make_async_copy(g_block(t, q, mine), out_block(t, mine), sem.end_in.at[t, 4])

    def end_copy(t, q, n):
        if n < 2:
            return remote(
                g_block(t, q, mine), out_block(t, mine), sem.end_send.at[t, n], sem.end_in.at[t, n],
                (next_x, next_y)[n],
            )
        if t == 0:
            return remote(
                g_block(t, q, mine), out_block(t, mine), sem.end_send.at[t, 2], sem.end_in.at[t, 2],
                (flip(next_x[0], by, 4), z),
            )
        ref = out_block(t, block_x, 0, block // 2) if n == 2 else out_block(t, block_y, block // 2, block // 2)
        return remote(ref, ref, sem.end_send.at[t, n], sem.end_in.at[t, n], (next_y, next_x)[n - 2])

    def end_pair(t, n):
        ref = out_block(t, (mine, block_x, block_y, block_d)[n])
        return remote(ref, ref, sem.end_send.at[t, 4 + n], sem.end_in.at[t, 5 + n], pair)

    def group_copy(t, q, step):
        return remote(
            g_block(t, q, mine), r.groups.at[t, step], sem.group_send.at[t, step], sem.group_in.at[t, step],
            ((w + 8 * step) % n_wide, z),
        )

    def grads_fourth(t):
        for q in range(2):

            @pl.when(far[q] == 0)
            def _():
                count = 3 if t == 0 else 2
                for slot in range(count):
                    landed(r.from_z.at[Z_SLOT[t] + slot], sem.gz_in.at[t, slot])
                add_to(g_block(t, q, mine), [r.from_z.at[Z_SLOT[t] + slot] for slot in range(count)])
                for step in range(1, groups):
                    group_copy(t, q, step).start()
                for step in range(1, groups):
                    group_copy(t, q, step).wait()
                for step in range(1, groups):
                    load = pltpu.make_async_copy(r.groups.at[t, step], r.from_z.at[Z_SLOT[t]], sem.group_load.at[t])
                    load.start()
                    load.wait()
                    add_to(g_block(t, q, mine), [r.from_z.at[Z_SLOT[t]]])
                if t == 0:
                    heads_leave(q)
                else:
                    end_local(t, q).start()
                    end_copy(t, q, 0).start()
                    end_copy(t, q, 1).start()

    def grads_fifth(t):
        for q in range(2):

            @pl.when(far[q] == 0)
            def _():
                landed(out_block(t, block_x), sem.end_in.at[t, 0])
                if t > 0:
                    end_copy(t, q, 2).start()
                pair_start(t, 1)
                landed(out_block(t, block_y), sem.end_in.at[t, 1])
                if t > 0:
                    end_copy(t, q, 3).start()
                pair_start(t, 2)
                end_local(t, q).wait()
                pair_start(t, 0)

    def grads_sixth(t):
        for q in range(2):

            @pl.when(far[q] == 0)
            def _():
                if t == 0:
                    landed(out_block(t, block_d), sem.end_in.at[t, 2])
                else:
                    landed(out_block(t, block_d, 0, block // 2), sem.end_in.at[t, 2])
                    landed(out_block(t, block_d, block // 2, block // 2), sem.end_in.at[t, 3])
                pair_start(t, 3)

    def grads_done(t):
        for q in range(2):
            for n in range(4):
                g_copy(t, q, n).wait_send()

            @pl.when(far[q] != 0)
            def _():
                g_home(t, q, 0).wait_send()

            @pl.when(far[q] == 0)
            def _():
                for n in range(3 if t == 0 else 4):
                    end_copy(t, q, n).wait_send()
                for n in range(4):
                    end_pair(t, n).wait_send()

        @pl.when(jnp.logical_not(home))
        def _():
            for index in range(4):
                landed(out_block(t, (mine, block_x, block_y, block_d)[index]), sem.end_in.at[t, 5 + index])

    def result_copies(kind, source, dest):
        window = pl.ds((dest // 2) * (size // 2) + (dest % 2) * 256, 128)
        slot = 2 * (z % 2) + c
        own = home & (z == dest)
        mains, rests_in = ((r.out_o, r.out_r), (r.in_o, r.in_r))[kind]
        ends = (
            (source.at[own_rows, window], mains.at[slot]),
            (r.result_rest.at[kind, dest], rests_in.at[slot]),
        )
        here = [
            pltpu.make_async_copy(ref, target, sem.out_in.at[kind, slot, n]) for n, (ref, target) in enumerate(ends)
        ]
        there = [
            remote(
                ref, target, sem.out_send.at[kind, dest, n], sem.out_in.at[kind, slot, n], (w - c + z // 2, dest)
            )
            for n, (ref, target) in enumerate(ends)
        ]
        return own, here, there

    def results_start(kind, source):
        for g in range(2):
            at = pl.ds(g * (size // 2) + 128, 128)
            base = pl.multiple_of(c * part, 128)
            upper = source[pl.ds(base, part // 2), at].astype(F32)
            lower = pltpu.roll(source[pl.ds(base + part // 2, part // 2), at].astype(F32), 64, 1)
            lane = lax.broadcasted_iota(jnp.int32, upper.shape, 1)
            r.result_rest[kind, 2 * g] = jnp.where(lane < 64, upper, lower).astype(BF16)
            r.result_rest[kind, 2 * g + 1] = jnp.where(lane < 64, lower, upper).astype(BF16)
        for dest in range(4):
            own, here, there = result_copies(kind, source, dest)

            @pl.when(own)
            def _():
                for copy in here:
                    copy.start()

            @pl.when(jnp.logical_not(own))
            def _():
                for copy in there:
                    copy.start()

    def results_done(kind, source):
        mains, rests_in = ((r.out_o, r.out_r), (r.in_o, r.in_r))[kind]
        for slot in range(4):
            landed(mains.at[slot], sem.out_in.at[kind, slot, 0])
            landed(rests_in.at[slot], sem.out_in.at[kind, slot, 1])
        for dest in range(4):
            own, _, there = result_copies(kind, source, dest)

            @pl.when(jnp.logical_not(own))
            def _():
                for copy in there:
                    copy.wait_send()

    def results_turn(kind, stage_at, target, stage_out):
        mains, rests_in = ((r.out_o, r.out_r), (r.in_o, r.in_r))[kind]
        loads = []
        for slot in range(4):
            main_at = stage_at.at[pl.ds((slot // 2) * part, part), pl.ds((slot % 2) * 128, 128)]
            rest_at = stage_at.at[pl.ds(slot * (part // 2), part // 2), pl.ds(256, 128)]
            loads.append(pltpu.make_async_copy(mains.at[slot], main_at, sem.load.at[14 + slot]))
            loads.append(pltpu.make_async_copy(rests_in.at[slot], rest_at, sem.load.at[20 + slot]))
        for load in loads:
            load.start()
        for load in loads:
            load.wait()
        same, upper, lower = unit(part), unit(part // 2), unit(part // 2, part // 2)
        pieces = []
        for slot in range(4):
            main = tn(stage_at[(slot // 2) * part : (slot // 2 + 1) * part, (slot % 2) * 128 : (slot % 2 + 1) * 128], same)
            packed = stage_at[slot * (part // 2) : (slot + 1) * (part // 2), 256:384]
            first, second = tn(packed, upper), tn(packed, lower)
            rest = jnp.where(odd, first[64:] + second[:64], first[:64] + second[64:])
            pieces.append(
                jnp.where(odd, jnp.concatenate([rest, main], axis=0), jnp.concatenate([main, rest], axis=0))
            )
        turned = pltpu.roll(jnp.concatenate(pieces, axis=1), shift, 1).astype(stage_out.dtype)
        stores = []
        for n in range(2):
            stage_out[n * width : (n + 1) * width, :] = turned[:, n * half : (n + 1) * half]
            stores.append(
                pltpu.make_async_copy(
                    stage_out.at[pl.ds(n * width, width)], target.at[:, pl.ds(n * half, half)], sem.load.at[18 + n]
                )
            )
            stores[-1].start()
        for store in stores:
            store.wait()

    w_ada_again = r.slope.at[0]
    ada_loads = [
        pltpu.make_async_copy(
            r.w_ada.at[:, pl.ds(i * size, size)], w_ada_again.at[pl.ds(i * cond, cond)], sem.load.at[7 + i]
        )
        for i in range(6)
    ]

    def finish_small():
        per_slab = half // (4 * MSG_ROWS)
        count = 2 * planes
        slabs = -(-count // per_slab)
        loads = []
        for i in range(count):
            place = r.probs.at[i // per_slab, pl.ds((i % per_slab) * 4 * MSG_ROWS, 4 * MSG_ROWS)]
            source = r.messages.at[i // planes, i % planes]
            loads += [
                pltpu.make_async_copy(source.at[j], place.at[pl.ds(j * MSG_ROWS, MSG_ROWS)], sem.msg_load.at[i, j])
                for j in range(4)
            ]
        for load in loads:
            load.start()
        for load in loads + ada_loads:
            load.wait()
        totals = [None, None]
        ada = [None] * 6
        for n in range(slabs):
            used = min(count - n * per_slab, per_slab) * 4 * MSG_ROWS
            every = r.probs[n, :used, :]
            column = lax.broadcasted_iota(jnp.int32, (MSG_ROWS, used), 1)
            row = lax.broadcasted_iota(jnp.int32, (MSG_ROWS, used), 0)
            early = column + n * half < planes * 4 * MSG_ROWS
            for part_of in range(2):
                wanted = (column % MSG_ROWS == row) & (early if part_of == 0 else jnp.logical_not(early))
                term = nn(jnp.where(wanted, 1.0, 0.0).astype(BF16), every)
                totals[part_of] = term if totals[part_of] is None else totals[part_of] + term
            contexts = every[:, :cond].astype(F32)
            at = lax.broadcasted_iota(jnp.int32, contexts.shape, 0) % MSG_ROWS
            contexts = jnp.where(at == MSG_CONTEXT, contexts, 0.0)
            for i in range(6):
                moved = pltpu.roll(contexts, used - MSG_CONTEXT + i, 0).astype(BF16)
                term = tn(moved, every)
                ada[i] = term if ada[i] is None else ada[i] + term
        for i in range(6):
            r.grad_one[i * cond : (i + 1) * cond, :] = ada[i]
        r.small[...] = totals[0] + totals[1]
        up_rows = jnp.where(z // 2 == 0, totals[0][MSG_B_UP : MSG_B_UP + 2], totals[1][MSG_B_UP : MSG_B_UP + 2])
        r.small[MSG_B_UP : MSG_B_UP + 1, :] = jnp.where(odd, up_rows[1:2], up_rows[0:1])
        own_slot = jnp.where(
            (spans_own[0] >= spans_own[1]) & (spans_own[0] >= spans_own[2]),
            0,
            jnp.where(spans_own[1] >= spans_own[2], 1, 2),
        )
        place = lax.broadcasted_iota(jnp.int32, (8, 1), 0)
        grads = jnp.zeros((8, cond), F32)
        for half_at, seg, after in ((0, 0, 0), (1, 0, 1), (1, 1, 2)):
            group_at = seg * planes + plane_at
            base = (group_at % per_slab) * 4 * MSG_ROWS + (2 * c + half_at) * MSG_ROWS
            rows_at = r.probs[group_at // per_slab, pl.ds(pl.multiple_of(base, MSG_ROWS), MSG_ROWS), :]
            row = lax.broadcasted_iota(jnp.int32, (MSG_ROWS, 1), 0)
            total = jnp.zeros((MSG_ROWS, cond), F32)
            for i in range(6):
                total = total + jnp.where(row == i, nt(rows_at, w_ada_again[i * cond : (i + 1) * cond, :]), 0.0)
            slot = own_slot + after
            slot = jnp.where(slot >= slots, slot - slots, slot)
            grads = grads + jnp.where(place == slot, jnp.sum(total, axis=0, keepdims=True), 0.0)
        times = r.info[0]
        gate = 1.0 / (1.0 + jnp.exp(-times))
        r.context[...] = grads * (gate + times * gate * (1.0 - gate))
        copies = []
        for i in range(6):
            ends = (r.grad_one.at[pl.ds(i * cond, cond)], r.ada_out.at[:, pl.ds(i * size, size)])
            copies.append(pltpu.make_async_copy(*ends, sem.end_small.at[i]))
            ends = (r.small.at[i], r.b_ada_out.at[pl.ds(i * size, size)])
            copies.append(pltpu.make_async_copy(*ends, sem.end_small.at[6 + i]))
        rows_out = (
            (MSG_B_DOWN, r.b_down_out), (MSG_GAIN_ONE, r.gain_one_out), (MSG_GAIN_TWO, r.gain_two_out),
            (MSG_B_UP, r.b_up_out),
        )
        for i, (row, ref) in enumerate(rows_out):
            copies.append(pltpu.make_async_copy(r.small.at[row], ref, sem.end_small.at[12 + i]))
        copies.append(pltpu.make_async_copy(r.context.at[pl.ds(0, slots)], r.time_out, sem.end_small.at[16]))
        for copy in copies:
            copy.start()
        return copies

    time_load.wait()
    lane = lax.broadcasted_iota(jnp.int32, (1, 128), 1)
    length_row = jnp.zeros((1, 128), F32)
    for i in range(slots):
        length_row = jnp.where(lane == i, r.lengths[0, i].astype(F32), length_row)
    r.info[0, slots : slots + 1, :] = length_row
    for load in loads[4:8]:
        load.wait()
    r.b_own[...] = r.small[0:8, :]

    pl.semaphore_wait(barrier, len(peers))
    weights_start(0)
    info_copy = remote(r.info.at[0], r.info.at[1], sem.pair.at[2], sem.pair_in.at[2], pair)
    info_copy.start()
    b_copies = [
        remote(r.b_own, r.b_all.at[z], sem.b_send.at[dz], sem.b_in.at[dz], (w, (z + dz) % 4)) for dz in range(1, 4)
    ]
    for copy in b_copies:
        copy.start()

    info_copy.wait()
    info = jnp.where(home, r.info[0], r.info[1])
    context = info / (1.0 + jnp.exp(-info))
    context_low = context.astype(BF16)
    spans = [info[slots : slots + 1, i : i + 1] for i in range(slots)]
    longest = [
        (spans[0] >= spans[1]) & (spans[0] >= spans[2]),
        (spans[1] > spans[0]) & (spans[1] >= spans[2]),
        (spans[2] > spans[0]) & (spans[2] > spans[1]),
    ]

    def slot_after(shift):
        return [longest[(i - shift) % slots] for i in range(slots)]

    def pick(flags, values):
        total = None
        for flag, value in zip(flags, values):
            term = jnp.where(flag, value, 0.0)
            total = term if total is None else total + term
        return total

    flags_a = [jnp.where(odd, after.astype(F32), at.astype(F32)) > 0.5 for after, at in zip(slot_after(1), longest)]
    flags_b = [jnp.where(odd, after.astype(F32), at.astype(F32)) > 0.5 for after, at in zip(slot_after(2), longest)]
    bound = jnp.where(odd, pick(slot_after(1), spans), float(half))
    r.context[0:1, :] = pick(flags_a, [context[i : i + 1, :] for i in range(slots)])
    r.context[1:2, :] = pick(flags_b, [context[i : i + 1, :] for i in range(slots)])
    for load in loads[8:]:
        load.wait()
    rises = {}
    for i in range(6):
        modulation = nn(context_low, w_ada[i * cond : (i + 1) * cond, :]) + r.small[ROW_B_ADA + i : ROW_B_ADA + i + 1, :]
        for seg, flags in enumerate((flags_a, flags_b)):
            row = pick(flags, [modulation[n : n + 1, :] for n in range(slots)])
            if i in (1, 4):
                gain = r.small[ROW_GAIN_ONE : ROW_GAIN_ONE + 1, :] if i == 1 else r.small[ROW_GAIN_TWO : ROW_GAIN_TWO + 1, :]
                rise = 8 * seg + (RISE_ONE if i == 1 else RISE_TWO)
                r.mods[rise : rise + 1, :] = 1.0 + row
                row = gain * (1.0 + row)
            at = 8 * seg + (SHIFT_ONE, GAIN_ONE, GATE_ONE, SHIFT_TWO, GAIN_TWO, GATE_TWO)[i]
            r.mods[at : at + 1, :] = row
    inverse = jnp.exp((lane % (HD // 2)).astype(F32) * (-9.210340371976184 / (HD // 2)))
    signs = jnp.where(lane % HD < HD // 2, -1.0, 1.0)

    def tables(s, start):
        row = (lax.broadcasted_iota(jnp.int32, (TILE, 1), 0) + start).astype(F32)
        angles = jnp.where(row < bound, row, row - bound) * inverse
        r.cosine[s, :] = jnp.cos(angles)
        r.sine[s, :] = jnp.sin(angles) * signs

    tiles(half, tables)
    r.scales[...] = jnp.zeros_like(r.scales)
    r.sums[...] = jnp.zeros_like(r.sums)
    r.bias_up[...] = jnp.zeros_like(r.bias_up)
    loads[0].wait()
    loads[1].wait()
    turn_rows(0)
    rows_start(0, True)
    weights_own(0, False)
    rows_start(0, False)
    loads[2].wait()
    loads[3].wait()
    turn_rows(1)
    weights_own(0, True)
    for n, copy in enumerate(b_copies):
        landed(r.b_all.at[(z + 3 - n) % 4], sem.b_in.at[n + 1])
    r.b_all[z] = r.b_own[...]
    weights_pass(0)
    rows_join(0)
    weights_start(1)
    weights_done(0)

    def project_some(i, carry):
        @pl.when(i == 2)
        def _():
            rows_whole(0)

        project(
            bound, ((2 * c + i) % 4) * (part // 2), part // 2, r.x_low, r.mods, r.cosine, r.sine, r.w_attn, r.in_one,
            r.q, r.k, r.v,
        )
        return carry

    lax.fori_loop(0, 4, project_some, 0)
    weights_start(2)
    weights_own(1, False)
    rows_sent(0)
    attend(bound, 0, r.q, r.k, r.v, r.probs, r.scales, r.mixed)
    weights_own(1, True)
    rows_start(1, True)
    rows_start(1, False)
    attend(bound, 1, r.q, r.k, r.v, r.probs, r.scales, r.mixed)
    weights_pass(1)
    weights_own(2, False)
    attend(bound, 2, r.q, r.k, r.v, r.probs, r.scales, r.mixed)
    weights_own(2, True)
    mix_out(r.mixed, r.w_attn, r.attn_part, sharing(0, r.attn_part))
    weights_done(1)
    b_up = jnp.where(c == 0, r.b_all[0, 0:1, :], r.b_all[2, 0:1, :]), jnp.where(c == 0, r.b_all[1, 0:1, :], r.b_all[3, 0:1, :])
    feed_up(
        bound, r.x_low, r.mods, r.attn_part, r.w_ff.at[0], b_up, r.in_two, r.act, r.slope, arriving(0, r.attn_part)
    )
    weights_pass(2)
    rows_join(1)
    rows_whole(1)
    rows_sent(1)
    feed_grads(bound, r.dy_low, r.mods, r.feed_low, r.sums)
    for q in range(2):
        weight_grad(r.act.at[q], r.feed_low, r.g_ff.at[1, q])
        grads_start(2, q)
    weights_done(2)
    feed_down(r.act, r.w_ff.at[1], r.feed_part, sharing(1, r.feed_part))
    grads_second(2, 0)
    feed_back(r.feed_low, r.slope, r.w_ff.at[1], r.bias_up)
    grads_second(2, 1)
    for q in range(2):
        weight_grad(r.in_two, r.slope.at[q], r.g_ff.at[0, q])
        grads_start(1, q)
    feed_in_back(r.slope, r.w_ff.at[0], r.back_part, sharing(2, r.back_part))
    b_down = r.small[ROW_B_DOWN : ROW_B_DOWN + 1, :]
    feed_out(
        bound, r.x_low, r.dy_low, r.mods, r.attn_part, r.feed_part, b_down, r.out_low, r.sums, arriving(1, r.feed_part)
    )
    results_start(0, r.out_low)
    norm_two_back(
        bound, r.x_low, r.dy_low, r.mods, r.back_part, r.attn_part, r.w_attn, r.grad_one, r.feed_low, r.grad_mixed,
        r.sums, arriving(2, r.back_part),
    )
    weight_grad(r.mixed, r.feed_low, r.g_attn.at[3])
    grads_third(2)
    grads_second(1, 0)
    for g in range(3):
        attend_back(
            g, r.q, r.k, r.v, r.probs, r.scales, r.mixed, r.grad_mixed, r.cosine, r.sine, r.total_k, r.total_v,
            r.grad_q, r.grad_k, r.grad_v,
        )
        for t, grads in enumerate((r.grad_q, r.grad_k, r.grad_v)):
            r.g_attn[t, g * 128 : (g + 1) * 128, :] = tn(grads[:, lanes(g)], r.in_one[...]).astype(BF16)
        if g == 0:
            grads_second(1, 1)
        if g == 1:
            grads_start(0, 0)
    grads_start(0, 1)
    grads_third(1)
    project_back(r.grad_q, r.grad_k, r.grad_v, r.w_attn, r.act, sharing(3, r.act))
    grads_second(0, 0)
    grads_second(0, 1)
    grads_middle(2)
    norm_one_back(
        bound, r.x_low, r.mods, r.act, r.grad_one, r.in_two, r.sums, arriving(3, r.act)
    )

    def sum_row(piece):
        return jnp.where(c == 0, r.sums[piece : piece + 1, :], r.sums[8 + piece : 9 + piece, :])

    def mod_row(piece):
        return jnp.where(c == 0, r.mods[piece : piece + 1, :], r.mods[8 + piece : 9 + piece, :])

    gain_one = r.small[ROW_GAIN_ONE : ROW_GAIN_ONE + 1, :]
    gain_two = r.small[ROW_GAIN_TWO : ROW_GAIN_TWO + 1, :]
    context_row = jnp.where(c == 0, r.context[0:1, :], r.context[1:2, :])
    message = [
        sum_row(SUM_G1),
        sum_row(SUM_G1N) * gain_one,
        sum_row(SUM_GATE_ONE),
        sum_row(SUM_G2),
        sum_row(SUM_G2N) * gain_two,
        sum_row(SUM_GATE_TWO),
        sum_row(SUM_DY) * mod_row(GATE_TWO),
        sum_row(SUM_G1N) * mod_row(RISE_ONE),
        sum_row(SUM_G2N) * mod_row(RISE_TWO),
        r.bias_up[0:1, :],
        r.bias_up[1:2, :],
        jnp.concatenate([context_row] + [jnp.zeros((1, 128), F32)] * (size // 128 - 1), axis=1),
        jnp.zeros((4, size), F32),
    ]
    r.message[...] = jnp.concatenate(message, axis=0).astype(BF16)
    message_at = r.messages.at[c, plane_at, z]
    message_local = pltpu.make_async_copy(r.message, message_at, sem.m_in.at[0])
    message_local.start()
    message_copies = [
        remote(r.message, message_at, sem.m_send.at[dz], sem.m_in.at[dz], (w, (z + dz) % 4)) for dz in range(1, 4)
    ]
    for copy in message_copies:
        copy.start()
    for load in ada_loads:
        load.start()
    results_done(0, r.out_low)
    results_turn(0, r.act.at[0], r.out_t, r.feed_low)
    grads_middle(1)
    grads_third(0)
    grads_fourth(2)
    grads_fourth(1)
    results_start(1, r.in_two)
    message_local.wait()
    for dz in range(1, 4):
        landed(r.messages.at[c, plane_at, (z + 4 - dz) % 4], sem.m_in.at[dz])
    plane_copies = []
    for step in range(1, planes):
        ref = r.messages.at[c, plane_at]
        plane_copies.append(
            remote(ref, ref, sem.mp_send.at[step], sem.mp_in.at[step], ((w + 2 * step) % n_wide, z))
        )
        plane_copies[-1].start()
    grads_fifth(2)
    grads_fifth(1)
    for step in range(1, planes):
        landed(r.messages.at[c, (plane_at + planes - step) % planes], sem.mp_in.at[step])
    message_pair = remote(r.messages.at[c], r.messages.at[c], sem.m_send.at[4], sem.m_in.at[4], pair)
    message_pair.start()
    grads_fourth(0)
    grads_sixth(2)
    grads_sixth(1)
    landed(r.messages.at[1 - c], sem.m_in.at[4])
    small_ends = finish_small()
    grads_fifth(0)
    for copy in small_ends:
        copy.wait()
    results_done(1, r.in_two)
    results_turn(1, r.act.at[1], r.in_t, r.grad_one)
    grads_sixth(0)

    for t in range(CHUNKS):
        weights_sent(t)
    for kind in range(2):
        pair_rows(kind).wait_send()
    for copy in b_copies + message_copies + plane_copies + [message_pair]:
        copy.wait_send()
    for t in range(CHUNKS):
        grads_done(t)


def layer(n_wide, lengths, x, *others):
    width, rows = x.shape
    w_up, times = others[3], others[-1]
    size = w_up.shape[0]
    slots, cond = times.shape
    buffers, semaphores = scratch_plan(n_wide, rows, width, size, cond)
    anywhere = pl.BlockSpec(memory_space=pl.ANY)
    part, planes, groups = rows // 4, n_wide // 2, n_wide // 8
    outs = (
        ((width, rows), BF16),
        ((width, rows), F32),
        ((4, part, 128), BF16),
        ((4, part, 128), BF16),
        ((4, part // 2, 128), BF16),
        ((4, part // 2, 128), BF16),
        ((3, size // 4, size), BF16),
        ((size // 4, size), BF16),
        ((size, size), BF16),
        ((size, size), BF16),
        ((2, planes, 4, MSG_ROWS, size), BF16),
        ((CHUNKS, groups, size // 4, size), BF16),
        ((cond, 6 * size), F32),
        ((6 * size,), F32),
        ((size,), F32),
        ((size,), F32),
        ((size,), F32),
        ((size,), F32),
        ((slots, cond), F32),
    )
    return pl.pallas_call(
        functools.partial(layer_kernel, n_wide, rows, width, size, cond, slots),
        out_shape=tuple(jax.ShapeDtypeStruct(shape, kind) for shape, kind in outs),
        in_specs=[pl.BlockSpec(memory_space=pltpu.SMEM)] + [anywhere] * (1 + len(others)),
        out_specs=(anywhere,) * len(outs),
        scratch_shapes=[pltpu.VMEM(shape, kind) for shape, kind in buffers.values()]
        + [pltpu.SemaphoreType.DMA(shape) for shape in semaphores.values()],
        compiler_params=pltpu.CompilerParams(
            collective_id=0, has_side_effects=True, vmem_limit_bytes=63 * 1024 * 1024
        ),
        name="layer",
    )(lengths, x, *others)


def body(
    n_wide,
    block_input,
    time_embed,
    seq_lengths,
    w_qkv,
    w_out,
    w_up,
    b_up,
    w_down,
    b_down,
    gain_one,
    gain_two,
    w_ada,
    b_ada,
    out_grad,
):
    results = layer(
        n_wide, seq_lengths, block_input.T, out_grad.T, jnp.swapaxes(w_qkv, 1, 2), w_out, w_up, w_down, b_up,
        b_down, gain_one, gain_two, w_ada, b_ada, time_embed,
    )
    out_t, in_t, _, _, _, _, g_qkv, g_o, g_up, g_down, _, _ = results[:12]
    ada, b_ada_sum, b_down_sum, gain_one_sum, gain_two_sum, b_up_sum, times = results[12:19]
    return (
        out_t.T,
        in_t.T,
        times,
        jnp.swapaxes(g_qkv.astype(F32), 1, 2),
        g_o.astype(F32),
        g_up.astype(F32),
        b_up_sum,
        g_down.astype(F32),
        b_down_sum,
        gain_one_sum,
        gain_two_sum,
        ada,
        b_ada_sum,
    )


def solution(mesh):
    return jax.shard_map(
        functools.partial(body, mesh.shape["wide"]),
        mesh=mesh,
        in_specs=(
            P("wide", "narrow"),
            P("wide", None),
            P("wide", None),
            P(None, None, "narrow"),
            P("narrow", None),
            P(None, "narrow"),
            P("narrow"),
            P("narrow", None),
            P(),
            P(),
            P(),
            P(),
            P(),
            P("wide", "narrow"),
        ),
        out_specs=(
            P("wide", "narrow"),
            P("wide", "narrow"),
            P("wide", None),
            P(None, None, "narrow"),
            P("narrow", None),
            P(None, "narrow"),
            P("narrow"),
            P("narrow", None),
            P(),
            P(),
            P(),
            P(),
            P(),
        ),
        check_vma=False,
    )
```
